32 devices in a mesh: ulysses: 4 (over x, core), blk: 8 (over z, y).
Axes of the slice: x: 2, y: 2, z: 4, core: 2. Of those that a mesh axis runs over, the one named last changes fastest.
Arguments:
- tokens: bfloat16 [2048, 2, 2048], P(('ulysses', 'blk')), may hold values from -6 to 6
- w_query: bfloat16 [2048, 2048], P(('ulysses', 'blk')), may hold values from -0.125 to 0.125
- w_key: bfloat16 [2048, 2048], P(('ulysses', 'blk')), may hold values from -0.125 to 0.125
- w_value: bfloat16 [2048, 2048], P(('ulysses', 'blk')), may hold values from -0.125 to 0.125
- w_out: bfloat16 [2048, 2048], P(('ulysses', 'blk')), may hold values from -0.75 to 0.75
- attn_gain: bfloat16 [2048], P(('ulysses', 'blk')), may hold values from 0.5 to 1.5
- ffn_gain: bfloat16 [2048], P(('ulysses', 'blk')), may hold values from 0.5 to 1.5
- qk_gain: bfloat16 [2, 128], P(None, ('ulysses', 'blk')), may hold values from 1.1953125 to 1.796875
- expert_gate: bfloat16 [64, 2048, 1024], P('blk', None, 'ulysses'), may hold values from -0.125 to 0.125
- expert_up: bfloat16 [64, 2048, 1024], P('blk', None, 'ulysses'), may hold values from -0.125 to 0.125
- expert_down: bfloat16 [64, 1024, 2048], P('blk', 'ulysses'), may hold values from -0.1875 to 0.1875
- routes: int32 [2048, 2, 8], P(('ulysses', 'blk')), may hold values from 0 to 63, all different within a row
- gates: float32 [2048, 2, 8], P(('ulysses', 'blk')), may hold values from 0.2 to 0.6
- order: int32 [32, 1024], P(('ulysses', 'blk')), may hold values from 0 to 1023, each once within a row
- cotangent: bfloat16 [2048, 2, 2048], P(('ulysses', 'blk')), may hold values from -6 to 6
Outputs:
- mixed: bfloat16 [2048, 2, 2048], P(('ulysses', 'blk'))
- input_grad: float32 [2048, 2, 2048], P(('ulysses', 'blk'))
- query_grad: float32 [2048, 2048], P(('ulysses', 'blk'))
- key_grad: float32 [2048, 2048], P(('ulysses', 'blk'))
- value_grad: float32 [2048, 2048], P(('ulysses', 'blk'))
- out_grad: float32 [2048, 2048], P(('ulysses', 'blk'))
- attn_gain_grad: float32 [2048], P(('ulysses', 'blk'))
- ffn_gain_grad: float32 [2048], P(('ulysses', 'blk'))
- qk_gain_grad: float32 [2, 128], P(None, ('ulysses', 'blk'))
- gate_grad: float32 [64, 2048, 1024], P('blk', None, 'ulysses')
- up_grad: float32 [64, 2048, 1024], P('blk', None, 'ulysses')
- down_grad: float32 [64, 1024, 2048], P('blk', 'ulysses')
The draws below stay inside these ranges and needn't reach their ends.
Inputs may be any that keep to these rules, and one draw needn't show every extreme that they name: `routes`: each token names 8 different experts, and every expert is named by some token. `order`: each row holds every number of its range once.
All inputs are finite; a program needn't handle non-finite values.
Results may differ from the reference program's by a relative error of at most 0.02.
Values may be sent and summed in bfloat16 or wider, within the bound.
A program may use at most 576 MiB of HBM per device.

```python
import math
import jax
import jax.numpy as jnp
from jax import lax

D = 2048
H = 16
HD = 128
FF = 1024
EXPERTS = 64
TOP = 8
SEQS = 2
CAP = 18
LEN = 2048
TOK_DEV = 128
BLOCKS = 32
N_ULYSSES = 4


def block_scale(rng, shape, pieces, smallest, top_value):
    def one(position, parts):
        draws = jax.random.uniform(jax.random.fold_in(jax.random.fold_in(rng, 6), position), (parts,), jnp.float32, smallest / len(pieces), top_value / len(pieces))
        return jnp.repeat(jnp.exp(draws), shape[position] // parts).reshape((-1,) + (1,) * (len(shape) - position - 1))

    gain = one(*pieces[0])
    for cut in pieces[1:]:
        gain = gain * one(*cut)
    return gain


def choose_distinct(rng, rows, number_of, top, lift):
    sequence = jax.random.permutation(jax.random.fold_in(rng, 1), number_of)
    pull = sequence
    for power in range(3):
        pull = pull * pull // number_of
    pull = pull * lift // number_of
    lots = jax.random.randint(jax.random.fold_in(rng, 2), (rows, number_of), 0, 4096) + pull
    sure = jax.random.permutation(jax.random.fold_in(rng, 3), rows)[jnp.arange(number_of) % rows]
    lots = jnp.where(jnp.arange(rows)[:, None] == sure[None, :], 1 << 14, lots)
    score = lots * number_of + jnp.arange(number_of)
    return lax.top_k(score.astype(jnp.int32), top)[1].astype(jnp.int32)


def bell_draw(key, shape, width, most, pieces=(), kind=jnp.bfloat16):
    loudness = block_scale(key, shape, pieces, -0.22, 0.18) if pieces else 1.0
    values = jax.random.normal(key, shape, jnp.float32) * width * loudness
    return jnp.minimum(jnp.maximum(values, -most), most).astype(kind)


def setup_inputs(seed: int = 0) -> dict:
    key_of = jax.random.split(jax.random.key(seed), 16)
    return {
        "tokens": bell_draw(key_of[0], (LEN, SEQS, D), 1.0, 6.0, ((0, 32),)),
        "w_query": bell_draw(key_of[1], (D, H * HD), D ** -0.5, 0.125, ((0, 32),)),
        "w_key": bell_draw(key_of[2], (D, H * HD), D ** -0.5, 0.125, ((0, 32),)),
        "w_value": bell_draw(key_of[3], (D, H * HD), D ** -0.5, 0.125, ((0, 32),)),
        "w_out": bell_draw(key_of[4], (H * HD, D), (H * HD // 32) ** -0.5, 0.75, ((0, 32),)),
        "attn_gain": jnp.clip(1.0 + 0.1 * jax.random.normal(key_of[5], (D,), jnp.float32), 0.5, 1.5).astype(jnp.bfloat16),
        "ffn_gain": jnp.clip(1.0 + 0.1 * jax.random.normal(key_of[6], (D,), jnp.float32), 0.5, 1.5).astype(jnp.bfloat16),
        "qk_gain": jnp.clip(1.1953125 + 0.6015625 * jax.random.uniform(key_of[7], (2, HD), jnp.float32) ** block_scale(key_of[7], (2, HD), ((1, 32),), -0.2, 0.2), 1.1953125, 1.796875).astype(jnp.bfloat16),
        "expert_gate": bell_draw(key_of[8], (EXPERTS, D, FF), D ** -0.5, 0.125, ((0, 8), (2, 4))),
        "expert_up": bell_draw(key_of[9], (EXPERTS, D, FF), D ** -0.5, 0.125, ((0, 8), (2, 4))),
        "expert_down": bell_draw(key_of[10], (EXPERTS, FF, D), FF ** -0.5, 0.1875, ((0, 8), (1, 4))),
        "routes": choose_distinct(key_of[11], LEN * SEQS, EXPERTS, TOP, 2048).reshape((LEN, SEQS, TOP)),
        "gates": jnp.clip(0.2 + 0.400000021 * jax.random.uniform(key_of[12], (LEN, SEQS, TOP), jnp.float32) ** block_scale(key_of[12], (LEN, SEQS, TOP), ((0, 32),), -0.2, 0.2), 0.2, 0.6),
        "order": jax.vmap(lambda own: jax.random.permutation(own, TOK_DEV * TOP))(jax.random.split(key_of[13], BLOCKS)).reshape((BLOCKS, TOK_DEV * TOP)).astype(jnp.int32),
        "cotangent": bell_draw(key_of[14], (LEN, SEQS, D), 1.0, 6.0, ((0, 32),)),
    }


EPSILON = 1e-06
ROPE_BASE = 10000.0
HIGHEST = lax.Precision.HIGHEST

@jax.custom_vjp
def low(v):
    return lax.optimization_barrier(v.astype(jnp.bfloat16)).astype(jnp.float32)

@jax.custom_vjp
def low_back(v):
    return v

def low_keep(v):
    return (low(v), None)

def low_pass(kept, grad):
    return (grad,)

def back_keep(v):
    return (v, None)

def back_low(kept, grad):
    return (low(grad),)
low.defvjp(low_keep, low_pass)
low_back.defvjp(back_keep, back_low)

def rms_norm(values, gains):
    return values * lax.rsqrt(lax.optimization_barrier(jnp.mean(values * values, axis=-1, keepdims=True)) + EPSILON) * gains

def rotate(values, positions):
    half_size = values.shape[-1] // 2
    inverse = ROPE_BASE ** (-2.0 * jnp.arange(half_size).astype(jnp.float32) / values.shape[-1])
    angles = positions[:, None] * inverse[None, :]
    cosine = jnp.cos(angles)[:, None, None, :]
    sine = jnp.sin(angles)[:, None, None, :]
    first_half = values[..., :half_size]
    second_half = values[..., half_size:]
    return jnp.concatenate([first_half * cosine - second_half * sine, second_half * cosine + first_half * sine], axis=-1)

def slot_tables(routes, gates, order):
    pair_count = TOK_DEV * TOP
    expert_ids = routes.reshape(BLOCKS, pair_count)

    def rank_block(operands):
        ids_block, prio_block = operands
        same_expert = ids_block[:, None] == ids_block[None, :]
        earlier = prio_block[None, :] < prio_block[:, None]
        return lax.optimization_barrier(jnp.sum((same_expert & earlier).astype(jnp.int32), axis=1))
    ranks = lax.map(rank_block, (expert_ids, order))
    block_ids = jnp.arange(BLOCKS, dtype=jnp.int32)[:, None]
    token_ids = block_ids * TOK_DEV + jnp.arange(pair_count, dtype=jnp.int32)[None, :] // TOP
    columns = jnp.where(ranks < CAP, block_ids * CAP + ranks, BLOCKS * CAP).astype(jnp.int32)
    token_table = jnp.full((EXPERTS, BLOCKS * CAP), LEN * SEQS, jnp.int32).at[expert_ids, columns].set(token_ids, mode='drop')
    gate_table = jnp.zeros((EXPERTS, BLOCKS * CAP), jnp.float32).at[expert_ids, columns].set(gates.reshape(BLOCKS, pair_count).astype(jnp.float32), mode='drop')
    return (token_table, gate_table)

def attention(queries, keys, values):
    block_rows = min(512, LEN)
    score_scale = 1.0 / math.sqrt(HD)

    def one_block(query_block):
        scores = low_back(jnp.einsum('qshd,kshd->qshk', query_block, keys, precision=HIGHEST) * score_scale)
        probs = jax.nn.softmax(scores, axis=-1)
        return jnp.einsum('qshk,kshd->qshd', low(probs), values, precision=HIGHEST)
    blocks = queries.reshape((LEN // block_rows, block_rows) + queries.shape[1:])
    return lax.map(jax.checkpoint(one_block), blocks).reshape(queries.shape)

def experts(normed, gate_all, up_all, down_all, token_table, gate_table):
    quarter_width = FF // N_ULYSSES

    def one_expert(operands):
        rows_index, pair_weights, gate_w, up_w, down_w = operands
        gathered = jnp.take(normed, rows_index, axis=0, mode='fill', fill_value=0.0)
        gate_act = low_back(jnp.dot(gathered, gate_w, precision=HIGHEST))
        up_act = low_back(jnp.dot(gathered, up_w, precision=HIGHEST))
        inner = low(jax.nn.silu(gate_act) * up_act)
        partials = low(low_back(jnp.einsum('rqf,qfd->rqd', inner.reshape(-1, N_ULYSSES, quarter_width), down_w.reshape(N_ULYSSES, quarter_width, D), precision=HIGHEST)))
        return lax.optimization_barrier(jnp.sum(partials, axis=1)) * pair_weights[:, None]
    outputs = lax.map(jax.checkpoint(one_expert), (token_table, gate_table, gate_all, up_all, down_all))
    return jnp.zeros_like(normed).at[token_table.reshape(-1)].add(outputs.reshape(-1, D), mode='drop')

def reference(tokens, w_query, w_key, w_value, w_out, attn_gain, ffn_gain, qk_gain, expert_gate, expert_up, expert_down, routes, gates, order, cotangent):
    token_table, gate_table = slot_tables(routes, gates, order)
    positions = jnp.arange(LEN).astype(jnp.float32)
    head_shape = (LEN, SEQS, H, HD)

    def layer(params):
        tokens_f, query_w, key_w, value_w, out_w, attn_g, ffn_g, qk_g, gate_all, up_all, down_all = params
        flat_in = tokens_f.reshape(LEN * SEQS, D)
        hidden = low(rms_norm(flat_in, attn_g))
        query_raw = low_back(jnp.dot(hidden, query_w, precision=HIGHEST)).reshape(head_shape)
        key_raw = low_back(jnp.dot(hidden, key_w, precision=HIGHEST)).reshape(head_shape)
        value_heads = low(low_back(jnp.dot(hidden, value_w, precision=HIGHEST))).reshape(head_shape)
        queries = low(low_back(rotate(rms_norm(query_raw, qk_g[0]), positions)))
        keys = low(low_back(rotate(rms_norm(key_raw, qk_g[1]), positions)))
        attended = low(low_back(attention(queries, keys, value_heads)))
        residual = flat_in + low_back(jnp.dot(attended.reshape(LEN * SEQS, H * HD), out_w, precision=HIGHEST))
        normed = low(rms_norm(residual, ffn_g))
        return residual + experts(normed, gate_all, up_all, down_all, token_table, gate_table)
    floats = tuple((item.astype(jnp.float32) for item in (tokens, w_query, w_key, w_value, w_out, attn_gain, ffn_gain, qk_gain, expert_gate, expert_up, expert_down)))
    result, pullback = jax.vjp(layer, floats)
    grads = pullback(cotangent.astype(jnp.float32).reshape(LEN * SEQS, D))[0]
    return (result.reshape(LEN, SEQS, D).astype(jnp.bfloat16), grads[0], grads[1], grads[2], grads[3], grads[4], grads[5], grads[6], grads[7], grads[8], grads[9], grads[10])
```

```python
import functools
import math

import jax
import jax.numpy as jnp
import numpy as np
from jax import lax
from jax.experimental import pallas as pl
from jax.experimental.pallas import tpu as pltpu
from jax.sharding import PartitionSpec as P

HD = 128
CAP = 18
EPSILON = 1e-06
ROPE_BASE = 10000.0
AXES = ("ulysses", "blk")
MESH = pl.DeviceIdType.MESH


class Place:
    def __init__(self, U, B):
        self.U, self.B = U, B
        self.X, self.Y = U // 2, 2
        self.Z = B // self.Y
        u, b = lax.axis_index("ulysses"), lax.axis_index("blk")
        self.c, self.x = lax.rem(u, 2), lax.div(u, 2)
        self.y, self.z = lax.rem(b, self.Y), lax.div(b, self.Y)
        self.core_peer = self.dev(self.x, self.y, self.z, 1 - self.c)

    def dev(self, x, y, z, c):
        return (x * 2 + c, z * self.Y + y)

    def block(self, x, y, z, c):
        return (x * 2 + c) * self.B + z * self.Y + y

    def others(self, axis):
        n = {"x": self.X, "y": self.Y, "z": self.Z}[axis]
        i = {"x": self.x, "y": self.y, "z": self.z}[axis]
        return [lax.rem(i + o, n) for o in range(1, n)]

    def barrier(self, chain):
        sem = pltpu.get_barrier_semaphore()

        def greet(d):
            pl.semaphore_signal(sem, inc=1, device_id=d, device_id_type=MESH)

        greet(self.core_peer)
        for k in self.others("x"):
            greet(self.dev(k, self.y, self.z, self.c))
        for k in self.others("y"):
            greet(self.dev(self.x, k, self.z, self.c))
        count = self.X + self.Y - 1
        if chain:
            below, above = self.z > 0, self.z < self.Z - 1

            @pl.when(below)
            def _():
                greet(self.dev(self.x, self.y, self.z - 1, self.c))

            @pl.when(above)
            def _():
                greet(self.dev(self.x, self.y, self.z + 1, self.c))

            count = count + jnp.where(below, 1, 0) + jnp.where(above, 1, 0)
        else:
            for k in self.others("z"):
                greet(self.dev(self.x, self.y, k, self.c))
            count += self.Z - 1
        pl.semaphore_wait(sem, count)


def gather_kernel(U, B, by_seq, src, out, send_sem, recv_sem, local_sem):
    p = Place(U, B)
    Z = p.Z
    p.barrier(True)
    started = []
    always = p.z >= 0

    def where(half, x, y, z):
        if by_seq:
            f = p.block(x, y, z, half)
            return out.at[f], (0, f)
        f = p.block(x, y, z, p.c)
        return out.at[f, half], (half, f)

    def send(cond, src_ref, dst_ref, ix, way, dev):
        cp = pltpu.make_async_remote_copy(
            src_ref=src_ref, dst_ref=dst_ref, send_sem=send_sem.at[(way,) + ix], recv_sem=recv_sem.at[ix],
            device_id=dev, device_id_type=MESH)

        @pl.when(cond)
        def _():
            cp.start()

        started.append((cond, cp))

    def wait(ref, ix):
        pltpu.make_async_remote_copy(
            src_ref=ref, dst_ref=ref, send_sem=send_sem.at[(0,) + ix], recv_sem=recv_sem.at[ix],
            device_id=p.core_peer, device_id_type=MESH).wait_recv()

    def along(cond, half, x, y, z, axes):
        ref, ix = where(half, x, y, z)
        for ax in axes:
            if ax == "core":
                if not by_seq:
                    send(cond, ref, ref, ix, 0, p.core_peer)
            elif ax == "up":
                send(cond & (p.z < Z - 1), ref, ref, ix, 1, p.dev(p.x, p.y, p.z + 1, p.c))
            elif ax == "down":
                send(cond & (p.z > 0), ref, ref, ix, 2, p.dev(p.x, p.y, p.z - 1, p.c))
            elif ax == "y":
                for i, k in enumerate(p.others("y")):
                    send(cond, ref, ref, ix, 3 + i, p.dev(p.x, k, p.z, p.c))
            else:
                for i, k in enumerate(p.others("x")):
                    send(cond, ref, ref, ix, 2 + p.Y + i, p.dev(k, p.y, p.z, p.c))

    me = p.block(p.x, p.y, p.z, p.c)
    sib = p.block(p.x, p.y, p.z, 1 - p.c)
    if by_seq:
        cp = pltpu.make_async_copy(src.at[p.c], out.at[me], local_sem.at[0])
        cp.start()
        send(always, src.at[1 - p.c], out.at[me], (0, me), 0, p.core_peer)
        cp.wait()
        wait(out.at[sib], (0, sib))
    else:
        cp = pltpu.make_async_copy(src, out.at[me], local_sem.at[0])
        cp.start()
        cp.wait()
    for half in (0, 1):
        along(always, half, p.x, p.y, p.z, ("up", "down", "y", "x"))
    for half in (0, 1):
        along(always, half, p.x, p.y, p.z, ("core",))

    def zs(step):
        if step == 0:
            return [(always, p.z, ())]
        return [(p.z - step >= 0, p.z - step, ("up",)), (p.z + step < Z, p.z + step, ("down",))]

    def arrive(cond, half, x, y, z, axes):
        ref, ix = where(half, x, y, z)

        @pl.when(cond)
        def _():
            wait(ref, ix)

        along(cond, half, x, y, z, axes)

    for step in range(1, Z + 2):
        if step < Z:
            for half in (0, 1):
                for cond, k, on in zs(step):
                    arrive(cond, half, p.x, p.y, k, on + ("y", "x", "core"))
        if 1 <= step <= Z:
            for cond, k, _ in zs(step - 1):
                for j in p.others("y"):
                    arrive(cond, 0, p.x, j, k, ("x", "core"))
                for j in p.others("x"):
                    arrive(cond, 1, j, p.y, k, ("y", "core"))
        if step >= 2:
            for cond, k, _ in zs(step - 2):
                for j in p.others("x"):
                    arrive(cond, 0, j, p.y, k, ("core",))
                for i in p.others("y"):
                    arrive(cond, 1, p.x, i, k, ("core",))
                for j in p.others("x"):
                    for i in p.others("y"):
                        arrive(cond, 0, j, i, k, ("core",))
                        arrive(cond, 1, j, i, k, ("core",))
    if not by_seq:
        for k in range(Z):
            for j in range(p.X):
                for i in range(p.Y):
                    for half in (0, 1):
                        f = p.block(j, i, k, 1 - p.c)
                        wait(out.at[f, half], (half, f))
    for cond, cp in started:
        @pl.when(cond)
        def _(cp=cp):
            cp.wait_send()


def gather_blocks(v, U, B, by_seq, cid):
    F = U * B
    shape = (F,) + (v.shape[1:] if by_seq else v.shape)
    n = 1 if by_seq else 2
    return pl.pallas_call(
        functools.partial(gather_kernel, U, B, by_seq),
        out_shape=jax.ShapeDtypeStruct(shape, v.dtype),
        in_specs=[pl.BlockSpec(memory_space=pl.ANY)],
        out_specs=pl.BlockSpec(memory_space=pl.ANY),
        scratch_shapes=[
            pltpu.SemaphoreType.DMA((2 + 2 + U // 2 - 1 + 0, n, F)),
            pltpu.SemaphoreType.DMA((n, F)),
            pltpu.SemaphoreType.DMA((1,)),
        ],
        compiler_params=pltpu.CompilerParams(collective_id=cid, has_side_effects=True),
    )(v)


def scatter_kernel(U, B, by_seq, src, out, acc, rc, rx0, rx1, ry0, ry1, rz, fin,
                   loc, scs, rcs, sxs, rxs, sys_, rys, szs, rzs, fs):
    p = Place(U, B)
    X, Y, Z = p.X, p.Y, p.Z
    rows = acc.shape[2]
    p.barrier(False)
    f32 = jnp.float32
    started = []

    def chip(x, y, z):
        return x * B + z * Y + y

    def remote(a, b, ss, rs, dev):
        return pltpu.make_async_remote_copy(
            src_ref=a, dst_ref=b, send_sem=ss, recv_sem=rs, device_id=dev, device_id_type=MESH)

    def start(*a):
        cp = remote(*a)
        cp.start()
        started.append(cp)

    def got(ref, rs):
        remote(ref, ref, fs.at[1], rs, p.core_peer).wait_recv()

    order = p.others("z") + [p.z]
    ox, oy = p.others("x"), p.others("y")

    def first_pieces(k):
        return [(0, j, i, k) for j in ox for i in range(Y)] + [(1, j, i, k) for i in oy for j in range(X)]

    def second_pieces(k):
        return [(0, p.x, i, k) for i in oy] + [(1, j, p.y, k) for j in ox]

    def third_pieces(k):
        return [(0, p.x, p.y, k), (1, p.x, p.y, k)]

    def load(h, j, i, k):
        q = chip(j, i, k)
        if by_seq:
            pltpu.make_async_copy(src.at[p.block(j, i, k, h)], acc.at[q, h], loc.at[q, h]).start()
        else:
            start(src.at[p.block(j, i, k, 1 - p.c), h], rc.at[q, h], scs.at[q, h], rcs.at[q, h], p.core_peer)
            pltpu.make_async_copy(src.at[p.block(j, i, k, p.c), h], acc.at[q, h], loc.at[q, h]).start()

    def ready(h, j, i, k):
        q = chip(j, i, k)
        pltpu.make_async_copy(acc.at[q, h], acc.at[q, h], loc.at[q, h]).wait()
        if by_seq:
            return []
        got(rc.at[q, h], rcs.at[q, h])
        return [rc.at[q, h]]

    step = 16

    def add(dst, srcs, f32_out=None):
        if not srcs and f32_out is None:
            return

        def one(n, _):
            r = pl.ds(pl.multiple_of(n * step, step), step)
            t = dst[r, :].astype(f32)
            for s in srcs:
                t = t + s[r, :].astype(f32)
            if f32_out is None:
                dst[r, :] = t.astype(dst.dtype)
            else:
                f32_out[r, :] = t
            return 0

        lax.fori_loop(0, rows // step, one, 0)

    def phase1(k):
        for h, j, i, kk in first_pieces(k):
            q = chip(j, i, k)
            add(acc.at[q, h], ready(h, j, i, k))
            if h == 0:
                s = k * Y + i
                start(acc.at[q, 0], rx0.at[p.x, s], sxs.at[0, j, s], rxs.at[0, p.x, s], p.dev(j, p.y, p.z, p.c))
            else:
                s = k * X + j
                start(acc.at[q, 1], ry1.at[p.y, s], sys_.at[1, i, s], rys.at[1, p.y, s], p.dev(p.x, i, p.z, p.c))

    def phase2(k):
        for h, j, i, kk in second_pieces(k):
            q = chip(j, i, k)
            extra = ready(h, j, i, k)
            if h == 0:
                s = k * Y + i
                for a in ox:
                    got(rx0.at[a, s], rxs.at[0, a, s])
                    extra.append(rx0.at[a, s])
                add(acc.at[q, 0], extra)
                start(acc.at[q, 0], ry0.at[p.y, k], sys_.at[0, i, k], rys.at[0, p.y, k], p.dev(p.x, i, p.z, p.c))
            else:
                s = k * X + j
                for a in oy:
                    got(ry1.at[a, s], rys.at[1, a, s])
                    extra.append(ry1.at[a, s])
                add(acc.at[q, 1], extra)
                start(acc.at[q, 1], rx1.at[p.x, k], sxs.at[1, j, k], rxs.at[1, p.x, k], p.dev(j, p.y, p.z, p.c))

    def phase3(n, k):
        for h, j, i, kk in third_pieces(k):
            q = chip(j, i, k)
            extra = ready(h, j, i, k)
            if h == 0:
                s = k * Y + i
                for a in ox:
                    got(rx0.at[a, s], rxs.at[0, a, s])
                    extra.append(rx0.at[a, s])
                for a in oy:
                    got(ry0.at[a, k], rys.at[0, a, k])
                    extra.append(ry0.at[a, k])
            else:
                s = k * X + j
                for a in oy:
                    got(ry1.at[a, s], rys.at[1, a, s])
                    extra.append(ry1.at[a, s])
                for a in ox:
                    got(rx1.at[a, k], rxs.at[1, a, k])
                    extra.append(rx1.at[a, k])
            if n < Z - 1:
                add(acc.at[q, h], extra)
                start(acc.at[q, h], rz.at[h, p.z], szs.at[h, k], rzs.at[h, p.z], p.dev(p.x, p.y, k, p.c))
            else:
                for a in p.others("z"):
                    got(rz.at[h, a], rzs.at[h, a])
                    extra.append(rz.at[h, a])
                add(acc.at[q, h], extra, fin.at[h])

    for k in order:
        for piece in first_pieces(k) + second_pieces(k) + third_pieces(k):
            load(*piece)
    for n in range(Z + 2):
        if n < Z:
            phase1(order[n])
        if 1 <= n <= Z:
            phase2(order[n - 1])
        if n >= 2:
            phase3(n - 2, order[n - 2])
    if by_seq:
        start(fin.at[1 - p.c], out.at[p.c], fs.at[2], fs.at[0], p.core_peer)
        cp = pltpu.make_async_copy(fin.at[p.c], out.at[p.c], fs.at[1])
        cp.start()
        cp.wait()
        got(out.at[1 - p.c], fs.at[0])
    else:
        cp = pltpu.make_async_copy(fin, out, fs.at[1])
        cp.start()
        cp.wait()
    for cp in started:
        cp.wait_send()


def scatter_blocks(v, U, B, by_seq, cid):
    F, Q = U * B, U * B // 2
    X, Y, Z = U // 2, 2, B // 2
    rows, D = v.shape[-2:]
    parts = max(1, F // 32)
    if parts > 1:
        w = D // parts
        return jnp.concatenate(
            [_scatter(v[..., n * w:(n + 1) * w], U, B, by_seq, cid) for n in range(parts)], axis=-1)
    return _scatter(v, U, B, by_seq, cid)


def _scatter(v, U, B, by_seq, cid):
    F, Q = U * B, U * B // 2
    X, Y, Z = U // 2, 2, B // 2
    rows, D = v.shape[-2:]
    t = v.dtype
    dma = pltpu.SemaphoreType.DMA
    big = max(Z * Y, Z * X)
    return pl.pallas_call(
        functools.partial(scatter_kernel, U, B, by_seq),
        out_shape=jax.ShapeDtypeStruct((2, rows, D), jnp.float32),
        in_specs=[pl.BlockSpec(memory_space=pl.ANY)],
        out_specs=pl.BlockSpec(memory_space=pl.ANY),
        scratch_shapes=[
            pltpu.VMEM((Q, 2, rows, D), t),
            pltpu.VMEM((1, 1, 16, 128) if by_seq else (Q, 2, rows, D), t),
            pltpu.VMEM((X, Z * Y, rows, D), t),
            pltpu.VMEM((X, Z, rows, D), t),
            pltpu.VMEM((Y, Z, rows, D), t),
            pltpu.VMEM((Y, Z * X, rows, D), t),
            pltpu.VMEM((2, Z, rows, D), t),
            pltpu.VMEM((2, rows, D), jnp.float32),
            dma((Q, 2)),
            dma((Q, 2)),
            dma((Q, 2)),
            dma((2, X, big)),
            dma((2, X, big)),
            dma((2, Y, big)),
            dma((2, Y, big)),
            dma((2, Z)),
            dma((2, Z)),
            dma((3,)),
        ],
        compiler_params=pltpu.CompilerParams(
            collective_id=cid, has_side_effects=True, vmem_limit_bytes=58 * 2**20),
    )(v)


def rms_norm(values, gains):
    return values * lax.rsqrt(jnp.mean(values * values, axis=-1, keepdims=True) + EPSILON) * gains


def rotate(values):
    half = values.shape[-1] // 2
    inverse = ROPE_BASE ** (-2.0 * jnp.arange(half).astype(jnp.float32) / values.shape[-1])
    angles = jnp.arange(values.shape[0]).astype(jnp.float32)[:, None] * inverse[None, :]
    cosine, sine = jnp.cos(angles), jnp.sin(angles)
    a, b = values[:, :half], values[:, half:]
    return jnp.concatenate([a * cosine - b * sine, b * cosine + a * sine], axis=-1)


def dot(a, b, ca, cb):
    return lax.dot_general(a, b, (((ca,), (cb,)), ((), ())), preferred_element_type=jnp.float32)


def attend_kernel(scale, q_ref, k_ref, vt_ref, o_ref, lse_ref):
    s = dot(k_ref[...], q_ref[...], 1, 1) * scale
    top = jnp.max(s, axis=0, keepdims=True)
    e = jnp.exp(s - top)
    total = jnp.sum(e, axis=0, keepdims=True)
    o = dot(vt_ref[...], e.astype(jnp.bfloat16), 1, 0) / total
    o_ref[...] = o.T.astype(o_ref.dtype)
    lse_ref[...] = top + jnp.log(total)


def attend(q, k, vt):
    n = q.shape[0]
    bq = 256 if n <= 2048 else 128
    return pl.pallas_call(
        functools.partial(attend_kernel, 1.0 / math.sqrt(HD)),
        grid=(n // bq,),
        in_specs=[
            pl.BlockSpec((bq, HD), lambda i: (i, 0)),
            pl.BlockSpec((n, HD), lambda i: (0, 0)),
            pl.BlockSpec((HD, n), lambda i: (0, 0)),
        ],
        out_specs=[pl.BlockSpec((bq, HD), lambda i: (i, 0)), pl.BlockSpec((1, bq), lambda i: (0, i))],
        out_shape=[jax.ShapeDtypeStruct((n, HD), jnp.bfloat16), jax.ShapeDtypeStruct((1, n), jnp.float32)],
        compiler_params=pltpu.CompilerParams(vmem_limit_bytes=58 * 2**20),
    )(q, k, vt)


def attend_back_kernel(scale, q_ref, do_ref, lse_ref, k_ref, kt_ref, v_ref, dq_ref, dk_ref, dv_ref):
    @pl.when(pl.program_id(0) == 0)
    def _():
        dk_ref[...] = jnp.zeros_like(dk_ref)
        dv_ref[...] = jnp.zeros_like(dv_ref)

    p = jnp.exp(dot(k_ref[...], q_ref[...], 1, 1) * scale - lse_ref[...])
    dp = dot(v_ref[...], do_ref[...], 1, 1)
    delta = jnp.sum(p * dp, axis=0, keepdims=True)
    ds = (p * (dp - delta)).astype(jnp.bfloat16)
    dv_ref[...] += dot(p.astype(jnp.bfloat16), do_ref[...], 1, 0)
    dk_ref[...] += dot(ds, q_ref[...], 1, 0) * scale
    dq_ref[...] = (dot(kt_ref[...], ds, 1, 0) * scale).T


def attend_back(q, do, lse, k, kt, v):
    n = q.shape[0]
    bq = 256 if n <= 2048 else 128
    row = lambda i: (i, 0)
    whole = lambda i: (0, 0)
    f32 = jax.ShapeDtypeStruct((n, HD), jnp.float32)
    return pl.pallas_call(
        functools.partial(attend_back_kernel, 1.0 / math.sqrt(HD)),
        grid=(n // bq,),
        in_specs=[
            pl.BlockSpec((bq, HD), row),
            pl.BlockSpec((bq, HD), row),
            pl.BlockSpec((1, bq), lambda i: (0, i)),
            pl.BlockSpec((n, HD), whole),
            pl.BlockSpec((HD, n), whole),
            pl.BlockSpec((n, HD), whole),
        ],
        out_specs=[pl.BlockSpec((bq, HD), row), pl.BlockSpec((n, HD), whole), pl.BlockSpec((n, HD), whole)],
        out_shape=[f32, f32, f32],
        compiler_params=pltpu.CompilerParams(vmem_limit_bytes=58 * 2**20),
    )(q, do, lse, k, kt, v)


def to_all(v):
    return lax.all_to_all(v, AXES, split_axis=0, concat_axis=0, tiled=True)


def body(tokens, w_query, w_key, w_value, w_out, attn_gain, ffn_gain, qk_gain,
         expert_gate, expert_up, expert_down, routes, gates, order, cotangent):
    f32, bf16 = jnp.float32, jnp.bfloat16
    positions, seqs, D = tokens.shape
    U, B = lax.axis_size("ulysses"), lax.axis_size("blk")
    F = U * B
    u, b = lax.axis_index("ulysses"), lax.axis_index("blk")
    H = w_query.shape[1] // HD
    W = w_query.shape[0]
    L = F * positions
    T = seqs * positions
    top_count = routes.shape[-1]
    local_experts = expert_gate.shape[0]
    E = local_experts * B
    chips = F // 2
    R = chips // H
    chip_of = np.array([(d // B // 2) * B + d % B for d in range(F)])
    head_of, seq_of = chip_of // R, np.array([(d // B) % 2 for d in range(F)])
    first_copy = lax.rem((u // 2) * B + b, R) == 0

    tok = tokens.transpose(1, 0, 2)
    cot = cotangent.transpose(1, 0, 2)
    rows_f = tok.reshape(T, D).astype(f32)

    gains_all = lax.all_gather(
        jnp.concatenate([attn_gain, ffn_gain, qk_gain[0], qk_gain[1]]), AXES, axis=0).astype(f32)
    nq = qk_gain.shape[1]
    attn_g = gains_all[:, :W].reshape(-1)
    ffn_g = gains_all[:, W:2 * W].reshape(-1)
    qk_g = jnp.stack([gains_all[:, 2 * W:2 * W + nq].reshape(-1), gains_all[:, 2 * W + nq:].reshape(-1)])
    seq_tok = gather_blocks(tok, U, B, True, 1).reshape(L, D)
    heads_w = jnp.stack([w_query, w_key, w_value]).reshape(3, W, H, HD).transpose(2, 1, 0, 3).reshape(H, W, 3 * HD)
    head_w = to_all(heads_w[head_of]).reshape(D, 3 * HD)
    out_w = lax.all_gather(w_out, AXES, axis=0, tiled=True)

    expert_of = routes.transpose(1, 0, 2).reshape(-1)
    prio = order.reshape(positions, seqs, top_count).transpose(1, 0, 2).reshape(-1)
    same = expert_of[:, None] == expert_of[None, :]
    ranks = jnp.sum((same & (prio[None, :] < prio[:, None])).astype(jnp.int32), axis=1)
    slot = jnp.where(ranks < CAP, expert_of * CAP + ranks, -1).astype(f32)
    gate_flat = gates.transpose(1, 0, 2).reshape(-1)
    table = lax.all_gather(jnp.stack([slot, gate_flat]), AXES, axis=0)
    GB = 4
    G = F // GB
    KB = GB * T
    RB = -(-GB * CAP // 16) * 16
    span = E * CAP
    slot_all = table[:, 0].astype(jnp.int32).reshape(G, GB, T, top_count)
    code = jnp.where(slot_all >= 0, slot_all + jnp.arange(GB, dtype=jnp.int32)[None, :, None, None] * span, -1)
    code = code.reshape(G, KB, top_count)
    gate_all = table[:, 1].reshape(G, KB, top_count)
    r_ix = np.arange(RB)
    r_code = np.where(r_ix < GB * CAP, (r_ix // CAP) * span + r_ix % CAP, -(1 << 24)).astype(np.int32)
    want = (b * local_experts + jnp.arange(local_experts, dtype=jnp.int32))[:, None] * CAP + r_code[None, :]
    onehot = jnp.zeros((G, local_experts, RB, KB), jnp.bool_)
    row_gate = jnp.zeros((G, local_experts, RB), f32)
    for j in range(top_count):
        hit = code[:, None, None, :, j] == want[None, :, :, None]
        onehot = onehot | hit
        row_gate = row_gate + jnp.sum(jnp.where(hit, gate_all[:, None, None, :, j], 0.0), axis=-1)
    onehot = onehot.astype(bf16)
    row_gate = row_gate.transpose(1, 0, 2).reshape(local_experts, G * RB, 1)

    def first_norm(v):
        return rms_norm(v, attn_g)

    hidden = first_norm(seq_tok.astype(f32)).astype(bf16)
    raw = jnp.dot(hidden, head_w, preferred_element_type=f32)

    def head_norms(query_in, key_in, gains):
        return rotate(rms_norm(query_in, gains[0])), rotate(rms_norm(key_in, gains[1]))

    (rot_q, rot_k), heads_back = jax.vjp(head_norms, raw[:, :HD], raw[:, HD:2 * HD], qk_g)
    q, k, v = rot_q.astype(bf16), rot_k.astype(bf16), raw[:, 2 * HD:].astype(bf16)
    att, lse = attend(q, k, v.T)
    att_rows = to_all(att.reshape(F, positions, HD))

    def from_heads(m):
        m = m.reshape(U // 2, 2, B, positions, HD).transpose(1, 3, 0, 2, 4)
        return m.reshape(2, positions, H, R, HD)[:, :, :, 0].reshape(T, H * HD)

    attended = from_heads(att_rows)
    residual = rows_f + jnp.dot(attended, out_w, preferred_element_type=f32)
    normed_full, ffn_back = jax.vjp(rms_norm, residual, ffn_g)
    normed = normed_full.astype(bf16).reshape(2, positions, D)

    normed_all = gather_blocks(normed, U, B, False, 2).reshape(G, KB, D)
    cot_all = gather_blocks(cot, U, B, False, 2).reshape(G, KB, D)

    def dispatch(m):
        x = jnp.einsum("gert,gtd->egrd", onehot, m, preferred_element_type=f32)
        return x.reshape(local_experts, G * RB, D)

    def combine(m):
        m = m.reshape(local_experts, G, RB, D)
        return jnp.einsum("gert,egrd->gtd", onehot, m, preferred_element_type=f32).astype(bf16).reshape(F, 2, positions, D)

    x = dispatch(normed_all).astype(bf16)
    pair_grad = (dispatch(cot_all) * row_gate).astype(bf16)
    gate_act = jnp.einsum("erd,edf->erf", x, expert_gate, preferred_element_type=f32)
    up_act = jnp.einsum("erd,edf->erf", x, expert_up, preferred_element_type=f32)
    sigma = jax.nn.sigmoid(gate_act)
    inner = (gate_act * sigma * up_act).astype(bf16)
    part = jnp.einsum("erf,efd->erd", inner, expert_down, preferred_element_type=f32)
    mixed_part = combine((part * row_gate).astype(bf16))
    mixed = residual + scatter_blocks(mixed_part, U, B, False, 3).reshape(T, D)
    mixed = mixed.reshape(2, positions, D).transpose(1, 0, 2).astype(bf16)
    inner_grad = jnp.einsum("erd,efd->erf", pair_grad, expert_down, preferred_element_type=f32)
    gate_act_grad = (inner_grad * up_act * sigma * (1.0 + gate_act * (1.0 - sigma))).astype(bf16)
    up_act_grad = (inner_grad * gate_act * sigma).astype(bf16)
    row_grads = (
        jnp.einsum("erf,edf->erd", gate_act_grad, expert_gate, preferred_element_type=f32)
        + jnp.einsum("erf,edf->erd", up_act_grad, expert_up, preferred_element_type=f32)
    )
    gate_grad = jnp.einsum("erd,erf->edf", x, gate_act_grad, preferred_element_type=f32)
    up_grad = jnp.einsum("erd,erf->edf", x, up_act_grad, preferred_element_type=f32)
    down_grad = jnp.einsum("erf,erd->efd", inner, pair_grad, preferred_element_type=f32)
    normed_grad = scatter_blocks(combine(row_grads.astype(bf16)), U, B, False, 3).reshape(T, D)

    residual_norm_grad, ffn_gain_part = ffn_back(normed_grad)
    residual_grad = cot.reshape(T, D).astype(f32) + residual_norm_grad
    attn_out_grad = residual_grad.astype(bf16)
    att_grad = dot(attn_out_grad, out_w, 1, 1).astype(bf16)
    att_grad = att_grad.reshape(2, positions, H, HD)
    to_heads = jnp.stack([att_grad[seq_of[d], :, head_of[d]] for d in range(F)])
    do = to_all(to_heads).reshape(L, HD)
    out_part = dot(attended, attn_out_grad, 0, 0).astype(bf16)
    out_part = out_part.reshape(F, W, 2, D // 2).transpose(0, 2, 1, 3)
    out_grad = scatter_blocks(out_part, U, B, False, 5).transpose(1, 0, 2).reshape(W, D)
    dq, dk, dv = attend_back(q, do, lse, k, k.T, v)
    query_raw_grad, key_raw_grad, qk_part = heads_back(
        (dq.astype(bf16).astype(f32), dk.astype(bf16).astype(f32)))
    head_grad = jnp.concatenate(
        [query_raw_grad.astype(bf16), key_raw_grad.astype(bf16), dv.astype(bf16)], axis=-1)
    head_grad = jnp.where(first_copy, head_grad, jnp.zeros_like(head_grad))
    qk_part = jnp.where(first_copy, qk_part, 0.0)
    weight_part = to_all(dot(hidden, head_grad, 0, 0).astype(bf16).reshape(F, W, 3 * HD))
    weight_grad = jnp.sum(weight_part.reshape(U // 2, 2, B, W, 3 * HD).astype(f32), axis=1)
    weight_grad = weight_grad.reshape(H, R, W, 3 * HD).sum(axis=1).transpose(1, 0, 2).reshape(W, H, 3, HD)
    query_grad, key_grad, value_grad = (weight_grad[:, :, n].reshape(W, H * HD) for n in range(3))
    hidden_part = dot(head_grad, head_w, 1, 1).astype(bf16).reshape(F, positions, D)
    hidden_grad = scatter_blocks(hidden_part, U, B, True, 4).reshape(T, D)
    _, attn_back = jax.vjp(rms_norm, rows_f, attn_g)
    token_grad, attn_gain_part = attn_back(hidden_grad)
    input_grad = (residual_grad + token_grad).reshape(2, positions, D).transpose(1, 0, 2)
    small = jnp.concatenate(
        [attn_gain_part.reshape(F, W), ffn_gain_part.reshape(F, W),
         qk_part[0].reshape(F, nq), qk_part[1].reshape(F, nq)], axis=1)
    small = jnp.sum(to_all(small), axis=0)
    return (
        mixed, input_grad, query_grad, key_grad, value_grad, out_grad,
        small[:W], small[W:2 * W], small[2 * W:].reshape(2, nq),
        gate_grad, up_grad, down_grad,
    )


def solution(mesh):
    rows = P(AXES, None, None)
    flat = P(AXES, None)
    by_expert = (P("blk", None, "ulysses"), P("blk", None, "ulysses"), P("blk", "ulysses", None))
    in_specs = (rows, flat, flat, flat, flat, P(AXES), P(AXES), P(None, AXES)) + by_expert + (rows, rows, flat, rows)
    out_specs = (rows, rows, flat, flat, flat, flat, P(AXES), P(AXES), P(None, AXES)) + by_expert
    return jax.shard_map(body, mesh=mesh, in_specs=in_specs, out_specs=out_specs, check_vma=False)
```

```python
import functools
import math

import jax
import jax.numpy as jnp
import numpy as np
from jax import lax
from jax.experimental import pallas as pl
from jax.experimental.pallas import tpu as pltpu
from jax.sharding import PartitionSpec as P

HD = 128
CAP = 18
EPSILON = 1e-06
ROPE_BASE = 10000.0
AXES = ("ulysses", "blk")
MESH = pl.DeviceIdType.MESH


class Place:
    def __init__(self, U, B):
        self.U, self.B = U, B
        self.X, self.Y = U // 2, 2
        self.Z = B // self.Y
        self.Q, self.F = self.X * B, U * B
        u, b = lax.axis_index("ulysses"), lax.axis_index("blk")
        self.c, self.x = lax.rem(u, 2), lax.div(u, 2)
        self.y, self.z = lax.rem(b, self.Y), lax.div(b, self.Y)
        self.q = self.x * B + b
        self.me, self.sib = self.at(self.q, self.c), self.at(self.q, 1 - self.c)
        self.core_peer = self.dev(self.x, self.y, self.z, 1 - self.c)

    def dev(self, x, y, z, c):
        return (x * 2 + c, z * self.Y + y)

    def block(self, x, y, z, c):
        return (x * 2 + c) * self.B + z * self.Y + y

    def chip(self, x, y, z):
        return x * self.B + z * self.Y + y

    def at(self, q, c):
        return (lax.div(q, self.B) * 2 + c) * self.B + lax.rem(q, self.B)

    def chip_dev(self, q):
        return (lax.div(q, self.B) * 2 + self.c, lax.rem(q, self.B))

    def flat_dev(self, f):
        return (lax.div(f, self.B), lax.rem(f, self.B))

    def others(self, axis):
        n = {"x": self.X, "y": self.Y, "z": self.Z}[axis]
        i = {"x": self.x, "y": self.y, "z": self.z}[axis]
        return [lax.rem(i + o, n) for o in range(1, n)]

    def barrier(self, reach):
        sem = pltpu.get_barrier_semaphore()

        def greet(d):
            pl.semaphore_signal(sem, inc=1, device_id=d, device_id_type=MESH)

        if reach == "every":
            @pl.loop(1, self.F)
            def _(o):
                greet(self.flat_dev(lax.rem(self.me + o, self.F)))

            pl.semaphore_wait(sem, self.F - 1)
            return
        greet(self.core_peer)
        if reach == "all":
            @pl.loop(1, self.Q)
            def _(o):
                greet(self.chip_dev(lax.rem(self.q + o, self.Q)))

            pl.semaphore_wait(sem, self.Q)
            return
        for k in self.others("x"):
            greet(self.dev(k, self.y, self.z, self.c))
        for k in self.others("y"):
            greet(self.dev(self.x, k, self.z, self.c))
        count = self.X + self.Y - 1
        if reach == "chain":
            below, above = self.z > 0, self.z < self.Z - 1

            @pl.when(below)
            def _():
                greet(self.dev(self.x, self.y, self.z - 1, self.c))

            @pl.when(above)
            def _():
                greet(self.dev(self.x, self.y, self.z + 1, self.c))

            count = count + jnp.where(below, 1, 0) + jnp.where(above, 1, 0)
        else:
            for k in self.others("z"):
                greet(self.dev(self.x, self.y, k, self.c))
            count += self.Z - 1
        pl.semaphore_wait(sem, count)


def remote(src, dst, send, recv, dev):
    return pltpu.make_async_remote_copy(
        src_ref=src, dst_ref=dst, send_sem=send, recv_sem=recv, device_id=dev, device_id_type=MESH)


class Gather:
    def __init__(self, p, by_seq, src, out, send_sem, recv_sem, local_sem):
        self.p, self.by_seq, self.src, self.out = p, by_seq, src, out
        self.send_sem, self.recv_sem, self.local_sem = send_sem, recv_sem, local_sem
        self.steps = p.Z + 2
        self.started = []
        self.always = p.z >= 0

    @staticmethod
    def semaphores(U, B, by_seq):
        n = 1 if by_seq else 2
        dma = pltpu.SemaphoreType.DMA
        return [dma((4 + U // 2 - 1 + 1, n, U * B)), dma((n, U * B)), dma((1,))]

    def where(self, half, x, y, z):
        p = self.p
        if self.by_seq:
            f = p.block(x, y, z, half)
            return self.out.at[f], (0, f)
        f = p.block(x, y, z, p.c)
        return self.out.at[f, half], (half, f)

    def send(self, cond, src_ref, dst_ref, ix, way, dev):
        cp = remote(src_ref, dst_ref, self.send_sem.at[(way,) + ix], self.recv_sem.at[ix], dev)

        @pl.when(cond)
        def _():
            cp.start()

        self.started.append((cond, cp))

    def wait(self, ref, ix):
        remote(ref, ref, self.send_sem.at[(0,) + ix], self.recv_sem.at[ix], self.p.core_peer).wait_recv()

    def along(self, cond, half, x, y, z, axes):
        p = self.p
        ref, ix = self.where(half, x, y, z)
        for ax in axes:
            if ax == "core":
                if not self.by_seq:
                    self.send(cond, ref, ref, ix, 0, p.core_peer)
            elif ax == "up":
                self.send(cond & (p.z < p.Z - 1), ref, ref, ix, 1, p.dev(p.x, p.y, p.z + 1, p.c))
            elif ax == "down":
                self.send(cond & (p.z > 0), ref, ref, ix, 2, p.dev(p.x, p.y, p.z - 1, p.c))
            elif ax == "y":
                for i, k in enumerate(p.others("y")):
                    self.send(cond, ref, ref, ix, 3 + i, p.dev(p.x, k, p.z, p.c))
            else:
                for i, k in enumerate(p.others("x")):
                    self.send(cond, ref, ref, ix, 2 + p.Y + i, p.dev(k, p.y, p.z, p.c))

    def zs(self, step):
        p = self.p
        if step == 0:
            return [(self.always, p.z, ())]
        return [(p.z - step >= 0, p.z - step, ("up",)), (p.z + step < p.Z, p.z + step, ("down",))]

    def arrive(self, cond, half, x, y, z, axes):
        ref, ix = self.where(half, x, y, z)

        @pl.when(cond)
        def _():
            self.wait(ref, ix)

        self.along(cond, half, x, y, z, axes)

    def step(self, n):
        p = self.p
        if n == 0:
            if self.by_seq:
                cp = pltpu.make_async_copy(self.src.at[p.c], self.out.at[p.me], self.local_sem.at[0])
                cp.start()
                self.send(self.always, self.src.at[1 - p.c], self.out.at[p.me], (0, p.me), 0, p.core_peer)
                cp.wait()
                self.wait(self.out.at[p.sib], (0, p.sib))
            else:
                cp = pltpu.make_async_copy(self.src, self.out.at[p.me], self.local_sem.at[0])
                cp.start()
                cp.wait()
            for half in (0, 1):
                self.along(self.always, half, p.x, p.y, p.z, ("up", "down", "y", "x"))
            for half in (0, 1):
                self.along(self.always, half, p.x, p.y, p.z, ("core",))
            return
        if n < p.Z:
            for half in (0, 1):
                for cond, k, on in self.zs(n):
                    self.arrive(cond, half, p.x, p.y, k, on + ("y", "x", "core"))
        if n <= p.Z:
            for cond, k, _ in self.zs(n - 1):
                for j in p.others("y"):
                    self.arrive(cond, 0, p.x, j, k, ("x", "core"))
                for j in p.others("x"):
                    self.arrive(cond, 1, j, p.y, k, ("y", "core"))
        if n >= 2:
            for cond, k, _ in self.zs(n - 2):
                for j in p.others("x"):
                    self.arrive(cond, 0, j, p.y, k, ("core",))
                for i in p.others("y"):
                    self.arrive(cond, 1, p.x, i, k, ("core",))
                for j in p.others("x"):
                    for i in p.others("y"):
                        self.arrive(cond, 0, j, i, k, ("core",))
                        self.arrive(cond, 1, j, i, k, ("core",))

    def from_core(self, cond, x, y, z):
        f = self.p.block(x, y, z, 1 - self.p.c)

        @pl.when(cond)
        def _():
            for half in (0, 1):
                self.wait(self.out.at[f, half], (half, f))

    def end(self):
        p = self.p
        if not self.by_seq:
            for k in range(p.Z):
                for j in range(p.X):
                    for i in range(p.Y):
                        self.from_core(self.always, j, i, k)
        self.sent()

    def sent(self):
        for cond, cp in self.started:
            @pl.when(cond)
            def _(cp=cp):
                cp.wait_send()


class Spread:
    def __init__(self, p, same, src, out, send_sem, recv_sem):
        self.p, self.same, self.src, self.out = p, same, src, out
        self.send_sem, self.recv_sem = send_sem, recv_sem

    @staticmethod
    def semaphores(U, B):
        dma = pltpu.SemaphoreType.DMA
        return [dma((2, U * B // 2)), dma((U * B,))]

    def part(self, q):
        return self.src if self.same else self.src.at[q]

    def out_to(self, o):
        p = self.p
        q = lax.rem(p.q + o, p.Q)
        return remote(self.part(q), self.out.at[p.me], self.send_sem.at[0, q], self.recv_sem.at[p.me], p.chip_dev(q))

    def across(self, q):
        f = self.p.at(q, self.p.c)
        return remote(self.out.at[f], self.out.at[f], self.send_sem.at[1, q], self.recv_sem.at[f], self.p.core_peer)

    def arrive(self, f):
        remote(self.out.at[f], self.out.at[f], self.send_sem.at[0, 0], self.recv_sem.at[f], self.p.core_peer).wait_recv()

    def begin(self):
        p = self.p

        @pl.loop(1, p.Q)
        def _(o):
            self.out_to(o).start()

        cp = pltpu.make_async_copy(self.part(p.q), self.out.at[p.me], self.send_sem.at[0, p.q])
        cp.start()
        cp.wait()
        self.across(p.q).start()

    def middle(self):
        p = self.p

        @pl.loop(1, p.Q)
        def _(o):
            q = lax.rem(p.q + o, p.Q)
            self.arrive(p.at(q, p.c))
            self.across(q).start()

    def end(self):
        p = self.p

        @pl.loop(0, p.Q)
        def _(q):
            self.arrive(p.at(q, 1 - p.c))
            self.across(q).wait_send()

        @pl.loop(1, p.Q)
        def _(o):
            self.out_to(o).wait_send()


def any_specs(n):
    return [pl.BlockSpec(memory_space=pl.ANY)] * n


def gather_kernel(U, B, by_seq, src, out, *sems):
    p = Place(U, B)
    p.barrier("chain")
    g = Gather(p, by_seq, src, out, *sems)
    for n in range(g.steps):
        g.step(n)
    g.end()


def gather_blocks(v, U, B, by_seq, cid):
    shape = (U * B,) + (v.shape[1:] if by_seq else v.shape)
    return pl.pallas_call(
        functools.partial(gather_kernel, U, B, by_seq),
        out_shape=jax.ShapeDtypeStruct(shape, v.dtype),
        in_specs=any_specs(1),
        out_specs=any_specs(1)[0],
        scratch_shapes=Gather.semaphores(U, B, by_seq),
        compiler_params=pltpu.CompilerParams(collective_id=cid, has_side_effects=True),
    )(v)


def front_kernel(U, B, tok, small, weights, tok_out, small_out, weights_out, *sems):
    p = Place(U, B)
    p.barrier("all")
    g = Gather(p, True, tok, tok_out, *sems[:3])
    s = Spread(p, True, small, small_out, *sems[3:5])
    w = Spread(p, False, weights, weights_out, *sems[5:7])
    s.begin()
    g.step(0)
    w.begin()
    for n in range(1, g.steps):
        g.step(n)
        if n == 1:
            s.middle()
        if n == 2:
            w.middle()
    s.end()
    w.end()
    g.end()


def front(tok, small, weights, U, B, cid):
    F = U * B
    return pl.pallas_call(
        functools.partial(front_kernel, U, B),
        out_shape=[
            jax.ShapeDtypeStruct((F,) + tok.shape[1:], tok.dtype),
            jax.ShapeDtypeStruct((F,) + small.shape, small.dtype),
            jax.ShapeDtypeStruct((F,) + weights.shape[1:], weights.dtype),
        ],
        in_specs=any_specs(3),
        out_specs=any_specs(3),
        scratch_shapes=Gather.semaphores(U, B, True) + Spread.semaphores(U, B) * 2,
        compiler_params=pltpu.CompilerParams(collective_id=cid, has_side_effects=True),
    )(tok, small, weights)


def exchange_kernel(U, B, src, out, send_sem, recv_sem):
    p = Place(U, B)
    p.barrier("every")

    def copy(o):
        f = lax.rem(p.me + o, p.F)
        return f, remote(src.at[f], out.at[p.me], send_sem.at[f], recv_sem.at[p.me], p.flat_dev(f))

    @pl.loop(1, p.F)
    def _(o):
        copy(o)[1].start()

    cp = pltpu.make_async_copy(src.at[p.me], out.at[p.me], recv_sem.at[p.me])
    cp.start()
    cp.wait()

    @pl.loop(1, p.F)
    def _(o):
        f, cp = copy(o)
        remote(out.at[f], out.at[f], send_sem.at[f], recv_sem.at[f], p.flat_dev(f)).wait_recv()
        cp.wait_send()


def exchange(v, U, B, cid):
    return pl.pallas_call(
        functools.partial(exchange_kernel, U, B),
        out_shape=jax.ShapeDtypeStruct(v.shape, v.dtype),
        in_specs=any_specs(1),
        out_specs=any_specs(1)[0],
        scratch_shapes=[pltpu.SemaphoreType.DMA((U * B,))] * 2,
        compiler_params=pltpu.CompilerParams(collective_id=cid, has_side_effects=True),
    )(v)


class Scatter:
    def __init__(self, p, by_seq, acc, rc, rx0, rx1, ry0, ry1, rz, fin, loc, cs, cr, xs, xr, ys, yr, zs, zr):
        self.p, self.by_seq = p, by_seq
        self.acc, self.rc, self.rx, self.ry, self.rz, self.fin = acc, rc, (rx0, rx1), (ry0, ry1), rz, fin
        self.loc, self.cs, self.cr = loc, cs, cr
        self.xs, self.xr, self.ys, self.yr, self.zs, self.zr = xs, xr, ys, yr, zs, zr
        self.order = p.others("z") + [p.z]
        self.steps = p.Z + 2
        self.started = []
        self.local = True

    @staticmethod
    def scratch(U, B, by_seq, rows, D, t):
        X, Y, Z, Q = U // 2, 2, B // 2, U * B // 2
        dma = pltpu.SemaphoreType.DMA
        x, y = max(X - 1, 1), Y - 1
        return [
            pltpu.VMEM((Q, 2, rows, D), t),
            pltpu.VMEM((1, 1, 16, 128) if by_seq else (Q, 2, rows, D), t),
            pltpu.VMEM((x, Z * Y, rows, D), t),
            pltpu.VMEM((x, Z, rows, D), t),
            pltpu.VMEM((y, Z, rows, D), t),
            pltpu.VMEM((y, Z * X, rows, D), t),
            pltpu.VMEM((2, Z, rows, D), t),
            pltpu.VMEM((2, rows, D), jnp.float32),
            dma((Q, 2)),
            dma((Q, 2)),
            dma((Q, 2)),
            dma((2, x, Z * Y)),
            dma((2, x, Z * Y)),
            dma((2, y, Z * X)),
            dma((2, y, Z * X)),
            dma((2, Z)),
            dma((2, Z)),
        ]

    SCRATCH = 17

    def start(self, *a):
        cp = remote(*a)
        cp.start()
        self.started.append(cp)

    def got(self, ref, sem):
        remote(ref, ref, sem, sem, self.p.core_peer).wait_recv()

    def pieces(self, k):
        p = self.p
        ox, oy = p.others("x"), p.others("y")
        return (
            [(0, j, i, k) for j in ox for i in range(p.Y)] + [(1, j, i, k) for i in oy for j in range(p.X)],
            [(0, p.x, i, k) for i in oy] + [(1, j, p.y, k) for j in ox],
            [(0, p.x, p.y, k), (1, p.x, p.y, k)],
        )

    def load(self, src):
        p = self.p
        for k in self.order:
            for some in self.pieces(k):
                for h, j, i, _ in some:
                    q = p.chip(j, i, k)
                    if self.by_seq:
                        mine = src.at[p.block(j, i, k, h)]
                    else:
                        self.across(src.at[p.block(j, i, k, 1 - p.c), h], q, h)
                        mine = src.at[p.block(j, i, k, p.c), h]
                    pltpu.make_async_copy(mine, self.acc.at[q, h], self.loc.at[q, h]).start()

    def across(self, src, q, h):
        self.start(src, self.rc.at[q, h], self.cs.at[q, h], self.cr.at[q, h], self.p.core_peer)

    def ready(self, h, j, i, k):
        q = self.p.chip(j, i, k)
        if self.local:
            pltpu.make_async_copy(self.acc.at[q, h], self.acc.at[q, h], self.loc.at[q, h]).wait()
        if self.by_seq:
            return []
        self.got(self.rc.at[q, h], self.cr.at[q, h])
        return [self.rc.at[q, h]]

    def add(self, dst, srcs, f32_out=None):
        if not srcs and f32_out is None:
            return
        step = 16

        def one(n, _):
            r = pl.ds(pl.multiple_of(n * step, step), step)
            t = dst[r, :].astype(jnp.float32)
            for s in srcs:
                t = t + s[r, :].astype(jnp.float32)
            if f32_out is None:
                dst[r, :] = t.astype(dst.dtype)
            else:
                f32_out[r, :] = t
            return 0

        lax.fori_loop(0, dst.shape[0] // step, one, 0)

    def send_x(self, h, q, j, s):
        p = self.p
        o = lax.rem(j - p.x + p.X, p.X) - 1
        self.start(self.acc.at[q, h], self.rx[h].at[o, s], self.xs.at[h, o, s], self.xr.at[h, o, s],
                   p.dev(j, p.y, p.z, p.c))

    def send_y(self, h, q, i, s):
        p = self.p
        o = lax.rem(i - p.y + p.Y, p.Y) - 1
        self.start(self.acc.at[q, h], self.ry[h].at[o, s], self.ys.at[h, o, s], self.yr.at[h, o, s],
                   p.dev(p.x, i, p.z, p.c))

    def from_x(self, h, s):
        out = []
        for o in range(self.p.X - 1):
            self.got(self.rx[h].at[o, s], self.xr.at[h, o, s])
            out.append(self.rx[h].at[o, s])
        return out

    def from_y(self, h, s):
        out = []
        for o in range(self.p.Y - 1):
            self.got(self.ry[h].at[o, s], self.yr.at[h, o, s])
            out.append(self.ry[h].at[o, s])
        return out

    def step(self, n):
        p = self.p
        X, Y, Z = p.X, p.Y, p.Z
        if n < Z:
            k = self.order[n]
            for h, j, i, _ in self.pieces(k)[0]:
                q = p.chip(j, i, k)
                self.add(self.acc.at[q, h], self.ready(h, j, i, k))
                if h == 0:
                    self.send_x(0, q, j, k * Y + i)
                else:
                    self.send_y(1, q, i, k * X + j)
        if 1 <= n <= Z:
            k = self.order[n - 1]
            for h, j, i, _ in self.pieces(k)[1]:
                q = p.chip(j, i, k)
                extra = self.ready(h, j, i, k)
                if h == 0:
                    self.add(self.acc.at[q, 0], extra + self.from_x(0, k * Y + i))
                    self.send_y(0, q, i, k)
                else:
                    self.add(self.acc.at[q, 1], extra + self.from_y(1, k * X + j))
                    self.send_x(1, q, j, k)
        if n >= 2:
            k = self.order[n - 2]
            for h, j, i, _ in self.pieces(k)[2]:
                q = p.chip(j, i, k)
                extra = self.ready(h, j, i, k)
                if h == 0:
                    extra = extra + self.from_x(0, k * Y + i) + self.from_y(0, k)
                else:
                    extra = extra + self.from_y(1, k * X + j) + self.from_x(1, k)
                if n - 2 < Z - 1:
                    self.add(self.acc.at[q, h], extra)
                    self.start(self.acc.at[q, h], self.rz.at[h, p.z], self.zs.at[h, k], self.zr.at[h, p.z],
                               p.dev(p.x, p.y, k, p.c))
                else:
                    for a in p.others("z"):
                        self.got(self.rz.at[h, a], self.zr.at[h, a])
                        extra.append(self.rz.at[h, a])
                    self.add(self.acc.at[q, h], extra, self.fin.at[h])

    def sent(self):
        for cp in self.started:
            cp.wait_send()


def give(p, by_seq, fin, out, sems):
    if by_seq:
        away = remote(fin.at[1 - p.c], out.at[p.c], sems.at[0], sems.at[1], p.core_peer)
        away.start()
        cp = pltpu.make_async_copy(fin.at[p.c], out.at[p.c], sems.at[2])
        cp.start()
        cp.wait()
        remote(out.at[1 - p.c], out.at[1 - p.c], sems.at[0], sems.at[1], p.core_peer).wait_recv()
        away.wait_send()
    else:
        cp = pltpu.make_async_copy(fin, out, sems.at[2])
        cp.start()
        cp.wait()


def scatter_kernel(U, B, by_seq, src, out, *scratch):
    p = Place(U, B)
    p.barrier("lines")
    s = Scatter(p, by_seq, *scratch[:Scatter.SCRATCH])
    s.load(src)
    for n in range(s.steps):
        s.step(n)
    give(p, by_seq, s.fin, out, scratch[-1])
    s.sent()


def in_parts(call, v, F, D):
    parts = max(1, F * D // 65536)
    w = D // parts
    return jnp.concatenate([call(v[..., n * w:(n + 1) * w]) for n in range(parts)], axis=-1)


def scatter_blocks(v, U, B, by_seq, cid):
    def call(m):
        rows, D = m.shape[-2:]
        return pl.pallas_call(
            functools.partial(scatter_kernel, U, B, by_seq),
            out_shape=jax.ShapeDtypeStruct((2, rows, D), jnp.float32),
            in_specs=any_specs(1),
            out_specs=any_specs(1)[0],
            scratch_shapes=Scatter.scratch(U, B, by_seq, rows, D, m.dtype) + [pltpu.SemaphoreType.DMA((3,))],
            compiler_params=pltpu.CompilerParams(
                collective_id=cid, has_side_effects=True, vmem_limit_bytes=58 * 2**20),
        )(m)

    return in_parts(call, v, U * B, v.shape[-1])


def pair_kernel(U, B, n, *refs):
    p = Place(U, B)
    p.barrier("lines")
    srcs, outs, scratch = refs[:n], refs[n:2 * n], refs[2 * n:]
    work = [Scatter(p, False, *scratch[Scatter.SCRATCH * i:Scatter.SCRATCH * (i + 1)]) for i in range(n)]
    for s, src in zip(work, srcs):
        s.load(src)
    for k in range(work[0].steps):
        for s in work:
            s.step(k)
    for i, s in enumerate(work):
        give(p, False, s.fin, outs[i], scratch[-1])
        s.sent()


def scatter_pair(a, b, U, B, cid):
    def call(v, w):
        rows, D = v.shape[-2:]
        return pl.pallas_call(
            functools.partial(pair_kernel, U, B, 2),
            out_shape=[jax.ShapeDtypeStruct((2, rows, D), jnp.float32)] * 2,
            in_specs=any_specs(2),
            out_specs=any_specs(2),
            scratch_shapes=Scatter.scratch(U, B, False, rows, D, v.dtype) * 2 + [pltpu.SemaphoreType.DMA((3,))],
            compiler_params=pltpu.CompilerParams(
                collective_id=cid, has_side_effects=True, vmem_limit_bytes=60 * 2**20),
        )(v, w)

    parts = max(1, U * B // 32)
    w = a.shape[-1] // parts
    got = [call(a[..., n * w:(n + 1) * w], b[..., n * w:(n + 1) * w]) for n in range(parts)]
    return tuple(jnp.concatenate([g[i] for g in got], axis=-1) for i in range(2))


class PairExchange:
    def __init__(self, p, src, out, acc, rc, local, send, recv):
        self.p, self.src, self.out, self.acc, self.rc = p, src, out, acc, rc
        self.local, self.send, self.recv = local, send, recv

    @staticmethod
    def scratch(U, B, rows, w, t):
        X, Q = U // 2, U * B // 2
        dma = pltpu.SemaphoreType.DMA
        return [pltpu.VMEM((Q, rows, w), t), pltpu.VMEM((Q, rows, w), t),
                dma((X,)), dma((X + Q,)), dma((X + Q,))]

    SCRATCH = 5

    def across(self, j):
        p = self.p
        part = self.rc.at[pl.ds(j * p.B, p.B)]
        return remote(self.src.at[j, 1 - p.c], part, self.send.at[j], self.recv.at[j], p.core_peer)

    def own(self, j):
        p = self.p
        return pltpu.make_async_copy(self.src.at[j, p.c], self.acc.at[pl.ds(j * p.B, p.B)], self.local.at[j])

    def away(self, o):
        p = self.p
        q = lax.rem(p.q + o, p.Q)
        return remote(self.acc.at[q], self.out.at[p.q], self.send.at[p.X + q], self.recv.at[p.X + p.q], p.chip_dev(q))

    def begin(self):
        for j in range(self.p.X):
            self.across(j).start()
            self.own(j).start()

    def middle(self):
        p = self.p
        for j in range(p.X):
            self.own(j).wait()
            self.across(j).wait_recv()

        @pl.loop(0, p.Q)
        def _(q):
            t = self.acc[q].astype(jnp.float32) + self.rc[q].astype(jnp.float32)
            self.acc[q] = t.astype(self.acc.dtype)

        @pl.loop(1, p.Q)
        def _(o):
            self.away(o).start()

        cp = pltpu.make_async_copy(self.acc.at[p.q], self.out.at[p.q], self.local.at[0])
        cp.start()
        cp.wait()

    def end(self):
        p = self.p
        for j in range(p.X):
            self.across(j).wait_send()

        @pl.loop(1, p.Q)
        def _(o):
            q = lax.rem(p.q + o, p.Q)
            part = self.out.at[q]
            remote(part, part, self.send.at[0], self.recv.at[p.X + q], p.core_peer).wait_recv()
            self.away(o).wait_send()


def finish_kernel(U, B, more, *refs):
    p = Place(U, B)
    p.barrier("all")
    n = 4 if more else 3
    srcs, outs, scratch = refs[:n], refs[n:2 * n], refs[2 * n:]
    k = Scatter.SCRATCH
    work = [Scatter(p, True, *scratch[:k])]
    if more:
        work.append(Scatter(p, False, *scratch[k:2 * k]))
    ex, at = [], k * len(work)
    for i in range(2):
        ex.append(PairExchange(p, srcs[i], outs[i], *scratch[at:at + PairExchange.SCRATCH]))
        at += PairExchange.SCRATCH
    for e in ex:
        e.begin()
    for s, src in zip(work, srcs[2:]):
        s.load(src)
    work[0].step(0)
    for e in ex:
        e.middle()
    for s in work[1:]:
        s.step(0)
    for j in range(1, p.Z + 2):
        for s in work:
            s.step(j)
    for s, out, by_seq in zip(work, outs[2:], (True, False)):
        give(p, by_seq, s.fin, out, scratch[-1])
    for s in work:
        s.sent()
    for e in ex:
        e.end()


def finish(weights, small, hidden, out, U, B, cid):
    X, F, Q = U // 2, U * B, U * B // 2
    parts = max(1, F // 32)
    rows, D = hidden.shape[-2:]
    D = D // parts
    sds, f32 = jax.ShapeDtypeStruct, jnp.float32

    def call(w, s, h, o):
        args = [w.reshape((X, 2, B) + w.shape[1:]), s.reshape((X, 2, B) + s.shape[1:]), h]
        shapes = [sds((Q,) + w.shape[1:], w.dtype), sds((Q,) + s.shape[1:], s.dtype), sds((2,) + h.shape[1:], f32)]
        scratch = Scatter.scratch(U, B, True, h.shape[1], h.shape[2], h.dtype)
        if o is not None:
            args.append(o)
            shapes.append(sds(o.shape[1:], f32))
            scratch += Scatter.scratch(U, B, False, o.shape[2], o.shape[3], o.dtype)
        for m in (w, s):
            scratch += PairExchange.scratch(U, B, m.shape[1], m.shape[2], m.dtype)
        return pl.pallas_call(
            functools.partial(finish_kernel, U, B, o is not None),
            out_shape=shapes,
            in_specs=any_specs(len(args)),
            out_specs=any_specs(len(args)),
            scratch_shapes=scratch + [pltpu.SemaphoreType.DMA((3,))],
            compiler_params=pltpu.CompilerParams(
                collective_id=cid, has_side_effects=True, vmem_limit_bytes=60 * 2**20),
        )(*args)

    if parts == 1:
        return call(weights, small, hidden, out)
    w, s, h = call(weights, small, hidden[..., :D], None)
    rest = [scatter_blocks(hidden[..., n * D:(n + 1) * D], U, B, True, cid + 1) for n in range(1, parts)]
    return w, s, jnp.concatenate([h] + rest, axis=-1), scatter_by_permutes(out, U, B)


def scatter_by_permutes(v, U, B):
    X, Y, Z = U // 2, 2, B // 2
    f32 = jnp.float32
    u, b = lax.axis_index("ulysses"), lax.axis_index("blk")
    c, x, y, z = lax.rem(u, 2), lax.div(u, 2), lax.rem(b, Y), lax.div(b, Y)
    where = {"c": c, "x": x, "y": y, "z": z}
    size = {"c": 2, "x": X, "y": Y, "z": Z}

    def pairs(axis, by):
        out = []
        for f in range(U * B):
            at = {"x": f // B // 2, "c": f // B % 2, "z": f % B // Y, "y": f % Y}
            at[axis] = (at[axis] + by) % size[axis]
            out.append((f, (at["x"] * 2 + at["c"]) * B + at["z"] * Y + at["y"]))
        return out

    def fold(m, axis, dim):
        n = size[axis]
        total = lax.dynamic_index_in_dim(m, where[axis], dim, keepdims=False).astype(f32)
        for by in range(1, n):
            part = lax.dynamic_index_in_dim(m, lax.rem(where[axis] + by, n), dim, keepdims=False)
            total = total + lax.ppermute(part, ("ulysses", "blk"), pairs(axis, by)).astype(f32)
        return total

    rows, D = v.shape[-2:]
    m = fold(v.reshape(X, 2, Z, Y, 2, rows, D), "c", 1).astype(v.dtype)
    first = fold(m[:, :, :, 0], "x", 0).astype(v.dtype)
    first = fold(first, "y", 1).astype(v.dtype)
    second = fold(m[:, :, :, 1], "y", 2).astype(v.dtype)
    second = fold(second, "x", 0).astype(v.dtype)
    return fold(jnp.stack([first, second], axis=1), "z", 0)


def rms_norm(values, gains):
    return values * lax.rsqrt(jnp.mean(values * values, axis=-1, keepdims=True) + EPSILON) * gains


def dot(a, b, ca, cb):
    return lax.dot_general(a, b, (((ca,), (cb,)), ((), ())), preferred_element_type=jnp.float32)


def attend_kernel(scale, q_ref, k_ref, vt_ref, o_ref, lse_ref):
    s = dot(k_ref[...], q_ref[...], 1, 1) * scale
    top = jnp.max(s, axis=0, keepdims=True)
    e = jnp.exp(s - top)
    total = jnp.sum(e, axis=0, keepdims=True)
    o = dot(vt_ref[...], e.astype(jnp.bfloat16), 1, 0) / total
    o_ref[...] = o.T.astype(o_ref.dtype)
    lse_ref[...] = top + jnp.log(total)


def attend(q, k, vt):
    n = q.shape[0]
    bq = 256 if n <= 2048 else 128
    return pl.pallas_call(
        functools.partial(attend_kernel, 1.0 / math.sqrt(HD)),
        grid=(n // bq,),
        in_specs=[
            pl.BlockSpec((bq, HD), lambda i: (i, 0)),
            pl.BlockSpec((n, HD), lambda i: (0, 0)),
            pl.BlockSpec((HD, n), lambda i: (0, 0)),
        ],
        out_specs=[pl.BlockSpec((bq, HD), lambda i: (i, 0)), pl.BlockSpec((1, bq), lambda i: (0, i))],
        out_shape=[jax.ShapeDtypeStruct((n, HD), jnp.bfloat16), jax.ShapeDtypeStruct((1, n), jnp.float32)],
        compiler_params=pltpu.CompilerParams(vmem_limit_bytes=58 * 2**20),
    )(q, k, vt)


def attend_back_kernel(scale, q_ref, do_ref, lse_ref, k_ref, kt_ref, v_ref, dq_ref, dk_ref, dv_ref):
    @pl.when(pl.program_id(0) == 0)
    def _():
        dk_ref[...] = jnp.zeros_like(dk_ref)
        dv_ref[...] = jnp.zeros_like(dv_ref)

    p = jnp.exp(dot(k_ref[...], q_ref[...], 1, 1) * scale - lse_ref[...])
    dp = dot(v_ref[...], do_ref[...], 1, 1)
    delta = jnp.sum(p * dp, axis=0, keepdims=True)
    ds = (p * (dp - delta)).astype(jnp.bfloat16)
    dv_ref[...] += dot(p.astype(jnp.bfloat16), do_ref[...], 1, 0)
    dk_ref[...] += dot(ds, q_ref[...], 1, 0) * scale
    dq_ref[...] = (dot(kt_ref[...], ds, 1, 0) * scale).T


def attend_back(q, do, lse, k, kt, v):
    n = q.shape[0]
    bq = 256 if n <= 2048 else 128
    row = lambda i: (i, 0)
    whole = lambda i: (0, 0)
    f32 = jax.ShapeDtypeStruct((n, HD), jnp.float32)
    return pl.pallas_call(
        functools.partial(attend_back_kernel, 1.0 / math.sqrt(HD)),
        grid=(n // bq,),
        in_specs=[
            pl.BlockSpec((bq, HD), row),
            pl.BlockSpec((bq, HD), row),
            pl.BlockSpec((1, bq), lambda i: (0, i)),
            pl.BlockSpec((n, HD), whole),
            pl.BlockSpec((HD, n), whole),
            pl.BlockSpec((n, HD), whole),
        ],
        out_specs=[pl.BlockSpec((bq, HD), row), pl.BlockSpec((n, HD), whole), pl.BlockSpec((n, HD), whole)],
        out_shape=[f32, f32, f32],
        compiler_params=pltpu.CompilerParams(vmem_limit_bytes=58 * 2**20),
    )(q, do, lse, k, kt, v)


def turn(v, cosine, sine):
    return v * cosine + pltpu.roll(v, HD // 2, 1) * sine


def project_kernel(tok_ref, gain_ref, w_ref, qk_ref, cos_ref, sin_ref,
                   q_ref, k_ref, v_ref, kt_ref, vt_ref, rq_ref, rk_ref):
    bf16 = jnp.bfloat16
    raw = dot(rms_norm(tok_ref[...].astype(jnp.float32), gain_ref[...]).astype(bf16), w_ref[...], 1, 0)
    rq, rk, v = raw[:, :HD], raw[:, HD:2 * HD], raw[:, 2 * HD:].astype(bf16)
    rq_ref[...] = rq
    rk_ref[...] = rk
    q_ref[...] = turn(rms_norm(rq, qk_ref[0:1]), cos_ref[...], sin_ref[...]).astype(bf16)
    k = turn(rms_norm(rk, qk_ref[1:2]), cos_ref[...], sin_ref[...])
    k_ref[...] = k.astype(bf16)
    kt_ref[...] = k.T.astype(bf16)
    v_ref[...] = v
    vt_ref[...] = raw[:, 2 * HD:].T.astype(bf16)


def project(tok, gain, w, qk, cosine, sine):
    n, D = tok.shape
    bm = 256
    row, whole = (lambda i: (i, 0)), (lambda i: (0, 0))
    head, across = pl.BlockSpec((bm, HD), row), pl.BlockSpec((HD, bm), lambda i: (0, i))
    sds = jax.ShapeDtypeStruct
    f32, bf16 = jnp.float32, jnp.bfloat16
    return pl.pallas_call(
        project_kernel,
        grid=(n // bm,),
        in_specs=[
            pl.BlockSpec((bm, D), row), pl.BlockSpec((1, D), whole), pl.BlockSpec((D, 3 * HD), whole),
            pl.BlockSpec((2, HD), whole), head, head,
        ],
        out_specs=[head, head, head, across, across, head, head],
        out_shape=[sds((n, HD), bf16)] * 3 + [sds((HD, n), bf16)] * 2 + [sds((n, HD), f32)] * 2,
        compiler_params=pltpu.CompilerParams(vmem_limit_bytes=58 * 2**20),
    )(tok, gain, w, qk, cosine, sine)


def head_back_kernel(dq_ref, dk_ref, dv_ref, rq_ref, rk_ref, cos_ref, sin_ref, qk_ref, tok_ref, gain_ref, w_ref,
                     part_ref, dw_ref, dg_ref, da_ref):
    f32, bf16 = jnp.float32, jnp.bfloat16

    @pl.when(pl.program_id(0) == 0)
    def _():
        dw_ref[...] = jnp.zeros_like(dw_ref)
        dg_ref[...] = jnp.zeros_like(dg_ref)
        da_ref[...] = jnp.zeros_like(da_ref)

    grads = []
    for n, (g_ref, raw_ref) in enumerate(((dq_ref, rq_ref), (dk_ref, rk_ref))):
        w = turn(g_ref[...].astype(bf16).astype(f32), cos_ref[...], -sin_ref[...])
        u = raw_ref[...]
        r = lax.rsqrt(jnp.mean(u * u, axis=-1, keepdims=True) + EPSILON)
        norm = u * r
        dg_ref[n:n + 1, :] += jnp.sum(w * norm, axis=0, keepdims=True)
        m = w * qk_ref[n:n + 1]
        grads.append((r * (m - norm * jnp.mean(m * norm, axis=-1, keepdims=True))).astype(bf16))
    grads.append(dv_ref[...].astype(bf16))
    grad = jnp.concatenate(grads, axis=1)
    tok = tok_ref[...].astype(f32)
    norm = tok * lax.rsqrt(jnp.mean(tok * tok, axis=-1, keepdims=True) + EPSILON)
    hidden = (norm * gain_ref[...]).astype(bf16)
    D = tok.shape[1]
    cut = min(D, 512)
    for n in range(0, D, cut):
        part = dot(grad, w_ref[n:n + cut, :], 1, 1)
        part_ref[:, n:n + cut] = part.astype(bf16)
        da_ref[0:1, n:n + cut] += jnp.sum(part * norm[:, n:n + cut], axis=0, keepdims=True)
        dw_ref[n:n + cut, :] += dot(hidden[:, n:n + cut], grad, 0, 0)


def head_back(dq, dk, dv, rq, rk, cosine, sine, qk, tok, gain, w):
    n, D = tok.shape
    bm = 512
    row, whole = (lambda i: (i, 0)), (lambda i: (0, 0))
    head = pl.BlockSpec((bm, HD), row)
    sds = jax.ShapeDtypeStruct
    return pl.pallas_call(
        head_back_kernel,
        grid=(n // bm,),
        in_specs=[head] * 7 + [
            pl.BlockSpec((2, HD), whole), pl.BlockSpec((bm, D), row), pl.BlockSpec((1, D), whole),
            pl.BlockSpec((D, 3 * HD), whole)],
        out_specs=[
            pl.BlockSpec((bm, D), row), pl.BlockSpec((D, 3 * HD), whole), pl.BlockSpec((8, HD), whole),
            pl.BlockSpec((8, D), whole)],
        out_shape=[sds((n, D), jnp.bfloat16), sds((D, 3 * HD), jnp.float32), sds((8, HD), jnp.float32),
                   sds((8, D), jnp.float32)],
        compiler_params=pltpu.CompilerParams(vmem_limit_bytes=58 * 2**20),
    )(dq, dk, dv, rq, rk, cosine, sine, qk, tok, gain, w)


def dispatch_kernel(val_ref, gate_ref, norm_ref, cot_ref, x_ref, pg_ref, hot_ref, rg_ref, rg_s):
    f32, bf16 = jnp.float32, jnp.bfloat16
    experts, KB = val_ref.shape[1:]
    RB, D = x_ref.shape[1:]
    at = lax.broadcasted_iota(jnp.int32, (RB, KB), 0)
    for e in range(experts):
        hit = at == val_ref[0, e:e + 1, :]
        hot_ref[0, e * RB:(e + 1) * RB, :] = jnp.where(hit, 1.0, 0.0).astype(bf16)
        weight = jnp.sum(jnp.where(hit, gate_ref[0, e:e + 1, :], 0.0), axis=1, keepdims=True)
        rg_s[e * RB:(e + 1) * RB, :] = weight
        rg_ref[e] = jnp.broadcast_to(weight, (RB, rg_ref.shape[2]))
    cut = min(D, 512)
    hot = hot_ref[0]
    norm = norm_ref[...].reshape(KB, D)
    cot = cot_ref[...].reshape(KB, D)
    for n in range(0, D, cut):
        x = dot(hot, norm[:, n:n + cut], 1, 0).astype(bf16)
        x_ref[:, :, n:n + cut] = x.reshape(experts, RB, cut)
        g = (dot(hot, cot[:, n:n + cut], 1, 0) * rg_s[...]).astype(bf16)
        pg_ref[:, :, n:n + cut] = g.reshape(experts, RB, cut)


def group_spec(shape, Z):
    X, two, _, Y, T, D = shape
    return pl.BlockSpec((1, two, 1, Y, T, D), lambda g: (g // Z, 0, g % Z, 0, 0, 0))


def dispatch(val, gate, normed, cot, RB):
    G, experts, KB = val.shape
    D, Z = normed.shape[-1], normed.shape[2]
    one = pl.BlockSpec((1, experts, KB), lambda g: (g, 0, 0))
    out = pl.BlockSpec((experts, RB, D), lambda g: (0, g, 0))
    sds = jax.ShapeDtypeStruct
    return pl.pallas_call(
        dispatch_kernel,
        grid=(G,),
        in_specs=[one, one, group_spec(normed.shape, Z), group_spec(cot.shape, Z)],
        out_specs=[out, out, pl.BlockSpec((1, experts * RB, KB), lambda g: (g, 0, 0)),
                   pl.BlockSpec((experts, RB, 128), lambda g: (0, g, 0))],
        out_shape=[sds((experts, G * RB, D), jnp.bfloat16)] * 2 + [
            sds((G, experts * RB, KB), jnp.bfloat16), sds((experts, G * RB, 128), jnp.float32)],
        scratch_shapes=[pltpu.VMEM((experts * RB, 1), jnp.float32)],
        compiler_params=pltpu.CompilerParams(vmem_limit_bytes=58 * 2**20),
    )(val, gate, normed, cot)


def expert_kernel(x_ref, pg_ref, rg_ref, wg_ref, wu_ref, wd_ref, y_ref, dx_ref, dwg_ref, dwu_ref, dwd_ref):
    bf16 = jnp.bfloat16
    x, pg = x_ref[0], pg_ref[0]
    D = x.shape[1]
    gate, up = dot(x, wg_ref[0], 1, 0), dot(x, wu_ref[0], 1, 0)
    sigma = jax.nn.sigmoid(gate)
    silu = gate * sigma
    inner = (silu * up).astype(bf16)
    back = dot(pg, wd_ref[0], 1, 1)
    dgate = (back * up * sigma * (1.0 + gate * (1.0 - sigma))).astype(bf16)
    dup = (back * silu).astype(bf16)
    cut = min(D, 512)
    weight = rg_ref[0, :, 0:1]
    first = pl.program_id(1) == 0

    def gather_in(ref, ix, value):
        if pl.num_programs(1) == 1:
            ref[ix] = value
        else:
            ref[ix] = value + jnp.where(first, 0.0, ref[ix])

    for n in range(0, D, cut):
        c = slice(n, n + cut)
        y_ref[0, :, c] = (dot(inner, wd_ref[0, :, c], 1, 0) * weight).astype(bf16)
        dx_ref[0, :, c] = (dot(dgate, wg_ref[0, c, :], 1, 1) + dot(dup, wu_ref[0, c, :], 1, 1)).astype(bf16)
        gather_in(dwg_ref, (0, c, slice(None)), dot(x_ref[0, :, c], dgate, 0, 0))
        gather_in(dwu_ref, (0, c, slice(None)), dot(x_ref[0, :, c], dup, 0, 0))
        gather_in(dwd_ref, (0, slice(None), c), dot(inner, pg_ref[0, :, c], 0, 0))


def expert_layer(x, pg, rg, wg, wu, wd):
    rows = x.shape[1]
    step = 640 if rows % 640 == 0 else rows
    some = lambda a: pl.BlockSpec((1, step) + a.shape[2:], lambda e, i: (e, i, 0))
    whole = lambda a: pl.BlockSpec((1,) + a.shape[1:], lambda e, i: (e, 0, 0))
    sds = jax.ShapeDtypeStruct
    return pl.pallas_call(
        expert_kernel,
        grid=(x.shape[0], rows // step),
        in_specs=[some(a) for a in (x, pg, rg)] + [whole(a) for a in (wg, wu, wd)],
        out_specs=[some(a) for a in (x, x)] + [whole(a) for a in (wg, wu, wd)],
        out_shape=[sds(x.shape, x.dtype)] * 2 + [sds(a.shape, jnp.float32) for a in (wg, wu, wd)],
        compiler_params=pltpu.CompilerParams(vmem_limit_bytes=60 * 2**20),
    )(x, pg, rg, wg, wu, wd)


def combine_kernel(hot_ref, y_ref, dx_ref, py_ref, pdx_ref):
    hot = hot_ref[0]
    rows, KB = hot.shape
    D = y_ref.shape[2]
    cut = min(D, 512)
    for src, dst in ((y_ref, py_ref), (dx_ref, pdx_ref)):
        for n in range(0, D, cut):
            t = dot(hot, src[:, :, n:n + cut].reshape(rows, cut), 0, 0)
            dst[:, :, :, :, :, n:n + cut] = t.astype(dst.dtype).reshape(dst.shape[:-1] + (cut,))


def combine(hot, y, dx, shape):
    G, rows, KB = hot.shape
    experts, D = y.shape[0], y.shape[2]
    RB = rows // experts
    part = pl.BlockSpec((experts, RB, D), lambda g: (0, g, 0))
    out = group_spec(shape, shape[2])
    return pl.pallas_call(
        combine_kernel,
        grid=(G,),
        in_specs=[pl.BlockSpec((1, rows, KB), lambda g: (g, 0, 0)), part, part],
        out_specs=[out, out],
        out_shape=[jax.ShapeDtypeStruct(shape, jnp.bfloat16)] * 2,
        compiler_params=pltpu.CompilerParams(vmem_limit_bytes=58 * 2**20),
    )(hot, y, dx)


def body(tokens, w_query, w_key, w_value, w_out, attn_gain, ffn_gain, qk_gain,
         expert_gate, expert_up, expert_down, routes, gates, order, cotangent):
    f32, bf16 = jnp.float32, jnp.bfloat16
    positions, seqs, D = tokens.shape
    U, B = lax.axis_size("ulysses"), lax.axis_size("blk")
    F = U * B
    u, b = lax.axis_index("ulysses"), lax.axis_index("blk")
    H = w_query.shape[1] // HD
    W = w_query.shape[0]
    L = F * positions
    T = seqs * positions
    top_count = routes.shape[-1]
    local_experts = expert_gate.shape[0]
    E = local_experts * B
    chips = F // 2
    R = chips // H
    first_copy = lax.rem((u // 2) * B + b, R) == 0

    tok = tokens.transpose(1, 0, 2)
    cot = cotangent.transpose(1, 0, 2)
    rows_f = tok.reshape(T, D).astype(f32)

    expert_of = routes.transpose(1, 0, 2).reshape(-1)
    prio = order.reshape(positions, seqs, top_count).transpose(1, 0, 2).reshape(-1)
    same = expert_of[:, None] == expert_of[None, :]
    ranks = jnp.sum((same & (prio[None, :] < prio[:, None])).astype(jnp.int32), axis=1)
    slot = jnp.where(ranks < CAP, expert_of * CAP + ranks, -1).astype(f32)
    pairs = slot.shape[0]

    nq = qk_gain.shape[1]
    small = jnp.concatenate(
        [slot, gates.transpose(1, 0, 2).reshape(-1)]
        + [g.astype(f32) for g in (attn_gain, ffn_gain, qk_gain[0], qk_gain[1])])
    small = jnp.pad(small, (0, -small.shape[0] % 1024)).reshape(-1, 128)
    heads_w = jnp.stack([w_query, w_key, w_value]).reshape(3, W, H, HD).transpose(2, 1, 0, 3).reshape(H, W, 3 * HD)
    if R > 1:
        heads_w = heads_w[np.arange(chips) // R]
    seq_tok, table, head_w = front(tok, small, heads_w, U, B, 1)
    seq_tok, head_w = seq_tok.reshape(L, D), head_w.reshape(D, 3 * HD)
    out_w = lax.all_gather(w_out, AXES, axis=0, tiled=True)
    cot_all = lax.all_gather(cot, AXES, axis=0)
    table = table.reshape(F, -1)
    cut = 2 * pairs
    attn_g = table[:, cut:cut + W].reshape(1, D)
    ffn_g = table[:, cut + W:cut + 2 * W].reshape(1, D)
    cut = cut + 2 * W
    qk_g = jnp.stack([table[:, cut:cut + nq].reshape(-1), table[:, cut + nq:cut + 2 * nq].reshape(-1)])

    groups = (U // 2, 2, B // 2, 2)
    GB = 4
    G, KB = F // GB, GB * T
    RB = -(-GB * CAP // 16) * 16
    slot_all = table[:, :pairs].astype(jnp.int32).reshape(F, T, top_count)
    gate_all = table[:, pairs:2 * pairs].reshape(F, T, top_count)
    place = ((np.arange(F) // B % 2) * 2 + np.arange(F) % 2).astype(np.int32)
    base = (b * local_experts + jnp.arange(local_experts, dtype=jnp.int32)) * CAP
    off = slot_all[:, :, :, None] - base
    mine = (off >= 0) & (off < CAP)
    val = jnp.sum(jnp.where(mine, off + 1, 0), axis=2)
    val = jnp.where(val > 0, val - 1 + jnp.asarray(place)[:, None, None] * CAP, -1)
    gate_of = jnp.sum(jnp.where(mine, gate_all[:, :, :, None], 0.0), axis=2)

    def by_group(m):
        return m.reshape(groups + (T, local_experts)).transpose(0, 2, 5, 1, 3, 4).reshape(G, local_experts, KB)

    val, gate_of = by_group(val), by_group(gate_of)

    half = HD // 2
    inverse = ROPE_BASE ** (-2.0 * jnp.arange(half).astype(f32) / HD)
    angles = jnp.arange(L).astype(f32)[:, None] * inverse[None, :]
    cosine = jnp.concatenate([jnp.cos(angles)] * 2, axis=1)
    sine = jnp.concatenate([-jnp.sin(angles), jnp.sin(angles)], axis=1)
    q, k, v, kt, vt, raw_q, raw_k = project(seq_tok, attn_g, head_w, qk_g, cosine, sine)
    att, lse = attend(q, k, vt)
    att_rows = exchange(att.reshape(F, positions, HD), U, B, 6)

    def from_heads(m):
        m = m.reshape(U // 2, 2, B, positions, HD).transpose(1, 3, 0, 2, 4)
        return m.reshape(2, positions, H, R, HD)[:, :, :, 0].reshape(T, H * HD)

    attended = from_heads(att_rows)
    residual = rows_f + jnp.dot(attended, out_w, preferred_element_type=f32)
    normed_full, ffn_back = jax.vjp(rms_norm, residual, ffn_g)
    normed = normed_full.astype(bf16).reshape(2, positions, D)

    normed_all = gather_blocks(normed, U, B, False, 2)
    shape = groups + (T, D)
    x, pair_grad, hot, row_gate = dispatch(val, gate_of, normed_all.reshape(shape), cot_all.reshape(shape), RB)
    y, dx, gate_grad, up_grad, down_grad = expert_layer(x, pair_grad, row_gate, expert_gate, expert_up, expert_down)
    mixed_part, normed_part = combine(hot, y, dx, shape)
    blocks = (F, 2, positions, D)
    mixed_sum, normed_grad = scatter_pair(mixed_part.reshape(blocks), normed_part.reshape(blocks), U, B, 3)
    mixed = (residual + mixed_sum.reshape(T, D)).reshape(2, positions, D).transpose(1, 0, 2).astype(bf16)
    normed_grad = normed_grad.reshape(T, D)

    residual_norm_grad, ffn_gain_part = ffn_back(normed_grad)
    residual_grad = cot.reshape(T, D).astype(f32) + residual_norm_grad
    attn_out_grad = residual_grad.astype(bf16)
    att_grad = dot(attn_out_grad, out_w, 1, 1).astype(bf16)
    att_grad = jnp.repeat(att_grad.reshape(2, positions, H, HD).transpose(2, 0, 1, 3), R, axis=0)
    att_grad = att_grad.reshape(U // 2, B, 2, positions, HD).transpose(0, 2, 1, 3, 4).reshape(F, positions, HD)
    do = exchange(att_grad, U, B, 6).reshape(L, HD)
    out_part = dot(attended, attn_out_grad, 0, 0).astype(bf16)
    out_part = out_part.reshape(F, 2, W // 2, D)
    dq, dk, dv = attend_back(q, do, lse, k, kt, v)
    if R > 1:
        dq, dk, dv = (jnp.where(first_copy, m, 0.0) for m in (dq, dk, dv))
    hidden_part, weight_part, qk_part, attn_gain_part = head_back(
        dq, dk, dv, raw_q, raw_k, cosine, sine, qk_g, seq_tok, attn_g, head_w)
    weight_part = weight_part.astype(bf16).reshape(F, W, 3 * HD)
    small = jnp.concatenate(
        [attn_gain_part[0].reshape(F, W), ffn_gain_part.reshape(F, W),
         qk_part[0].reshape(F, nq), qk_part[1].reshape(F, nq)], axis=1)
    small = jnp.pad(small, ((0, 0), (0, -small.shape[1] % 1024))).reshape(F, -1, 128)
    weight_grad, small, hidden_grad, out_grad = finish(
        weight_part, small, hidden_part.reshape(F, positions, D), out_part, U, B, 4)
    small = jnp.sum(small, axis=0).reshape(-1)
    weight_grad = weight_grad.reshape(H, R, W, 3 * HD).astype(f32).sum(axis=1)
    weight_grad = weight_grad.transpose(1, 0, 2).reshape(W, H, 3, HD)
    query_grad, key_grad, value_grad = (weight_grad[:, :, n].reshape(W, H * HD) for n in range(3))
    hidden_grad, out_grad = hidden_grad.reshape(T, D), out_grad.reshape(W, D)
    inv = lax.rsqrt(jnp.mean(rows_f * rows_f, axis=-1, keepdims=True) + EPSILON)
    norm = rows_f * inv
    m = hidden_grad * attn_g
    token_grad = inv * (m - norm * jnp.mean(m * norm, axis=-1, keepdims=True))
    input_grad = (residual_grad + token_grad).reshape(2, positions, D).transpose(1, 0, 2)
    return (
        mixed, input_grad, query_grad, key_grad, value_grad, out_grad,
        small[:W], small[W:2 * W], small[2 * W:2 * W + 2 * nq].reshape(2, nq),
        gate_grad, up_grad, down_grad,
    )


def solution(mesh):
    rows = P(AXES, None, None)
    flat = P(AXES, None)
    by_expert = (P("blk", None, "ulysses"), P("blk", None, "ulysses"), P("blk", "ulysses", None))
    in_specs = (rows, flat, flat, flat, flat, P(AXES), P(AXES), P(None, AXES)) + by_expert + (rows, rows, flat, rows)
    out_specs = (rows, rows, flat, flat, flat, flat, P(AXES), P(AXES), P(None, AXES)) + by_expert
    return jax.shard_map(body, mesh=mesh, in_specs=in_specs, out_specs=out_specs, check_vma=False)
```

```python
import functools
import math

import jax
import jax.numpy as jnp
import numpy as np
from jax import lax
from jax.experimental import pallas as pl
from jax.experimental.pallas import tpu as pltpu
from jax.sharding import PartitionSpec as P

HD = 128
CAP = 18
EPSILON = 1e-06
ROPE_BASE = 10000.0
AXES = ("ulysses", "blk")
MESH = pl.DeviceIdType.MESH


class Place:
    def __init__(self, U, B):
        self.U, self.B = U, B
        self.X, self.Y = U // 2, 2
        self.Z = B // self.Y
        self.Q, self.F = self.X * B, U * B
        u, b = lax.axis_index("ulysses"), lax.axis_index("blk")
        self.c, self.x = lax.rem(u, 2), lax.div(u, 2)
        self.y, self.z = lax.rem(b, self.Y), lax.div(b, self.Y)
        self.r = self.c * B + b
        self.me = u * B + b
        self.core_peer = self.dev(self.x, self.y, self.z, 1 - self.c)
        self.x_peer = self.dev(1 - self.x, self.y, self.z, self.c)

    def dev(self, x, y, z, c):
        return (x * 2 + c, z * self.Y + y)

    def block(self, x, y, z, c):
        return (x * 2 + c) * self.B + z * self.Y + y

    def chip(self, x, y, z):
        return x * self.B + z * self.Y + y

    def at(self, r, x):
        return x * 2 * self.B + r

    def plane_dev(self, r):
        return (self.x * 2 + lax.div(r, self.B), lax.rem(r, self.B))

    def flat_dev(self, f):
        return (lax.div(f, self.B), lax.rem(f, self.B))

    def others(self, axis):
        n = {"x": self.X, "y": self.Y, "z": self.Z}[axis]
        i = {"x": self.x, "y": self.y, "z": self.z}[axis]
        return [lax.rem(i + o, n) for o in range(1, n)]

    def barrier(self, reach):
        sem = pltpu.get_barrier_semaphore()

        def greet(d):
            pl.semaphore_signal(sem, inc=1, device_id=d, device_id_type=MESH)

        if reach == "every":
            @pl.loop(1, self.F)
            def _(o):
                greet(self.flat_dev(lax.rem(self.me + o, self.F)))

            pl.semaphore_wait(sem, self.F - 1)
            return
        if reach == "plane":
            greet(self.x_peer)

            @pl.loop(1, 2 * self.B)
            def _(o):
                greet(self.plane_dev(lax.rem(self.r + o, 2 * self.B)))

            pl.semaphore_wait(sem, 2 * self.B)
            return
        greet(self.core_peer)
        for k in self.others("x"):
            greet(self.dev(k, self.y, self.z, self.c))
        for k in self.others("y"):
            greet(self.dev(self.x, k, self.z, self.c))
        count = self.X + self.Y - 1
        if reach == "chain":
            below, above = self.z > 0, self.z < self.Z - 1

            @pl.when(below)
            def _():
                greet(self.dev(self.x, self.y, self.z - 1, self.c))

            @pl.when(above)
            def _():
                greet(self.dev(self.x, self.y, self.z + 1, self.c))

            count = count + jnp.where(below, 1, 0) + jnp.where(above, 1, 0)
        else:
            for k in self.others("z"):
                greet(self.dev(self.x, self.y, k, self.c))
            count += self.Z - 1
        pl.semaphore_wait(sem, count)


def remote(src, dst, send, recv, dev):
    return pltpu.make_async_remote_copy(
        src_ref=src, dst_ref=dst, send_sem=send, recv_sem=recv, device_id=dev, device_id_type=MESH)


class Gather:
    def __init__(self, p, src, out, send_sem, recv_sem, local_sem):
        self.p, self.src, self.out = p, src, out
        self.send_sem, self.recv_sem, self.local_sem = send_sem, recv_sem, local_sem
        self.steps = p.Z + 2
        self.started = []
        self.always = p.z >= 0

    @staticmethod
    def semaphores(U, B):
        dma = pltpu.SemaphoreType.DMA
        return [dma((4 + U // 2, 2, U * B)), dma((2, U * B)), dma((1,))]

    def where(self, half, x, y, z):
        f = self.p.block(x, y, z, self.p.c)
        return self.out.at[f, half], (half, f)

    def send(self, cond, src_ref, dst_ref, ix, way, dev):
        cp = remote(src_ref, dst_ref, self.send_sem.at[(way,) + ix], self.recv_sem.at[ix], dev)

        @pl.when(cond)
        def _():
            cp.start()

        self.started.append((cond, cp))

    def wait(self, ref, ix):
        remote(ref, ref, self.send_sem.at[(0,) + ix], self.recv_sem.at[ix], self.p.core_peer).wait_recv()

    def along(self, cond, half, x, y, z, axes):
        p = self.p
        ref, ix = self.where(half, x, y, z)
        for ax in axes:
            if ax == "core":
                self.send(cond, ref, ref, ix, 0, p.core_peer)
            elif ax == "up":
                self.send(cond & (p.z < p.Z - 1), ref, ref, ix, 1, p.dev(p.x, p.y, p.z + 1, p.c))
            elif ax == "down":
                self.send(cond & (p.z > 0), ref, ref, ix, 2, p.dev(p.x, p.y, p.z - 1, p.c))
            elif ax == "y":
                for i, k in enumerate(p.others("y")):
                    self.send(cond, ref, ref, ix, 3 + i, p.dev(p.x, k, p.z, p.c))
            else:
                for i, k in enumerate(p.others("x")):
                    self.send(cond, ref, ref, ix, 2 + p.Y + i, p.dev(k, p.y, p.z, p.c))

    def zs(self, step):
        p = self.p
        if step == 0:
            return [(self.always, p.z, ())]
        return [(p.z - step >= 0, p.z - step, ("up",)), (p.z + step < p.Z, p.z + step, ("down",))]

    def arrive(self, cond, half, x, y, z, axes):
        ref, ix = self.where(half, x, y, z)

        @pl.when(cond)
        def _():
            self.wait(ref, ix)

        self.along(cond, half, x, y, z, axes)

    def step(self, n):
        p = self.p
        if n == 0:
            cp = pltpu.make_async_copy(self.src, self.out.at[p.me], self.local_sem.at[0])
            cp.start()
            cp.wait()
            for half in (0, 1):
                self.along(self.always, half, p.x, p.y, p.z, ("up", "down", "y", "x"))
            for half in (0, 1):
                self.along(self.always, half, p.x, p.y, p.z, ("core",))
            return
        if n < p.Z:
            for half in (0, 1):
                for cond, k, on in self.zs(n):
                    self.arrive(cond, half, p.x, p.y, k, on + ("y", "x", "core"))
        if n <= p.Z:
            for cond, k, _ in self.zs(n - 1):
                for j in p.others("y"):
                    self.arrive(cond, 0, p.x, j, k, ("x", "core"))
                for j in p.others("x"):
                    self.arrive(cond, 1, j, p.y, k, ("y", "core"))
        if n >= 2:
            for cond, k, _ in self.zs(n - 2):
                for j in p.others("x"):
                    self.arrive(cond, 0, j, p.y, k, ("core",))
                for i in p.others("y"):
                    self.arrive(cond, 1, p.x, i, k, ("core",))
                for j in p.others("x"):
                    for i in p.others("y"):
                        self.arrive(cond, 0, j, i, k, ("core",))
                        self.arrive(cond, 1, j, i, k, ("core",))

    def end(self):
        p = self.p
        for k in range(p.Z):
            for j in range(p.X):
                for i in range(p.Y):
                    f = p.block(j, i, k, 1 - p.c)
                    for half in (0, 1):
                        self.wait(self.out.at[f, half], (half, f))
        for cond, cp in self.started:
            @pl.when(cond)
            def _(cp=cp):
                cp.wait_send()


class PlaneGather(Gather):
    def __init__(self, *a):
        super().__init__(*a)
        self.steps = self.p.Z + 1

    @staticmethod
    def semaphores(U, B):
        dma = pltpu.SemaphoreType.DMA
        return [dma((5, 1, U * B)), dma((1, U * B)), dma((1,))]

    def where(self, half, x, y, z):
        f = self.p.block(half, y, z, self.p.c)
        return self.out.at[f], (0, f)

    def step(self, n):
        p = self.p
        if n == 0:
            cp = pltpu.make_async_copy(self.src.at[p.x], self.out.at[p.me], self.local_sem.at[0])
            cp.start()
            self.send(self.always, self.src.at[1 - p.x], self.out.at[p.me], (0, p.me), 4, p.x_peer)
            cp.wait()
            self.along(self.always, p.x, p.x, p.y, p.z, ("up", "down", "y", "core"))
            self.arrive(self.always, 1 - p.x, p.x, p.y, p.z, ("up", "down", "y", "core"))
            return
        if n < p.Z:
            for half in (0, 1):
                for cond, k, on in self.zs(n):
                    self.arrive(cond, half, p.x, p.y, k, on + ("y", "core"))
        for half in (0, 1):
            for cond, k, _ in self.zs(n - 1):
                for i in p.others("y"):
                    self.arrive(cond, half, p.x, i, k, ("core",))

    def end(self):
        p = self.p
        for k in range(p.Z):
            for i in range(p.Y):
                for half in (0, 1):
                    f = p.block(half, i, k, 1 - p.c)
                    self.wait(self.out.at[f], (0, f))
        for cond, cp in self.started:
            @pl.when(cond)
            def _(cp=cp):
                cp.wait_send()


class Spread:
    def __init__(self, p, same, src, out, send_sem, recv_sem):
        self.p, self.same, self.src, self.out = p, same, src, out
        self.send_sem, self.recv_sem = send_sem, recv_sem

    @staticmethod
    def semaphores(U, B):
        dma = pltpu.SemaphoreType.DMA
        return [dma((2, 2 * B)), dma((U * B,))]

    def part(self, r):
        return self.src if self.same else self.src.at[r]

    def out_to(self, o):
        p = self.p
        r = lax.rem(p.r + o, 2 * p.B)
        return remote(self.part(r), self.out.at[p.me], self.send_sem.at[0, r], self.recv_sem.at[p.me], p.plane_dev(r))

    def across(self, r):
        f = self.p.at(r, self.p.x)
        return remote(self.out.at[f], self.out.at[f], self.send_sem.at[1, r], self.recv_sem.at[f], self.p.x_peer)

    def arrive(self, f):
        remote(self.out.at[f], self.out.at[f], self.send_sem.at[0, 0], self.recv_sem.at[f], self.p.x_peer).wait_recv()

    def begin(self):
        p = self.p

        @pl.loop(1, 2 * p.B)
        def _(o):
            self.out_to(o).start()

        cp = pltpu.make_async_copy(self.part(p.r), self.out.at[p.me], self.send_sem.at[0, p.r])
        cp.start()
        cp.wait()
        self.across(p.r).start()

    def middle(self):
        p = self.p

        @pl.loop(1, 2 * p.B)
        def _(o):
            r = lax.rem(p.r + o, 2 * p.B)
            self.arrive(p.at(r, p.x))
            self.across(r).start()

    def end(self):
        p = self.p

        @pl.loop(0, 2 * p.B)
        def _(r):
            self.arrive(p.at(r, 1 - p.x))
            self.across(r).wait_send()

        @pl.loop(1, 2 * p.B)
        def _(o):
            self.out_to(o).wait_send()


def any_specs(n):
    return [pl.BlockSpec(memory_space=pl.ANY)] * n


def gather_kernel(U, B, src, out, *sems):
    p = Place(U, B)
    p.barrier("chain")
    g = Gather(p, src, out, *sems)
    for n in range(g.steps):
        g.step(n)
    g.end()


def gather_blocks(v, U, B, cid):
    return pl.pallas_call(
        functools.partial(gather_kernel, U, B),
        out_shape=jax.ShapeDtypeStruct((U * B,) + v.shape, v.dtype),
        in_specs=any_specs(1),
        out_specs=any_specs(1)[0],
        scratch_shapes=Gather.semaphores(U, B),
        compiler_params=pltpu.CompilerParams(collective_id=cid, has_side_effects=True),
    )(v)


def front_kernel(U, B, tok, small, weights, tok_out, small_out, weights_out, *sems):
    p = Place(U, B)
    p.barrier("plane")
    g = PlaneGather(p, tok, tok_out, *sems[:3])
    s = Spread(p, True, small, small_out, *sems[3:5])
    w = Spread(p, False, weights, weights_out, *sems[5:7])
    s.begin()
    g.step(0)
    w.begin()
    for n in range(1, g.steps):
        g.step(n)
        if n == 1:
            s.middle()
        if n == 2:
            w.middle()
    s.end()
    w.end()
    g.end()


def front(tok, small, weights, U, B, cid):
    F = U * B
    return pl.pallas_call(
        functools.partial(front_kernel, U, B),
        out_shape=[
            jax.ShapeDtypeStruct((F,) + tok.shape[1:], tok.dtype),
            jax.ShapeDtypeStruct((F,) + small.shape, small.dtype),
            jax.ShapeDtypeStruct((F,) + weights.shape[1:], weights.dtype),
        ],
        in_specs=any_specs(3),
        out_specs=any_specs(3),
        scratch_shapes=PlaneGather.semaphores(U, B) + Spread.semaphores(U, B) * 2,
        compiler_params=pltpu.CompilerParams(collective_id=cid, has_side_effects=True),
    )(tok, small, weights)


def exchange_kernel(U, B, src, out, send_sem, recv_sem):
    p = Place(U, B)
    p.barrier("every")

    def copy(o):
        f = lax.rem(p.me + o, p.F)
        return f, remote(src.at[f], out.at[p.me], send_sem.at[f], recv_sem.at[p.me], p.flat_dev(f))

    @pl.loop(1, p.F)
    def _(o):
        copy(o)[1].start()

    cp = pltpu.make_async_copy(src.at[p.me], out.at[p.me], recv_sem.at[p.me])
    cp.start()
    cp.wait()

    @pl.loop(1, p.F)
    def _(o):
        f, cp = copy(o)
        remote(out.at[f], out.at[f], send_sem.at[f], recv_sem.at[f], p.flat_dev(f)).wait_recv()
        cp.wait_send()


def exchange(v, U, B, cid):
    return pl.pallas_call(
        functools.partial(exchange_kernel, U, B),
        out_shape=jax.ShapeDtypeStruct(v.shape, v.dtype),
        in_specs=any_specs(1),
        out_specs=any_specs(1)[0],
        scratch_shapes=[pltpu.SemaphoreType.DMA((U * B,))] * 2,
        compiler_params=pltpu.CompilerParams(collective_id=cid, has_side_effects=True),
    )(v)


class Scatter:
    def __init__(self, p, acc, rc, rx0, rx1, ry0, ry1, rz, fin, loc, cs, cr, xs, xr, ys, yr, zs, zr):
        self.p = p
        self.acc, self.rc, self.rx, self.ry, self.rz, self.fin = acc, rc, (rx0, rx1), (ry0, ry1), rz, fin
        self.loc, self.cs, self.cr = loc, cs, cr
        self.xs, self.xr, self.ys, self.yr, self.zs, self.zr = xs, xr, ys, yr, zs, zr
        self.order = p.others("z") + [p.z]
        self.steps = p.Z + 2
        self.started = []
        self.local = True

    @staticmethod
    def scratch(U, B, rows, D, t):
        X, Y, Z, Q = U // 2, 2, B // 2, U * B // 2
        dma = pltpu.SemaphoreType.DMA
        x, y = max(X - 1, 1), Y - 1
        return [
            pltpu.VMEM((Q, 2, rows, D), t),
            pltpu.VMEM((Q, 2, rows, D), t),
            pltpu.VMEM((x, Z * Y, rows, D), t),
            pltpu.VMEM((x, Z, rows, D), t),
            pltpu.VMEM((y, Z, rows, D), t),
            pltpu.VMEM((y, Z * X, rows, D), t),
            pltpu.VMEM((2, Z, rows, D), t),
            pltpu.VMEM((2, rows, D), jnp.float32),
            dma((Q, 2)),
            dma((Q, 2)),
            dma((Q, 2)),
            dma((2, x, Z * Y)),
            dma((2, x, Z * Y)),
            dma((2, y, Z * X)),
            dma((2, y, Z * X)),
            dma((2, Z)),
            dma((2, Z)),
        ]

    SCRATCH = 17

    def start(self, *a):
        cp = remote(*a)
        cp.start()
        self.started.append(cp)

    def got(self, ref, sem):
        remote(ref, ref, sem, sem, self.p.core_peer).wait_recv()

    def load(self, src):
        p = self.p
        for k in self.order:
            for j in p.others("x") + [p.x]:
                for i in range(p.Y):
                    for h in (0, 1):
                        q = p.chip(j, i, k)
                        cp = self.across(src.at[p.block(j, i, k, 1 - p.c), h], q, h)
                        cp.start()
                        self.started.append(cp)
                        self.keep(src.at[p.block(j, i, k, p.c), h], q, h).start()

    def keep(self, src, q, h):
        return pltpu.make_async_copy(src, self.acc.at[q, h], self.loc.at[q, h])

    def across(self, src, q, h):
        return remote(src, self.rc.at[q, h], self.cs.at[q, h], self.cr.at[q, h], self.p.core_peer)

    def ready(self, h, j, i, k):
        q = self.p.chip(j, i, k)
        if self.local:
            self.keep(self.acc.at[q, h], q, h).wait()
        self.got(self.rc.at[q, h], self.cr.at[q, h])
        return [self.rc.at[q, h]]

    def send_x(self, h, q, j, s):
        p = self.p
        o = lax.rem(j - p.x + p.X, p.X) - 1
        self.start(self.acc.at[q, h], self.rx[h].at[o, s], self.xs.at[h, o, s], self.xr.at[h, o, s],
                   p.dev(j, p.y, p.z, p.c))

    def send_y(self, h, q, i, s):
        p = self.p
        o = lax.rem(i - p.y + p.Y, p.Y) - 1
        self.start(self.acc.at[q, h], self.ry[h].at[o, s], self.ys.at[h, o, s], self.yr.at[h, o, s],
                   p.dev(p.x, i, p.z, p.c))

    def from_x(self, h, s):
        out = []
        for o in range(self.p.X - 1):
            self.got(self.rx[h].at[o, s], self.xr.at[h, o, s])
            out.append(self.rx[h].at[o, s])
        return out

    def from_y(self, h, s):
        out = []
        for o in range(self.p.Y - 1):
            self.got(self.ry[h].at[o, s], self.yr.at[h, o, s])
            out.append(self.ry[h].at[o, s])
        return out

    def last(self, n, h, q, extra):
        p = self.p
        k = self.order[n]
        if n < p.Z - 1:
            add(self.acc.at[q, h], extra)
            self.start(self.acc.at[q, h], self.rz.at[h, p.z], self.zs.at[h, k], self.zr.at[h, p.z],
                       p.dev(p.x, p.y, k, p.c))
        else:
            for a in p.others("z"):
                self.got(self.rz.at[h, a], self.zr.at[h, a])
                extra.append(self.rz.at[h, a])
            add(self.acc.at[q, h], extra, self.fin.at[h])

    def first(self, n, j):
        p = self.p
        k = self.order[n]
        if j is not p.x:
            for i in range(p.Y):
                q = p.chip(j, i, k)
                add(self.acc.at[q, 0], self.ready(0, j, i, k))
                self.send_x(0, q, j, k * p.Y + i)
        for i in p.others("y"):
            q = p.chip(j, i, k)
            add(self.acc.at[q, 1], self.ready(1, j, i, k))
            self.send_y(1, q, i, k * p.X + j)

    def rest(self, n):
        p = self.p
        X, Y, Z = p.X, p.Y, p.Z
        if 1 <= n <= Z:
            k = self.order[n - 1]
            for i in p.others("y"):
                q = p.chip(p.x, i, k)
                add(self.acc.at[q, 0], self.ready(0, p.x, i, k) + self.from_x(0, k * Y + i))
                self.send_y(0, q, i, k)
            for j in p.others("x"):
                q = p.chip(j, p.y, k)
                add(self.acc.at[q, 1], self.ready(1, j, p.y, k) + self.from_y(1, k * X + j))
                self.send_x(1, q, j, k)
        if n >= 2:
            k = self.order[n - 2]
            q = p.chip(p.x, p.y, k)
            self.last(n - 2, 0, q, self.ready(0, p.x, p.y, k) + self.from_x(0, k * Y + p.y) + self.from_y(0, k))
            self.last(n - 2, 1, q, self.ready(1, p.x, p.y, k) + self.from_y(1, k * X + p.x) + self.from_x(1, k))

    def step(self, n):
        if n < self.p.Z:
            for j in self.p.others("x") + [self.p.x]:
                self.first(n, j)
        self.rest(n)

    def sent(self):
        for cp in self.started:
            cp.wait_send()


def add(dst, srcs, f32_out=None):
    step = 16

    def one(n, _):
        r = pl.ds(pl.multiple_of(n * step, step), step)
        t = dst[r, :].astype(jnp.float32)
        for s in srcs:
            t = t + s[r, :].astype(jnp.float32)
        if f32_out is None:
            dst[r, :] = t.astype(dst.dtype)
        else:
            f32_out[r, :] = t
        return 0

    lax.fori_loop(0, dst.shape[0] // step, one, 0)


class PlaneScatter(Scatter):
    def __init__(self, p, acc, rc, ry, rz, fin, loc, cs, cr, ys, yr, zs, zr):
        self.p = p
        self.acc, self.rc, self.rz, self.fin, self.ry = acc, rc, rz, fin, (ry.at[0], ry.at[1])
        self.loc, self.cs, self.cr = loc, cs, cr
        self.ys, self.yr, self.zs, self.zr = ys, yr, zs, zr
        self.order = p.others("z") + [p.z]
        self.steps = p.Z + 1
        self.started = []
        self.local = True

    @staticmethod
    def scratch(U, B, rows, D, t):
        Y, Z = 2, B // 2
        dma = pltpu.SemaphoreType.DMA
        return [
            pltpu.VMEM((B, 2, rows, D), t),
            pltpu.VMEM((B, 2, rows, D), t),
            pltpu.VMEM((2, Y - 1, Z, rows, D), t),
            pltpu.VMEM((2, Z, rows, D), t),
            pltpu.VMEM((2, rows, D), jnp.float32),
            dma((B, 2)),
            dma((B, 2)),
            dma((B, 2)),
            dma((2, Y - 1, Z)),
            dma((2, Y - 1, Z)),
            dma((2, Z)),
            dma((2, Z)),
        ]

    SCRATCH = 12

    def load(self, src):
        p = self.p
        for k in self.order:
            for i in p.others("y") + [p.y]:
                for h in (0, 1):
                    q = p.chip(0, i, k)
                    cp = self.across(src.at[p.block(h, i, k, 1 - p.c)], q, h)
                    cp.start()
                    self.started.append(cp)
                    self.keep(src.at[p.block(h, i, k, p.c)], q, h).start()

    def step(self, n):
        p = self.p
        if n < p.Z:
            k = self.order[n]
            for i in p.others("y"):
                q = p.chip(0, i, k)
                for h in (0, 1):
                    add(self.acc.at[q, h], self.ready(h, 0, i, k))
                    self.send_y(h, q, i, k)
        if n >= 1:
            k = self.order[n - 1]
            q = p.chip(0, p.y, k)
            for h in (0, 1):
                self.last(n - 1, h, q, self.ready(h, 0, p.y, k) + self.from_y(h, k))


def keep_sum(fin, out, sem):
    cp = pltpu.make_async_copy(fin, out, sem)
    cp.start()
    cp.wait()


class Combine:
    def __init__(self, s, rows_in, hot_in, cols, rows_buf, hot_buf, stage, sems):
        self.s, self.p = s, s.p
        self.rows_in, self.hot_in, self.cols = rows_in, hot_in, cols
        self.rows_buf, self.hot_buf, self.stage, self.sems = rows_buf, hot_buf, stage, sems
        self.sent = []
        s.local = False

    def loads(self, j, k):
        g = j * self.p.Z + k
        RB = self.rows_buf.shape[1]
        rows = pl.ds(pl.multiple_of(g * RB, RB), RB)
        return (
            pltpu.make_async_copy(self.rows_in.at[:, rows, self.cols], self.rows_buf, self.sems.at[0]),
            pltpu.make_async_copy(self.hot_in.at[g], self.hot_buf, self.sems.at[1]),
        )

    def fetch(self, j, k):
        for cp in self.loads(j, k):
            cp.start()

    def make(self, j, k):
        p, s = self.p, self.s
        for cp in self.loads(j, k):
            cp.wait()
        for cp in self.sent:
            cp.wait_send()
        self.sent.clear()
        experts, RB, D = self.rows_buf.shape
        KB = self.hot_buf.shape[1]
        cut = min(D, 512)

        for n in range(0, D, cut):
            t = lax.dot_general(self.hot_buf[...], self.rows_buf[:, :, n:n + cut].reshape(experts * RB, cut),
                                (((0,), (0,)), ((), ())), preferred_element_type=jnp.float32)
            self.stage[:, :, :, n:n + cut] = t.astype(self.stage.dtype).reshape(self.stage.shape[:3] + (cut,))
        kept = []
        for i in range(p.Y):
            for h in (0, 1):
                q = p.chip(j, i, k)
                cp = s.across(self.stage.at[(1 - p.c) * p.Y + i, h], q, h)
                cp.start()
                self.sent.append(cp)
                cp = s.keep(self.stage.at[p.c * p.Y + i, h], q, h)
                cp.start()
                kept.append(cp)
        for cp in kept:
            cp.wait()

    def end(self):
        for cp in self.sent:
            cp.wait_send()


def pair_kernel(U, B, cols, a, b, hot, out_a, out_b, *scratch):
    p = Place(U, B)
    p.barrier("lines")
    k = Scatter.SCRATCH
    work = [Scatter(p, *scratch[k * i:k * (i + 1)]) for i in range(2)]
    feed = [Combine(s, m, hot, cols, *scratch[2 * k:2 * k + 4]) for s, m in zip(work, (a, b))]
    feed[1].sent = feed[0].sent
    xs = p.others("x") + [p.x]
    todo = [(f, j, z) for z in work[0].order for f in feed for j in xs]
    todo[0][0].fetch(*todo[0][1:])
    at = 0
    for n in range(work[0].steps):
        for s in work:
            if n < p.Z:
                for x in xs:
                    f, j, z = todo[at]
                    f.make(j, z)
                    at += 1
                    if at < len(todo):
                        todo[at][0].fetch(*todo[at][1:])
                    s.first(n, x)
            s.rest(n)
    feed[0].end()
    for s, out in zip(work, (out_a, out_b)):
        keep_sum(s.fin, out, scratch[-1].at[0])
        s.sent()


def scatter_pair(a, b, hot, rows, U, B, cid):
    F = U * B
    experts, _, D = a.shape
    G, n, KB = hot.shape
    RB = n // experts
    parts = max(1, F // 32)
    D = D // parts
    dma = pltpu.SemaphoreType.DMA

    def call(c):
        return pl.pallas_call(
            functools.partial(pair_kernel, U, B, pl.ds(c * D, D)),
            out_shape=[jax.ShapeDtypeStruct((2, rows, D), jnp.float32)] * 2,
            in_specs=any_specs(3),
            out_specs=any_specs(2),
            scratch_shapes=Scatter.scratch(U, B, rows, D, a.dtype) * 2 + [
                pltpu.VMEM((experts, RB, D), a.dtype), pltpu.VMEM((n, KB), hot.dtype),
                pltpu.VMEM((4, 2, rows, D), a.dtype), dma((2,)), dma((1,))],
            compiler_params=pltpu.CompilerParams(
                collective_id=cid, has_side_effects=True, vmem_limit_bytes=62 * 2**20),
        )(a, b, hot)

    got = [call(c) for c in range(parts)]
    return tuple(jnp.concatenate([g[i] for g in got], axis=-1) for i in range(2))


class PairExchange:
    def __init__(self, p, src, out, acc, rc, local, send, recv):
        self.p, self.src, self.out, self.acc, self.rc = p, src, out, acc, rc
        self.local, self.send, self.recv = local, send, recv

    @staticmethod
    def scratch(U, B, rows, w, t):
        dma = pltpu.SemaphoreType.DMA
        return [pltpu.VMEM((2 * B, rows, w), t), pltpu.VMEM((2 * B, rows, w), t),
                dma((1,)), dma((1 + 2 * B,)), dma((1 + 2 * B,))]

    SCRATCH = 5

    def across(self):
        p = self.p
        return remote(self.src.at[1 - p.x], self.rc, self.send.at[0], self.recv.at[0], p.x_peer)

    def own(self):
        return pltpu.make_async_copy(self.src.at[self.p.x], self.acc, self.local.at[0])

    def away(self, o):
        p = self.p
        r = lax.rem(p.r + o, 2 * p.B)
        return remote(self.acc.at[r], self.out.at[p.r], self.send.at[1 + r], self.recv.at[1 + p.r], p.plane_dev(r))

    def begin(self):
        self.across().start()
        self.own().start()

    def middle(self):
        p = self.p
        self.own().wait()
        self.across().wait_recv()

        @pl.loop(0, 2 * p.B)
        def _(r):
            t = self.acc[r].astype(jnp.float32) + self.rc[r].astype(jnp.float32)
            self.acc[r] = t.astype(self.acc.dtype)

        @pl.loop(1, 2 * p.B)
        def _(o):
            self.away(o).start()

        cp = pltpu.make_async_copy(self.acc.at[p.r], self.out.at[p.r], self.local.at[0])
        cp.start()
        cp.wait()

    def end(self):
        p = self.p
        self.across().wait_send()

        @pl.loop(1, 2 * p.B)
        def _(o):
            r = lax.rem(p.r + o, 2 * p.B)
            part = self.out.at[r]
            remote(part, part, self.send.at[0], self.recv.at[1 + r], p.x_peer).wait_recv()
            self.away(o).wait_send()


def finish_kernel(U, B, more, *refs):
    p = Place(U, B)
    p.barrier("plane")
    n = 4 if more else 3
    srcs, outs, scratch = refs[:n], refs[n:2 * n + 1], refs[2 * n + 1:]
    at = PlaneScatter.SCRATCH
    work = [PlaneScatter(p, *scratch[:at])]
    if more:
        work.append(Scatter(p, *scratch[at:at + Scatter.SCRATCH]))
        at += Scatter.SCRATCH
    ex = []
    for i in range(2):
        ex.append(PairExchange(p, srcs[i], outs[i], *scratch[at:at + PairExchange.SCRATCH]))
        at += PairExchange.SCRATCH
    stage, sems = scratch[at:]
    for s, src in zip(work, srcs[2:]):
        s.load(src)
    for e in ex:
        e.begin()
    work[0].step(0)
    for e in ex:
        e.middle()
    for s in work[1:]:
        s.step(0)
    for j in range(1, p.Z + 1):
        for s in work:
            s.step(j)
    fin = work[0].fin
    rows = fin.shape[1]

    def one(m, _):
        r = pl.ds(pl.multiple_of(m * 16, 16), 16)
        stage[r, :] = fin[1 - p.x, r, :].astype(stage.dtype)
        return 0

    lax.fori_loop(0, rows // 16, one, 0)
    away = remote(stage, outs[3], sems.at[0], sems.at[1], p.x_peer)
    away.start()
    keep_sum(fin.at[p.x], outs[2], sems.at[2])
    if more:
        work[1].step(p.Z + 1)
        keep_sum(work[1].fin, outs[4], sems.at[2])
    away.wait_recv()
    away.wait_send()
    for s in work:
        s.sent()
    for e in ex:
        e.end()


def finish(weights, small, hidden, out, U, B, cid):
    F = U * B
    parts = max(1, F // 32)
    D = hidden.shape[-1] // parts
    sds, f32 = jax.ShapeDtypeStruct, jnp.float32

    def call(h, o, cid):
        args = [m.reshape((2, 2 * B) + m.shape[1:]) for m in (weights, small)] + [h]
        shapes = [sds((2 * B,) + m.shape[1:], m.dtype) for m in (weights, small)]
        shapes += [sds(h.shape[1:], f32), sds(h.shape[1:], h.dtype)]
        scratch = PlaneScatter.scratch(U, B, h.shape[1], h.shape[2], h.dtype)
        if o is not None:
            args.append(o)
            shapes.append(sds(o.shape[1:], f32))
            scratch += Scatter.scratch(U, B, o.shape[2], o.shape[3], o.dtype)
        for m in (weights, small):
            scratch += PairExchange.scratch(U, B, m.shape[1], m.shape[2], m.dtype)
        return pl.pallas_call(
            functools.partial(finish_kernel, U, B, o is not None),
            out_shape=shapes,
            in_specs=any_specs(len(args)),
            out_specs=any_specs(len(shapes)),
            scratch_shapes=scratch + [pltpu.VMEM(h.shape[1:], h.dtype), pltpu.SemaphoreType.DMA((3,))],
            compiler_params=pltpu.CompilerParams(
                collective_id=cid, has_side_effects=True, vmem_limit_bytes=62 * 2**20),
        )(*args)

    if parts == 1:
        return call(hidden, out, cid)
    got = [call(hidden[..., n * D:(n + 1) * D], None, cid) for n in range(parts)]
    own, other = (jnp.concatenate([g[i] for g in got], axis=-1) for i in (2, 3))
    return got[0][0], got[0][1], own, other, scatter_by_permutes(out, U, B)


def scatter_by_permutes(v, U, B):
    X, Y, Z = U // 2, 2, B // 2
    f32 = jnp.float32
    u, b = lax.axis_index("ulysses"), lax.axis_index("blk")
    c, x, y, z = lax.rem(u, 2), lax.div(u, 2), lax.rem(b, Y), lax.div(b, Y)
    where = {"c": c, "x": x, "y": y, "z": z}
    size = {"c": 2, "x": X, "y": Y, "z": Z}

    def pairs(axis, by):
        out = []
        for f in range(U * B):
            at = {"x": f // B // 2, "c": f // B % 2, "z": f % B // Y, "y": f % Y}
            at[axis] = (at[axis] + by) % size[axis]
            out.append((f, (at["x"] * 2 + at["c"]) * B + at["z"] * Y + at["y"]))
        return out

    def fold(m, axis, dim):
        n = size[axis]
        total = lax.dynamic_index_in_dim(m, where[axis], dim, keepdims=False).astype(f32)
        for by in range(1, n):
            part = lax.dynamic_index_in_dim(m, lax.rem(where[axis] + by, n), dim, keepdims=False)
            total = total + lax.ppermute(part, ("ulysses", "blk"), pairs(axis, by)).astype(f32)
        return total

    rows, D = v.shape[-2:]
    m = fold(v.reshape(X, 2, Z, Y, 2, rows, D), "c", 1).astype(v.dtype)
    first = fold(m[:, :, :, 0], "x", 0).astype(v.dtype)
    first = fold(first, "y", 1).astype(v.dtype)
    second = fold(m[:, :, :, 1], "y", 2).astype(v.dtype)
    second = fold(second, "x", 0).astype(v.dtype)
    return fold(jnp.stack([first, second], axis=1), "z", 0)


def rms_norm(values, gains):
    return values * lax.rsqrt(jnp.mean(values * values, axis=-1, keepdims=True) + EPSILON) * gains


def dot(a, b, ca, cb):
    return lax.dot_general(a, b, (((ca,), (cb,)), ((), ())), preferred_element_type=jnp.float32)


def attend_kernel(scale, q_ref, k_ref, vt_ref, o_ref, lse_ref):
    s = dot(k_ref[...], q_ref[...], 1, 1) * scale
    top = jnp.max(s, axis=0, keepdims=True)
    e = jnp.exp(s - top)
    total = jnp.sum(e, axis=0, keepdims=True)
    o = dot(vt_ref[...], e.astype(jnp.bfloat16), 1, 0) / total
    o_ref[...] = o.T.astype(o_ref.dtype)
    lse_ref[...] = top + jnp.log(total)


def attend(q, k, vt):
    n = q.shape[0]
    bq = 256 if n <= 2048 else 128
    return pl.pallas_call(
        functools.partial(attend_kernel, 1.0 / math.sqrt(HD)),
        grid=(n // bq,),
        in_specs=[
            pl.BlockSpec((bq, HD), lambda i: (i, 0)),
            pl.BlockSpec((n, HD), lambda i: (0, 0)),
            pl.BlockSpec((HD, n), lambda i: (0, 0)),
        ],
        out_specs=[pl.BlockSpec((bq, HD), lambda i: (i, 0)), pl.BlockSpec((1, bq), lambda i: (0, i))],
        out_shape=[jax.ShapeDtypeStruct((n, HD), jnp.bfloat16), jax.ShapeDtypeStruct((1, n), jnp.float32)],
        compiler_params=pltpu.CompilerParams(vmem_limit_bytes=58 * 2**20),
    )(q, k, vt)


def attend_back_kernel(scale, q_ref, do_ref, lse_ref, k_ref, kt_ref, v_ref, dq_ref, dk_ref, dv_ref):
    @pl.when(pl.program_id(0) == 0)
    def _():
        dk_ref[...] = jnp.zeros_like(dk_ref)
        dv_ref[...] = jnp.zeros_like(dv_ref)

    p = jnp.exp(dot(k_ref[...], q_ref[...], 1, 1) * scale - lse_ref[...])
    dp = dot(v_ref[...], do_ref[...], 1, 1)
    delta = jnp.sum(p * dp, axis=0, keepdims=True)
    ds = (p * (dp - delta)).astype(jnp.bfloat16)
    dv_ref[...] += dot(p.astype(jnp.bfloat16), do_ref[...], 1, 0)
    dk_ref[...] += dot(ds, q_ref[...], 1, 0) * scale
    dq_ref[...] = (dot(kt_ref[...], ds, 1, 0) * scale).T


def attend_back(q, do, lse, k, kt, v):
    n = q.shape[0]
    bq = 256 if n <= 2048 else 128
    row = lambda i: (i, 0)
    whole = lambda i: (0, 0)
    f32 = jax.ShapeDtypeStruct((n, HD), jnp.float32)
    return pl.pallas_call(
        functools.partial(attend_back_kernel, 1.0 / math.sqrt(HD)),
        grid=(n // bq,),
        in_specs=[
            pl.BlockSpec((bq, HD), row),
            pl.BlockSpec((bq, HD), row),
            pl.BlockSpec((1, bq), lambda i: (0, i)),
            pl.BlockSpec((n, HD), whole),
            pl.BlockSpec((HD, n), whole),
            pl.BlockSpec((n, HD), whole),
        ],
        out_specs=[pl.BlockSpec((bq, HD), row), pl.BlockSpec((n, HD), whole), pl.BlockSpec((n, HD), whole)],
        out_shape=[f32, f32, f32],
        compiler_params=pltpu.CompilerParams(vmem_limit_bytes=58 * 2**20),
    )(q, do, lse, k, kt, v)


def turn(v, cosine, sine):
    return v * cosine + pltpu.roll(v, HD // 2, 1) * sine


def project_kernel(tok_ref, gain_ref, w_ref, qk_ref, cos_ref, sin_ref,
                   q_ref, k_ref, v_ref, kt_ref, vt_ref, rq_ref, rk_ref):
    bf16 = jnp.bfloat16
    raw = dot(rms_norm(tok_ref[...].astype(jnp.float32), gain_ref[...]).astype(bf16), w_ref[...], 1, 0)
    rq, rk, v = raw[:, :HD], raw[:, HD:2 * HD], raw[:, 2 * HD:].astype(bf16)
    rq_ref[...] = rq
    rk_ref[...] = rk
    q_ref[...] = turn(rms_norm(rq, qk_ref[0:1]), cos_ref[...], sin_ref[...]).astype(bf16)
    k = turn(rms_norm(rk, qk_ref[1:2]), cos_ref[...], sin_ref[...])
    k_ref[...] = k.astype(bf16)
    kt_ref[...] = k.T.astype(bf16)
    v_ref[...] = v
    vt_ref[...] = raw[:, 2 * HD:].T.astype(bf16)


def project(tok, gain, w, qk, cosine, sine):
    n, D = tok.shape
    bm = 256
    row, whole = (lambda i: (i, 0)), (lambda i: (0, 0))
    head, across = pl.BlockSpec((bm, HD), row), pl.BlockSpec((HD, bm), lambda i: (0, i))
    sds = jax.ShapeDtypeStruct
    f32, bf16 = jnp.float32, jnp.bfloat16
    return pl.pallas_call(
        project_kernel,
        grid=(n // bm,),
        in_specs=[
            pl.BlockSpec((bm, D), row), pl.BlockSpec((1, D), whole), pl.BlockSpec((D, 3 * HD), whole),
            pl.BlockSpec((2, HD), whole), head, head,
        ],
        out_specs=[head, head, head, across, across, head, head],
        out_shape=[sds((n, HD), bf16)] * 3 + [sds((HD, n), bf16)] * 2 + [sds((n, HD), f32)] * 2,
        compiler_params=pltpu.CompilerParams(vmem_limit_bytes=58 * 2**20),
    )(tok, gain, w, qk, cosine, sine)


def head_back_kernel(dq_ref, dk_ref, dv_ref, rq_ref, rk_ref, cos_ref, sin_ref, qk_ref, tok_ref, gain_ref, w_ref,
                     part_ref, dw_ref, dg_ref, da_ref):
    f32, bf16 = jnp.float32, jnp.bfloat16

    @pl.when(pl.program_id(0) == 0)
    def _():
        dw_ref[...] = jnp.zeros_like(dw_ref)
        dg_ref[...] = jnp.zeros_like(dg_ref)
        da_ref[...] = jnp.zeros_like(da_ref)

    grads = []
    for n, (g_ref, raw_ref) in enumerate(((dq_ref, rq_ref), (dk_ref, rk_ref))):
        w = turn(g_ref[...].astype(bf16).astype(f32), cos_ref[...], -sin_ref[...])
        u = raw_ref[...]
        r = lax.rsqrt(jnp.mean(u * u, axis=-1, keepdims=True) + EPSILON)
        norm = u * r
        dg_ref[n:n + 1, :] += jnp.sum(w * norm, axis=0, keepdims=True)
        m = w * qk_ref[n:n + 1]
        grads.append((r * (m - norm * jnp.mean(m * norm, axis=-1, keepdims=True))).astype(bf16))
    grads.append(dv_ref[...].astype(bf16))
    grad = jnp.concatenate(grads, axis=1)
    tok = tok_ref[...].astype(f32)
    norm = tok * lax.rsqrt(jnp.mean(tok * tok, axis=-1, keepdims=True) + EPSILON)
    hidden = (norm * gain_ref[...]).astype(bf16)
    D = tok.shape[1]
    cut = min(D, 512)
    for n in range(0, D, cut):
        part = dot(grad, w_ref[n:n + cut, :], 1, 1)
        part_ref[:, n:n + cut] = part.astype(bf16)
        da_ref[0:1, n:n + cut] += jnp.sum(part * norm[:, n:n + cut], axis=0, keepdims=True)
        dw_ref[n:n + cut, :] += dot(hidden[:, n:n + cut], grad, 0, 0)


def head_back(dq, dk, dv, rq, rk, cosine, sine, qk, tok, gain, w):
    n, D = tok.shape
    bm = 512
    row, whole = (lambda i: (i, 0)), (lambda i: (0, 0))
    head = pl.BlockSpec((bm, HD), row)
    sds = jax.ShapeDtypeStruct
    return pl.pallas_call(
        head_back_kernel,
        grid=(n // bm,),
        in_specs=[head] * 7 + [
            pl.BlockSpec((2, HD), whole), pl.BlockSpec((bm, D), row), pl.BlockSpec((1, D), whole),
            pl.BlockSpec((D, 3 * HD), whole)],
        out_specs=[
            pl.BlockSpec((bm, D), row), pl.BlockSpec((D, 3 * HD), whole), pl.BlockSpec((8, HD), whole),
            pl.BlockSpec((8, D), whole)],
        out_shape=[sds((n, D), jnp.bfloat16), sds((D, 3 * HD), jnp.float32), sds((8, HD), jnp.float32),
                   sds((8, D), jnp.float32)],
        compiler_params=pltpu.CompilerParams(vmem_limit_bytes=58 * 2**20),
    )(dq, dk, dv, rq, rk, cosine, sine, qk, tok, gain, w)


def dispatch_kernel(val_ref, gate_ref, norm_ref, cot_ref, x_ref, pg_ref, hot_ref, rg_ref, rg_s):
    f32, bf16 = jnp.float32, jnp.bfloat16
    experts, KB = val_ref.shape[1:]
    RB, D = x_ref.shape[1:]
    at = lax.broadcasted_iota(jnp.int32, (RB, KB), 0)
    for e in range(experts):
        hit = at == val_ref[0, e:e + 1, :]
        hot_ref[0, e * RB:(e + 1) * RB, :] = jnp.where(hit, 1.0, 0.0).astype(bf16)
        weight = jnp.sum(jnp.where(hit, gate_ref[0, e:e + 1, :], 0.0), axis=1, keepdims=True)
        rg_s[e * RB:(e + 1) * RB, :] = weight
        rg_ref[e] = jnp.broadcast_to(weight, (RB, rg_ref.shape[2]))
    cut = min(D, 512)
    hot = hot_ref[0]
    norm = norm_ref[...].reshape(KB, D)
    cot = cot_ref[...].reshape(KB, D)
    for n in range(0, D, cut):
        x = dot(hot, norm[:, n:n + cut], 1, 0).astype(bf16)
        x_ref[:, :, n:n + cut] = x.reshape(experts, RB, cut)
        g = (dot(hot, cot[:, n:n + cut], 1, 0) * rg_s[...]).astype(bf16)
        pg_ref[:, :, n:n + cut] = g.reshape(experts, RB, cut)


def group_spec(shape, Z):
    X, two, _, Y, T, D = shape
    return pl.BlockSpec((1, two, 1, Y, T, D), lambda g: (g // Z, 0, g % Z, 0, 0, 0))


def dispatch(val, gate, normed, cot, RB):
    G, experts, KB = val.shape
    D, Z = normed.shape[-1], normed.shape[2]
    one = pl.BlockSpec((1, experts, KB), lambda g: (g, 0, 0))
    out = pl.BlockSpec((experts, RB, D), lambda g: (0, g, 0))
    sds = jax.ShapeDtypeStruct
    return pl.pallas_call(
        dispatch_kernel,
        grid=(G,),
        in_specs=[one, one, group_spec(normed.shape, Z), group_spec(cot.shape, Z)],
        out_specs=[out, out, pl.BlockSpec((1, experts * RB, KB), lambda g: (g, 0, 0)),
                   pl.BlockSpec((experts, RB, 128), lambda g: (0, g, 0))],
        out_shape=[sds((experts, G * RB, D), jnp.bfloat16)] * 2 + [
            sds((G, experts * RB, KB), jnp.bfloat16), sds((experts, G * RB, 128), jnp.float32)],
        scratch_shapes=[pltpu.VMEM((experts * RB, 1), jnp.float32)],
        compiler_params=pltpu.CompilerParams(vmem_limit_bytes=58 * 2**20),
    )(val, gate, normed, cot)


def expert_kernel(x_ref, pg_ref, rg_ref, wg_ref, wu_ref, wd_ref, y_ref, dx_ref, dwg_ref, dwu_ref, dwd_ref):
    bf16 = jnp.bfloat16
    x, pg = x_ref[0], pg_ref[0]
    D = x.shape[1]
    gate, up = dot(x, wg_ref[0], 1, 0), dot(x, wu_ref[0], 1, 0)
    sigma = jax.nn.sigmoid(gate)
    silu = gate * sigma
    inner = (silu * up).astype(bf16)
    back = dot(pg, wd_ref[0], 1, 1)
    dgate = (back * up * sigma * (1.0 + gate * (1.0 - sigma))).astype(bf16)
    dup = (back * silu).astype(bf16)
    cut = min(D, 512)
    weight = rg_ref[0, :, 0:1]
    first = pl.program_id(1) == 0

    def gather_in(ref, ix, value):
        if pl.num_programs(1) == 1:
            ref[ix] = value
        else:
            ref[ix] = value + jnp.where(first, 0.0, ref[ix])

    for n in range(0, D, cut):
        c = slice(n, n + cut)
        y_ref[0, :, c] = (dot(inner, wd_ref[0, :, c], 1, 0) * weight).astype(bf16)
        dx_ref[0, :, c] = (dot(dgate, wg_ref[0, c, :], 1, 1) + dot(dup, wu_ref[0, c, :], 1, 1)).astype(bf16)
        gather_in(dwg_ref, (0, c, slice(None)), dot(x_ref[0, :, c], dgate, 0, 0))
        gather_in(dwu_ref, (0, c, slice(None)), dot(x_ref[0, :, c], dup, 0, 0))
        gather_in(dwd_ref, (0, slice(None), c), dot(inner, pg_ref[0, :, c], 0, 0))


def expert_layer(x, pg, rg, wg, wu, wd):
    rows = x.shape[1]
    step = 640 if rows % 640 == 0 else rows
    some = lambda a: pl.BlockSpec((1, step) + a.shape[2:], lambda e, i: (e, i, 0))
    whole = lambda a: pl.BlockSpec((1,) + a.shape[1:], lambda e, i: (e, 0, 0))
    sds = jax.ShapeDtypeStruct
    return pl.pallas_call(
        expert_kernel,
        grid=(x.shape[0], rows // step),
        in_specs=[some(a) for a in (x, pg, rg)] + [whole(a) for a in (wg, wu, wd)],
        out_specs=[some(a) for a in (x, x)] + [whole(a) for a in (wg, wu, wd)],
        out_shape=[sds(x.shape, x.dtype)] * 2 + [sds(a.shape, jnp.float32) for a in (wg, wu, wd)],
        compiler_params=pltpu.CompilerParams(vmem_limit_bytes=60 * 2**20),
    )(x, pg, rg, wg, wu, wd)


def body(tokens, w_query, w_key, w_value, w_out, attn_gain, ffn_gain, qk_gain,
         expert_gate, expert_up, expert_down, routes, gates, order, cotangent):
    f32, bf16 = jnp.float32, jnp.bfloat16
    positions, seqs, D = tokens.shape
    U, B = lax.axis_size("ulysses"), lax.axis_size("blk")
    F = U * B
    u, b = lax.axis_index("ulysses"), lax.axis_index("blk")
    H = w_query.shape[1] // HD
    W = w_query.shape[0]
    L = F * positions
    T = seqs * positions
    top_count = routes.shape[-1]
    local_experts = expert_gate.shape[0]
    E = local_experts * B
    R = 2 * B // H
    x_here = u // 2
    first_copy = lax.rem((u % 2) * B + b, R) == 0

    tok = tokens.transpose(1, 0, 2)
    cot = cotangent.transpose(1, 0, 2)
    rows_f = tok.reshape(T, D).astype(f32)

    expert_of = routes.transpose(1, 0, 2).reshape(-1)
    prio = order.reshape(positions, seqs, top_count).transpose(1, 0, 2).reshape(-1)
    same = expert_of[:, None] == expert_of[None, :]
    ranks = jnp.sum((same & (prio[None, :] < prio[:, None])).astype(jnp.int32), axis=1)
    slot = jnp.where(ranks < CAP, expert_of * CAP + ranks, -1).astype(f32)
    pairs = slot.shape[0]

    nq = qk_gain.shape[1]
    small = jnp.concatenate(
        [slot, gates.transpose(1, 0, 2).reshape(-1)]
        + [g.astype(f32) for g in (attn_gain, ffn_gain, qk_gain[0], qk_gain[1])])
    small = jnp.pad(small, (0, -small.shape[0] % 1024)).reshape(-1, 128)
    heads_w = jnp.stack([w_query, w_key, w_value]).reshape(3, W, H, HD).transpose(2, 1, 0, 3).reshape(H, W, 3 * HD)
    if R > 1:
        heads_w = heads_w[np.arange(2 * B) // R]
    seq_tok, table, head_w = front(tok, small, heads_w, U, B, 1)
    seq_tok, head_w = seq_tok.reshape(L, D), head_w.reshape(D, 3 * HD)
    out_w = lax.all_gather(w_out, AXES, axis=0, tiled=True)
    cot_all = lax.all_gather(cot, AXES, axis=0)
    table = table.reshape(F, -1)
    cut = 2 * pairs
    attn_g = table[:, cut:cut + W].reshape(1, D)
    ffn_g = table[:, cut + W:cut + 2 * W].reshape(1, D)
    cut = cut + 2 * W
    qk_g = jnp.stack([table[:, cut:cut + nq].reshape(-1), table[:, cut + nq:cut + 2 * nq].reshape(-1)])

    groups = (U // 2, 2, B // 2, 2)
    GB = 4
    G, KB = F // GB, GB * T
    RB = -(-GB * CAP // 16) * 16
    slot_all = table[:, :pairs].astype(jnp.int32).reshape(F, T, top_count)
    gate_all = table[:, pairs:2 * pairs].reshape(F, T, top_count)
    place = ((np.arange(F) // B % 2) * 2 + np.arange(F) % 2).astype(np.int32)
    base = (b * local_experts + jnp.arange(local_experts, dtype=jnp.int32)) * CAP
    off = slot_all[:, :, :, None] - base
    mine = (off >= 0) & (off < CAP)
    val = jnp.sum(jnp.where(mine, off + 1, 0), axis=2)
    val = jnp.where(val > 0, val - 1 + jnp.asarray(place)[:, None, None] * CAP, -1)
    gate_of = jnp.sum(jnp.where(mine, gate_all[:, :, :, None], 0.0), axis=2)

    def by_group(m):
        return m.reshape(groups + (T, local_experts)).transpose(0, 2, 5, 1, 3, 4).reshape(G, local_experts, KB)

    val, gate_of = by_group(val), by_group(gate_of)

    half = HD // 2
    inverse = ROPE_BASE ** (-2.0 * jnp.arange(half).astype(f32) / HD)
    angles = jnp.arange(L).astype(f32)[:, None] * inverse[None, :]
    cosine = jnp.concatenate([jnp.cos(angles)] * 2, axis=1)
    sine = jnp.concatenate([-jnp.sin(angles), jnp.sin(angles)], axis=1)
    q, k, v, kt, vt, raw_q, raw_k = project(seq_tok, attn_g, head_w, qk_g, cosine, sine)
    att, lse = attend(q, k, vt)
    att_rows = exchange(att.reshape(F, positions, HD), U, B, 6)

    def from_heads(m):
        m = m.reshape(2, 2 * B, positions, HD).transpose(0, 2, 1, 3)
        return m.reshape(2, positions, H, R, HD)[:, :, :, 0].reshape(T, H * HD)

    attended = from_heads(att_rows)
    residual = rows_f + jnp.dot(attended, out_w, preferred_element_type=f32)
    normed_full, ffn_back = jax.vjp(rms_norm, residual, ffn_g)
    normed = normed_full.astype(bf16).reshape(2, positions, D)

    normed_all = gather_blocks(normed, U, B, 2)
    shape = groups + (T, D)
    x, pair_grad, hot, row_gate = dispatch(val, gate_of, normed_all.reshape(shape), cot_all.reshape(shape), RB)
    y, dx, gate_grad, up_grad, down_grad = expert_layer(x, pair_grad, row_gate, expert_gate, expert_up, expert_down)
    normed_grad, mixed_sum = scatter_pair(dx, y, hot, positions, U, B, 3)
    mixed = (residual + mixed_sum.reshape(T, D)).reshape(2, positions, D).transpose(1, 0, 2).astype(bf16)
    normed_grad = normed_grad.reshape(T, D)

    residual_norm_grad, ffn_gain_part = ffn_back(normed_grad)
    residual_grad = cot.reshape(T, D).astype(f32) + residual_norm_grad
    attn_out_grad = residual_grad.astype(bf16)
    att_grad = dot(attn_out_grad, out_w, 1, 1).astype(bf16)
    att_grad = jnp.repeat(att_grad.reshape(2, positions, H, HD).transpose(0, 2, 1, 3), R, axis=1)
    att_grad = att_grad.reshape(F, positions, HD)
    do = exchange(att_grad, U, B, 6).reshape(L, HD)
    out_part = dot(attended, attn_out_grad, 0, 0).astype(bf16)
    out_part = out_part.reshape(F, 2, W // 2, D)
    dq, dk, dv = attend_back(q, do, lse, k, kt, v)
    if R > 1:
        dq, dk, dv = (jnp.where(first_copy, m, 0.0) for m in (dq, dk, dv))
    hidden_part, weight_part, qk_part, attn_gain_part = head_back(
        dq, dk, dv, raw_q, raw_k, cosine, sine, qk_g, seq_tok, attn_g, head_w)
    weight_part = weight_part.astype(bf16).reshape(F, W, 3 * HD)
    small = jnp.concatenate(
        [attn_gain_part[0].reshape(F, W), ffn_gain_part.reshape(F, W),
         qk_part[0].reshape(F, nq), qk_part[1].reshape(F, nq)], axis=1)
    small = jnp.pad(small, ((0, 0), (0, -small.shape[1] % 1024))).reshape(F, -1, 128)
    weight_grad, small, own, other, out_grad = finish(
        weight_part, small, hidden_part.reshape(F, positions, D), out_part, U, B, 4)
    other = other.astype(f32)
    hidden_grad = jnp.where(x_here == 0, jnp.stack([own, other]), jnp.stack([other, own]))
    small = jnp.sum(small, axis=0).reshape(-1)
    weight_grad = weight_grad.reshape(H, R, W, 3 * HD).astype(f32).sum(axis=1)
    weight_grad = weight_grad.transpose(1, 0, 2).reshape(W, H, 3, HD)
    query_grad, key_grad, value_grad = (weight_grad[:, :, n].reshape(W, H * HD) for n in range(3))
    hidden_grad, out_grad = hidden_grad.reshape(T, D), out_grad.reshape(W, D)
    inv = lax.rsqrt(jnp.mean(rows_f * rows_f, axis=-1, keepdims=True) + EPSILON)
    norm = rows_f * inv
    m = hidden_grad * attn_g
    token_grad = inv * (m - norm * jnp.mean(m * norm, axis=-1, keepdims=True))
    input_grad = (residual_grad + token_grad).reshape(2, positions, D).transpose(1, 0, 2)
    return (
        mixed, input_grad, query_grad, key_grad, value_grad, out_grad,
        small[:W], small[W:2 * W], small[2 * W:2 * W + 2 * nq].reshape(2, nq),
        gate_grad, up_grad, down_grad,
    )


def solution(mesh):
    rows = P(AXES, None, None)
    flat = P(AXES, None)
    by_expert = (P("blk", None, "ulysses"), P("blk", None, "ulysses"), P("blk", "ulysses", None))
    in_specs = (rows, flat, flat, flat, flat, P(AXES), P(AXES), P(None, AXES)) + by_expert + (rows, rows, flat, rows)
    out_specs = (rows, rows, flat, flat, flat, flat, P(AXES), P(AXES), P(None, AXES)) + by_expert
    return jax.shard_map(body, mesh=mesh, in_specs=in_specs, out_specs=out_specs, check_vma=False)
```

```python
import functools
import math

import jax
import jax.numpy as jnp
import numpy as np
from jax import lax
from jax.experimental import pallas as pl
from jax.experimental.pallas import tpu as pltpu
from jax.sharding import PartitionSpec as P

HD = 128
CAP = 18
EPSILON = 1e-06
ROPE_BASE = 10000.0
AXES = ("ulysses", "blk")
MESH = pl.DeviceIdType.MESH


class Place:
    def __init__(self, U, B):
        self.U, self.B = U, B
        self.X, self.Y = U // 2, 2
        self.Z = B // self.Y
        self.Q, self.F = self.X * B, U * B
        u, b = lax.axis_index("ulysses"), lax.axis_index("blk")
        self.c, self.x = lax.rem(u, 2), lax.div(u, 2)
        self.y, self.z = lax.rem(b, self.Y), lax.div(b, self.Y)
        self.r = self.c * B + b
        self.me = u * B + b
        self.core_peer = self.dev(self.x, self.y, self.z, 1 - self.c)
        self.x_peer = self.dev(1 - self.x, self.y, self.z, self.c)

    def dev(self, x, y, z, c):
        return (x * 2 + c, z * self.Y + y)

    def block(self, x, y, z, c):
        return (x * 2 + c) * self.B + z * self.Y + y

    def chip(self, x, y, z):
        return x * self.B + z * self.Y + y

    def at(self, r, x):
        return x * 2 * self.B + r

    def plane_dev(self, r):
        return (self.x * 2 + lax.div(r, self.B), lax.rem(r, self.B))

    def flat_dev(self, f):
        return (lax.div(f, self.B), lax.rem(f, self.B))

    def others(self, axis):
        n = {"x": self.X, "y": self.Y, "z": self.Z}[axis]
        i = {"x": self.x, "y": self.y, "z": self.z}[axis]
        return [lax.rem(i + o, n) for o in range(1, n)]

    def barrier(self, reach):
        sem = pltpu.get_barrier_semaphore()

        def greet(d):
            pl.semaphore_signal(sem, inc=1, device_id=d, device_id_type=MESH)

        if reach == "every":
            @pl.loop(1, self.F)
            def _(o):
                greet(self.flat_dev(lax.rem(self.me + o, self.F)))

            pl.semaphore_wait(sem, self.F - 1)
            return
        if reach == "plane":
            greet(self.x_peer)

            @pl.loop(1, 2 * self.B)
            def _(o):
                greet(self.plane_dev(lax.rem(self.r + o, 2 * self.B)))

            pl.semaphore_wait(sem, 2 * self.B)
            return
        greet(self.core_peer)
        for k in self.others("x"):
            greet(self.dev(k, self.y, self.z, self.c))
        for k in self.others("y"):
            greet(self.dev(self.x, k, self.z, self.c))
        count = self.X + self.Y - 1
        if reach == "chain":
            below, above = self.z > 0, self.z < self.Z - 1

            @pl.when(below)
            def _():
                greet(self.dev(self.x, self.y, self.z - 1, self.c))

            @pl.when(above)
            def _():
                greet(self.dev(self.x, self.y, self.z + 1, self.c))

            count = count + jnp.where(below, 1, 0) + jnp.where(above, 1, 0)
        else:
            for k in self.others("z"):
                greet(self.dev(self.x, self.y, k, self.c))
            count += self.Z - 1
        pl.semaphore_wait(sem, count)


def remote(src, dst, send, recv, dev):
    return pltpu.make_async_remote_copy(
        src_ref=src, dst_ref=dst, send_sem=send, recv_sem=recv, device_id=dev, device_id_type=MESH)


class Gather:
    def __init__(self, p, src, out, send_sem, recv_sem, local_sem, like=(0, 1)):
        self.p, self.src, self.out, self.like = p, src, out, like
        self.send_sem, self.recv_sem, self.local_sem = send_sem, recv_sem, local_sem
        self.steps = p.Z + 2
        self.started = []
        self.always = p.z >= 0

    @staticmethod
    def semaphores(U, B):
        dma = pltpu.SemaphoreType.DMA
        return [dma((4 + U // 2, 2, U * B)), dma((2, U * B)), dma((1,))]

    def where(self, half, x, y, z):
        f = self.p.block(x, y, z, self.p.c)
        return self.out.at[f, half], (half, f)

    def send(self, cond, src_ref, dst_ref, ix, way, dev):
        cp = remote(src_ref, dst_ref, self.send_sem.at[(way,) + ix], self.recv_sem.at[ix], dev)

        @pl.when(cond)
        def _():
            cp.start()

        self.started.append((cond, cp))

    def wait(self, ref, ix):
        remote(ref, ref, self.send_sem.at[(0,) + ix], self.recv_sem.at[ix], self.p.core_peer).wait_recv()

    def along(self, cond, half, x, y, z, axes):
        p = self.p
        ref, ix = self.where(half, x, y, z)
        for ax in axes:
            if ax == "core":
                self.send(cond, ref, ref, ix, 0, p.core_peer)
            elif ax == "up":
                self.send(cond & (p.z < p.Z - 1), ref, ref, ix, 1, p.dev(p.x, p.y, p.z + 1, p.c))
            elif ax == "down":
                self.send(cond & (p.z > 0), ref, ref, ix, 2, p.dev(p.x, p.y, p.z - 1, p.c))
            elif ax == "y":
                for i, k in enumerate(p.others("y")):
                    self.send(cond, ref, ref, ix, 3 + i, p.dev(p.x, k, p.z, p.c))
            else:
                for i, k in enumerate(p.others("x")):
                    self.send(cond, ref, ref, ix, 2 + p.Y + i, p.dev(k, p.y, p.z, p.c))

    def zs(self, step):
        p = self.p
        if step == 0:
            return [(self.always, p.z, ())]
        return [(p.z - step >= 0, p.z - step, ("up",)), (p.z + step < p.Z, p.z + step, ("down",))]

    def arrive(self, cond, half, x, y, z, axes):
        ref, ix = self.where(half, x, y, z)

        @pl.when(cond)
        def _():
            self.wait(ref, ix)

        self.along(cond, half, x, y, z, axes)

    def step(self, n):
        p = self.p
        if n == 0:
            cp = pltpu.make_async_copy(self.src, self.out.at[p.me], self.local_sem.at[0])
            cp.start()
            cp.wait()
            for half in (0, 1):
                self.along(self.always, half, p.x, p.y, p.z, ("up", "down", "y", "x"))
            for half in (0, 1):
                self.along(self.always, half, p.x, p.y, p.z, ("core",))
            return
        if n < p.Z:
            for half in (0, 1):
                for cond, k, on in self.zs(n):
                    self.arrive(cond, half, p.x, p.y, k, on + ("y", "x", "core"))
        if n <= p.Z:
            for cond, k, _ in self.zs(n - 1):
                for half, way in enumerate(self.like):
                    if way == 0:
                        for i in p.others("y"):
                            self.arrive(cond, half, p.x, i, k, ("x", "core"))
                    else:
                        for j in p.others("x"):
                            self.arrive(cond, half, j, p.y, k, ("y", "core"))
        if n >= 2:
            for cond, k, _ in self.zs(n - 2):
                for half, way in enumerate(self.like):
                    if way == 0:
                        for j in p.others("x"):
                            self.arrive(cond, half, j, p.y, k, ("core",))
                    else:
                        for i in p.others("y"):
                            self.arrive(cond, half, p.x, i, k, ("core",))
                for half in (0, 1):
                    for j in p.others("x"):
                        for i in p.others("y"):
                            self.arrive(cond, half, j, i, k, ("core",))

    def end(self):
        p = self.p
        for k in range(p.Z):
            for j in range(p.X):
                for i in range(p.Y):
                    f = p.block(j, i, k, 1 - p.c)
                    for half in (0, 1):
                        self.wait(self.out.at[f, half], (half, f))
        for cond, cp in self.started:
            @pl.when(cond)
            def _(cp=cp):
                cp.wait_send()


class PlaneGather(Gather):
    def __init__(self, *a):
        super().__init__(*a)
        self.steps = self.p.Z + 1

    @staticmethod
    def semaphores(U, B):
        dma = pltpu.SemaphoreType.DMA
        return [dma((5, 1, U * B)), dma((1, U * B)), dma((1,))]

    def where(self, half, x, y, z):
        f = self.p.block(half, y, z, self.p.c)
        return self.out.at[f], (0, f)

    def step(self, n):
        p = self.p
        if n == 0:
            cp = pltpu.make_async_copy(self.src.at[p.x], self.out.at[p.me], self.local_sem.at[0])
            cp.start()
            self.send(self.always, self.src.at[1 - p.x], self.out.at[p.me], (0, p.me), 4, p.x_peer)
            cp.wait()
            self.along(self.always, p.x, p.x, p.y, p.z, ("up", "down", "y", "core"))
            self.arrive(self.always, 1 - p.x, p.x, p.y, p.z, ("up", "down", "y", "core"))
            return
        if n < p.Z:
            for half in (0, 1):
                for cond, k, on in self.zs(n):
                    self.arrive(cond, half, p.x, p.y, k, on + ("y", "core"))
        for half in (0, 1):
            for cond, k, _ in self.zs(n - 1):
                for i in p.others("y"):
                    self.arrive(cond, half, p.x, i, k, ("core",))

    def end(self):
        p = self.p
        for k in range(p.Z):
            for i in range(p.Y):
                for half in (0, 1):
                    f = p.block(half, i, k, 1 - p.c)
                    self.wait(self.out.at[f], (0, f))
        for cond, cp in self.started:
            @pl.when(cond)
            def _(cp=cp):
                cp.wait_send()


class Spread:
    def __init__(self, p, same, src, out, send_sem, recv_sem):
        self.p, self.same, self.src, self.out = p, same, src, out
        self.send_sem, self.recv_sem = send_sem, recv_sem

    @staticmethod
    def semaphores(U, B):
        dma = pltpu.SemaphoreType.DMA
        return [dma((2, 2 * B)), dma((U * B,))]

    def part(self, r):
        return self.src if self.same else self.src.at[r]

    def out_to(self, o):
        p = self.p
        r = lax.rem(p.r + o, 2 * p.B)
        return remote(self.part(r), self.out.at[p.me], self.send_sem.at[0, r], self.recv_sem.at[p.me], p.plane_dev(r))

    def across(self, r):
        f = self.p.at(r, self.p.x)
        return remote(self.out.at[f], self.out.at[f], self.send_sem.at[1, r], self.recv_sem.at[f], self.p.x_peer)

    def arrive(self, f):
        remote(self.out.at[f], self.out.at[f], self.send_sem.at[0, 0], self.recv_sem.at[f], self.p.x_peer).wait_recv()

    def begin(self):
        p = self.p

        @pl.loop(1, 2 * p.B)
        def _(o):
            self.out_to(o).start()

        cp = pltpu.make_async_copy(self.part(p.r), self.out.at[p.me], self.send_sem.at[0, p.r])
        cp.start()
        cp.wait()
        self.across(p.r).start()

    def middle(self):
        p = self.p

        @pl.loop(1, 2 * p.B)
        def _(o):
            r = lax.rem(p.r + o, 2 * p.B)
            self.arrive(p.at(r, p.x))
            self.across(r).start()

    def end(self):
        p = self.p

        @pl.loop(0, 2 * p.B)
        def _(r):
            self.arrive(p.at(r, 1 - p.x))
            self.across(r).wait_send()

        @pl.loop(1, 2 * p.B)
        def _(o):
            self.out_to(o).wait_send()


def any_specs(n):
    return [pl.BlockSpec(memory_space=pl.ANY)] * n


def gather_kernel(U, B, experts, RB, src, val, gate, out, hot_out, rg_out, send, recv, local, hot, rg, store):
    p = Place(U, B)
    p.barrier("chain")
    g = Gather(p, src, out, send, recv, local)
    G, _, KB = val.shape
    per = -(-G // (g.steps - 2))
    at = lax.broadcasted_iota(jnp.int32, (RB, KB), 0)
    saves = [pltpu.make_async_copy(hot, hot_out, store.at[0]), pltpu.make_async_copy(rg, rg_out, store.at[1])]
    for n in range(g.steps):
        g.step(n)

        @pl.loop(min(n * per, G), min((n + 1) * per, G))
        def _(m):
            for e in range(experts):
                hit = at == val[m, e:e + 1, :]
                hot[m, e * RB:(e + 1) * RB, :] = jnp.where(hit, 1.0, 0.0).astype(hot.dtype)
                w = jnp.sum(jnp.where(hit, gate[m, e:e + 1, :], 0.0), axis=1, keepdims=True)
                rg[e, pl.ds(pl.multiple_of(m * RB, RB), RB), :] = jnp.broadcast_to(w, (RB, 128))

        if n == g.steps - 2:
            for cp in saves:
                cp.start()
    g.end()
    for cp in saves:
        cp.wait()


def gather_blocks(v, val, gate, RB, U, B, cid):
    G, experts, KB = val.shape
    sds = jax.ShapeDtypeStruct
    vmem = pl.BlockSpec(memory_space=pltpu.VMEM)
    hot, rg = sds((G, experts * RB, KB), jnp.bfloat16), sds((experts, G * RB, 128), jnp.float32)
    return pl.pallas_call(
        functools.partial(gather_kernel, U, B, experts, RB),
        out_shape=[sds((U * B,) + v.shape, v.dtype), hot, rg],
        in_specs=any_specs(1) + [vmem, vmem],
        out_specs=any_specs(3),
        scratch_shapes=Gather.semaphores(U, B) + [
            pltpu.VMEM(hot.shape, hot.dtype), pltpu.VMEM(rg.shape, rg.dtype), pltpu.SemaphoreType.DMA((2,))],
        compiler_params=pltpu.CompilerParams(
            collective_id=cid, has_side_effects=True, vmem_limit_bytes=32 * 2**20),
    )(v, val, gate)


def front_kernel(U, B, tok, small, weights, tok_out, small_out, weights_out, *sems):
    p = Place(U, B)
    p.barrier("plane")
    g = PlaneGather(p, tok, tok_out, *sems[:3])
    s = Spread(p, True, small, small_out, *sems[3:5])
    w = Spread(p, False, weights, weights_out, *sems[5:7])
    s.begin()
    g.step(0)
    w.begin()
    for n in range(1, g.steps):
        g.step(n)
        if n == 1:
            s.middle()
        if n == 2:
            w.middle()
    s.end()
    w.end()
    g.end()


def front(tok, small, weights, U, B, cid):
    F = U * B
    return pl.pallas_call(
        functools.partial(front_kernel, U, B),
        out_shape=[
            jax.ShapeDtypeStruct((F,) + tok.shape[1:], tok.dtype),
            jax.ShapeDtypeStruct((F,) + small.shape, small.dtype),
            jax.ShapeDtypeStruct((F,) + weights.shape[1:], weights.dtype),
        ],
        in_specs=any_specs(3),
        out_specs=any_specs(3),
        scratch_shapes=PlaneGather.semaphores(U, B) + Spread.semaphores(U, B) * 2,
        compiler_params=pltpu.CompilerParams(collective_id=cid, has_side_effects=True),
    )(tok, small, weights)


def exchange_kernel(U, B, src, out, send_sem, recv_sem):
    p = Place(U, B)
    p.barrier("every")

    def copy(o):
        f = lax.rem(p.me + o, p.F)
        return f, remote(src.at[f], out.at[p.me], send_sem.at[f], recv_sem.at[p.me], p.flat_dev(f))

    @pl.loop(1, p.F)
    def _(o):
        copy(o)[1].start()

    cp = pltpu.make_async_copy(src.at[p.me], out.at[p.me], recv_sem.at[p.me])
    cp.start()
    cp.wait()

    @pl.loop(1, p.F)
    def _(o):
        f, cp = copy(o)
        remote(out.at[f], out.at[f], send_sem.at[f], recv_sem.at[f], p.flat_dev(f)).wait_recv()
        cp.wait_send()


def exchange(v, U, B, cid):
    return pl.pallas_call(
        functools.partial(exchange_kernel, U, B),
        out_shape=jax.ShapeDtypeStruct(v.shape, v.dtype),
        in_specs=any_specs(1),
        out_specs=any_specs(1)[0],
        scratch_shapes=[pltpu.SemaphoreType.DMA((U * B,))] * 2,
        compiler_params=pltpu.CompilerParams(collective_id=cid, has_side_effects=True),
    )(v)


class Scatter:
    def __init__(self, p, acc, rc, rx0, rx1, ry0, ry1, rz, fin, loc, cs, cr, xs, xr, ys, yr, zs, zr, like=(0, 1)):
        self.p, self.like = p, like
        self.acc, self.rc, self.rx, self.ry, self.rz, self.fin = acc, rc, (rx0, rx1), (ry0, ry1), rz, fin
        self.loc, self.cs, self.cr = loc, cs, cr
        self.xs, self.xr, self.ys, self.yr, self.zs, self.zr = xs, xr, ys, yr, zs, zr
        self.order = p.others("z") + [p.z]
        self.steps = p.Z + 2
        self.started = []
        self.local = True

    @staticmethod
    def scratch(U, B, rows, D, t, like=(0, 1)):
        X, Y, Z, Q = U // 2, 2, B // 2, U * B // 2
        dma = pltpu.SemaphoreType.DMA
        x, y = max(X - 1, 1), Y - 1
        return [
            pltpu.VMEM((Q, 2, rows, D), t),
            pltpu.VMEM((Q, 2, rows, D), t),
            pltpu.VMEM((x, Z * Y, rows, D), t),
            pltpu.VMEM((x, Z if like[1] else Z * Y, rows, D), t),
            pltpu.VMEM((y, Z, rows, D), t),
            pltpu.VMEM((y, Z * X if like[1] else Z, rows, D), t),
            pltpu.VMEM((2, Z, rows, D), t),
            pltpu.VMEM((2, rows, D), jnp.float32),
            dma((Q, 2)),
            dma((Q, 2)),
            dma((Q, 2)),
            dma((2, x, Z * Y)),
            dma((2, x, Z * Y)),
            dma((2, y, Z * X)),
            dma((2, y, Z * X)),
            dma((2, Z)),
            dma((2, Z)),
        ]

    SCRATCH = 17

    def start(self, *a):
        cp = remote(*a)
        cp.start()
        self.started.append(cp)

    def got(self, ref, sem):
        remote(ref, ref, sem, sem, self.p.core_peer).wait_recv()

    def load(self, src):
        p = self.p
        for k in self.order:
            for j in p.others("x") + [p.x]:
                for i in range(p.Y):
                    for h in (0, 1):
                        q = p.chip(j, i, k)
                        cp = self.across(src.at[p.block(j, i, k, 1 - p.c), h], q, h)
                        cp.start()
                        self.started.append(cp)
                        self.keep(src.at[p.block(j, i, k, p.c), h], q, h).start()

    def keep(self, src, q, h):
        return pltpu.make_async_copy(src, self.acc.at[q, h], self.loc.at[q, h])

    def across(self, src, q, h):
        return remote(src, self.rc.at[q, h], self.cs.at[q, h], self.cr.at[q, h], self.p.core_peer)

    def ready(self, h, j, i, k):
        q = self.p.chip(j, i, k)
        if self.local:
            self.keep(self.acc.at[q, h], q, h).wait()
        self.got(self.rc.at[q, h], self.cr.at[q, h])
        return [self.rc.at[q, h]]

    def send_x(self, h, q, j, s):
        p = self.p
        o = lax.rem(j - p.x + p.X, p.X) - 1
        self.start(self.acc.at[q, h], self.rx[h].at[o, s], self.xs.at[h, o, s], self.xr.at[h, o, s],
                   p.dev(j, p.y, p.z, p.c))

    def send_y(self, h, q, i, s):
        p = self.p
        o = lax.rem(i - p.y + p.Y, p.Y) - 1
        self.start(self.acc.at[q, h], self.ry[h].at[o, s], self.ys.at[h, o, s], self.yr.at[h, o, s],
                   p.dev(p.x, i, p.z, p.c))

    def from_x(self, h, s):
        out = []
        for o in range(self.p.X - 1):
            self.got(self.rx[h].at[o, s], self.xr.at[h, o, s])
            out.append(self.rx[h].at[o, s])
        return out

    def from_y(self, h, s):
        out = []
        for o in range(self.p.Y - 1):
            self.got(self.ry[h].at[o, s], self.yr.at[h, o, s])
            out.append(self.ry[h].at[o, s])
        return out

    def last(self, n, h, q, extra):
        p = self.p
        k = self.order[n]
        if n < p.Z - 1:
            add(self.acc.at[q, h], extra)
            self.start(self.acc.at[q, h], self.rz.at[h, p.z], self.zs.at[h, k], self.zr.at[h, p.z],
                       p.dev(p.x, p.y, k, p.c))
        else:
            for a in p.others("z"):
                self.got(self.rz.at[h, a], self.zr.at[h, a])
                extra.append(self.rz.at[h, a])
            add(self.acc.at[q, h], extra, self.fin.at[h])

    def first(self, n, j):
        p = self.p
        k = self.order[n]
        for h, way in enumerate(self.like):
            if way == 0 and j is not p.x:
                for i in range(p.Y):
                    q = p.chip(j, i, k)
                    add(self.acc.at[q, h], self.ready(h, j, i, k))
                    self.send_x(h, q, j, k * p.Y + i)
            if way == 1:
                for i in p.others("y"):
                    q = p.chip(j, i, k)
                    add(self.acc.at[q, h], self.ready(h, j, i, k))
                    self.send_y(h, q, i, k * p.X + j)

    def rest(self, n):
        p = self.p
        X, Y, Z = p.X, p.Y, p.Z
        if 1 <= n <= Z:
            k = self.order[n - 1]
            for h, way in enumerate(self.like):
                if way == 0:
                    for i in p.others("y"):
                        q = p.chip(p.x, i, k)
                        add(self.acc.at[q, h], self.ready(h, p.x, i, k) + self.from_x(h, k * Y + i))
                        self.send_y(h, q, i, k)
                else:
                    for j in p.others("x"):
                        q = p.chip(j, p.y, k)
                        add(self.acc.at[q, h], self.ready(h, j, p.y, k) + self.from_y(h, k * X + j))
                        self.send_x(h, q, j, k)
        if n >= 2:
            k = self.order[n - 2]
            q = p.chip(p.x, p.y, k)
            for h, way in enumerate(self.like):
                extra = self.ready(h, p.x, p.y, k)
                if way == 0:
                    extra = extra + self.from_x(h, k * Y + p.y) + self.from_y(h, k)
                else:
                    extra = extra + self.from_y(h, k * X + p.x) + self.from_x(h, k)
                self.last(n - 2, h, q, extra)

    def step(self, n):
        if n < self.p.Z:
            for j in self.p.others("x") + [self.p.x]:
                self.first(n, j)
        self.rest(n)

    def sent(self):
        for cp in self.started:
            cp.wait_send()


def add(dst, srcs, f32_out=None):
    step = 16

    def one(n, _):
        r = pl.ds(pl.multiple_of(n * step, step), step)
        t = dst[r, :].astype(jnp.float32)
        for s in srcs:
            t = t + s[r, :].astype(jnp.float32)
        if f32_out is None:
            dst[r, :] = t.astype(dst.dtype)
        else:
            f32_out[r, :] = t
        return 0

    lax.fori_loop(0, dst.shape[0] // step, one, 0)


class PlaneScatter(Scatter):
    def __init__(self, p, acc, rc, ry, rz, fin, loc, cs, cr, ys, yr, zs, zr):
        self.p = p
        self.acc, self.rc, self.rz, self.fin, self.ry = acc, rc, rz, fin, (ry.at[0], ry.at[1])
        self.loc, self.cs, self.cr = loc, cs, cr
        self.ys, self.yr, self.zs, self.zr = ys, yr, zs, zr
        self.order = p.others("z") + [p.z]
        self.steps = p.Z + 1
        self.started = []
        self.local = True

    @staticmethod
    def scratch(U, B, rows, D, t):
        Y, Z = 2, B // 2
        dma = pltpu.SemaphoreType.DMA
        return [
            pltpu.VMEM((B, 2, rows, D), t),
            pltpu.VMEM((B, 2, rows, D), t),
            pltpu.VMEM((2, Y - 1, Z, rows, D), t),
            pltpu.VMEM((2, Z, rows, D), t),
            pltpu.VMEM((2, rows, D), jnp.float32),
            dma((B, 2)),
            dma((B, 2)),
            dma((B, 2)),
            dma((2, Y - 1, Z)),
            dma((2, Y - 1, Z)),
            dma((2, Z)),
            dma((2, Z)),
        ]

    SCRATCH = 12

    def load(self, src):
        p = self.p
        for k in self.order:
            for i in p.others("y") + [p.y]:
                for h in (0, 1):
                    q = p.chip(0, i, k)
                    cp = self.across(src.at[p.block(h, i, k, 1 - p.c)], q, h)
                    cp.start()
                    self.started.append(cp)
                    self.keep(src.at[p.block(h, i, k, p.c)], q, h).start()

    def step(self, n):
        p = self.p
        if n < p.Z:
            k = self.order[n]
            for i in p.others("y"):
                q = p.chip(0, i, k)
                for h in (0, 1):
                    add(self.acc.at[q, h], self.ready(h, 0, i, k))
                    self.send_y(h, q, i, k)
        if n >= 1:
            k = self.order[n - 1]
            q = p.chip(0, p.y, k)
            for h in (0, 1):
                self.last(n - 1, h, q, self.ready(h, 0, p.y, k) + self.from_y(h, k))


def keep_sum(fin, out, sem):
    cp = pltpu.make_async_copy(fin, out, sem)
    cp.start()
    cp.wait()


class Combine:
    def __init__(self, s, rows_in, hot_in, cols, rows_buf, hot_buf, stage, sems):
        self.s, self.p = s, s.p
        self.rows_in, self.hot_in, self.cols = rows_in, hot_in, cols
        self.rows_buf, self.hot_buf, self.stage, self.sems = rows_buf, hot_buf, stage, sems
        self.sent = []
        s.local = False

    def loads(self, j, k):
        g = j * self.p.Z + k
        RB = self.rows_buf.shape[1]
        rows = pl.ds(pl.multiple_of(g * RB, RB), RB)
        return (
            pltpu.make_async_copy(self.rows_in.at[:, rows, self.cols], self.rows_buf, self.sems.at[0]),
            pltpu.make_async_copy(self.hot_in.at[g], self.hot_buf, self.sems.at[1]),
        )

    def fetch(self, j, k):
        for cp in self.loads(j, k):
            cp.start()

    def make(self, j, k):
        p, s = self.p, self.s
        for cp in self.loads(j, k):
            cp.wait()
        for cp in self.sent:
            cp.wait_send()
        self.sent.clear()
        experts, RB, D = self.rows_buf.shape
        KB = self.hot_buf.shape[1]
        cut = min(D, 512)

        for n in range(0, D, cut):
            t = lax.dot_general(self.hot_buf[...], self.rows_buf[:, :, n:n + cut].reshape(experts * RB, cut),
                                (((0,), (0,)), ((), ())), preferred_element_type=jnp.float32)
            self.stage[:, :, :, n:n + cut] = t.astype(self.stage.dtype).reshape(self.stage.shape[:3] + (cut,))
        kept = []
        for i in range(p.Y):
            for h in (0, 1):
                q = p.chip(j, i, k)
                cp = s.across(self.stage.at[(1 - p.c) * p.Y + i, h], q, h)
                cp.start()
                self.sent.append(cp)
                cp = s.keep(self.stage.at[p.c * p.Y + i, h], q, h)
                cp.start()
                kept.append(cp)
        for cp in kept:
            cp.wait()

    def end(self):
        for cp in self.sent:
            cp.wait_send()


def pair_kernel(U, B, cols, a, b, hot, out_a, out_b, *scratch):
    p = Place(U, B)
    p.barrier("lines")
    k = Scatter.SCRATCH
    work = [Scatter(p, *scratch[k * i:k * (i + 1)]) for i in range(2)]
    feed = [Combine(s, m, hot, cols, *scratch[2 * k:2 * k + 4]) for s, m in zip(work, (a, b))]
    feed[1].sent = feed[0].sent
    xs = p.others("x") + [p.x]
    todo = [(f, j, z) for z in work[0].order for f in feed for j in xs]
    todo[0][0].fetch(*todo[0][1:])
    at = 0
    for n in range(work[0].steps):
        for s in work:
            if n < p.Z:
                for x in xs:
                    f, j, z = todo[at]
                    f.make(j, z)
                    at += 1
                    if at < len(todo):
                        todo[at][0].fetch(*todo[at][1:])
                    s.first(n, x)
            s.rest(n)
    feed[0].end()
    for s, out in zip(work, (out_a, out_b)):
        keep_sum(s.fin, out, scratch[-1].at[0])
        s.sent()


def scatter_pair(a, b, hot, rows, U, B, cid):
    F = U * B
    experts, _, D = a.shape
    G, n, KB = hot.shape
    RB = n // experts
    parts = max(1, F // 32)
    D = D // parts
    dma = pltpu.SemaphoreType.DMA

    def call(c):
        return pl.pallas_call(
            functools.partial(pair_kernel, U, B, pl.ds(c * D, D)),
            out_shape=[jax.ShapeDtypeStruct((2, rows, D), jnp.float32)] * 2,
            in_specs=any_specs(3),
            out_specs=any_specs(2),
            scratch_shapes=Scatter.scratch(U, B, rows, D, a.dtype) * 2 + [
                pltpu.VMEM((experts, RB, D), a.dtype), pltpu.VMEM((n, KB), hot.dtype),
                pltpu.VMEM((4, 2, rows, D), a.dtype), dma((2,)), dma((1,))],
            compiler_params=pltpu.CompilerParams(
                collective_id=cid, has_side_effects=True, vmem_limit_bytes=62 * 2**20),
        )(a, b, hot)

    got = [call(c) for c in range(parts)]
    return tuple(jnp.concatenate([g[i] for g in got], axis=-1) for i in range(2))


class PairExchange:
    def __init__(self, p, src, out, acc, rc, local, send, recv):
        self.p, self.src, self.out, self.acc, self.rc = p, src, out, acc, rc
        self.local, self.send, self.recv = local, send, recv

    @staticmethod
    def scratch(U, B, rows, w, t):
        dma = pltpu.SemaphoreType.DMA
        return [pltpu.VMEM((2 * B, rows, w), t), pltpu.VMEM((2 * B, rows, w), t),
                dma((1,)), dma((1 + 2 * B,)), dma((1 + 2 * B,))]

    SCRATCH = 5

    def across(self):
        p = self.p
        return remote(self.src.at[1 - p.x], self.rc, self.send.at[0], self.recv.at[0], p.x_peer)

    def own(self):
        return pltpu.make_async_copy(self.src.at[self.p.x], self.acc, self.local.at[0])

    def away(self, o):
        p = self.p
        r = lax.rem(p.r + o, 2 * p.B)
        return remote(self.acc.at[r], self.out.at[p.r], self.send.at[1 + r], self.recv.at[1 + p.r], p.plane_dev(r))

    def begin(self):
        self.across().start()
        self.own().start()

    def middle(self):
        p = self.p
        self.own().wait()
        self.across().wait_recv()

        @pl.loop(0, 2 * p.B)
        def _(r):
            t = self.acc[r].astype(jnp.float32) + self.rc[r].astype(jnp.float32)
            self.acc[r] = t.astype(self.acc.dtype)

        @pl.loop(1, 2 * p.B)
        def _(o):
            self.away(o).start()

        cp = pltpu.make_async_copy(self.acc.at[p.r], self.out.at[p.r], self.local.at[0])
        cp.start()
        cp.wait()

    def end(self):
        p = self.p
        self.across().wait_send()

        @pl.loop(1, 2 * p.B)
        def _(o):
            r = lax.rem(p.r + o, 2 * p.B)
            part = self.out.at[r]
            remote(part, part, self.send.at[0], self.recv.at[1 + r], p.x_peer).wait_recv()
            self.away(o).wait_send()


def finish_kernel(U, B, more, *refs):
    p = Place(U, B)
    p.barrier("plane")
    n = 4 if more else 3
    srcs, outs, scratch = refs[:n], refs[n:2 * n + 1], refs[2 * n + 1:]
    at = PlaneScatter.SCRATCH
    work = [PlaneScatter(p, *scratch[:at])]
    if more:
        work.append(Scatter(p, *scratch[at:at + Scatter.SCRATCH], like=(0, 0)))
        at += Scatter.SCRATCH
    ex = []
    for i in range(2):
        ex.append(PairExchange(p, srcs[i], outs[i], *scratch[at:at + PairExchange.SCRATCH]))
        at += PairExchange.SCRATCH
    stage, sems = scratch[at:]
    for s, src in zip(work, srcs[2:]):
        s.load(src)
    for e in ex:
        e.begin()
    work[0].step(0)
    for e in ex:
        e.middle()
    for s in work[1:]:
        s.step(0)
    for j in range(1, p.Z + 1):
        for s in work:
            s.step(j)
    fin = work[0].fin
    rows = fin.shape[1]

    def one(m, _):
        r = pl.ds(pl.multiple_of(m * 16, 16), 16)
        stage[r, :] = fin[1 - p.x, r, :].astype(stage.dtype)
        return 0

    lax.fori_loop(0, rows // 16, one, 0)
    away = remote(stage, outs[3], sems.at[0], sems.at[1], p.x_peer)
    away.start()
    keep_sum(fin.at[p.x], outs[2], sems.at[2])
    if more:
        work[1].step(p.Z + 1)
        keep_sum(work[1].fin, outs[4], sems.at[2])
    away.wait_recv()
    away.wait_send()
    for s in work:
        s.sent()
    for e in ex:
        e.end()


def finish(weights, small, hidden, out, U, B, cid):
    F = U * B
    parts = max(1, F // 32)
    D = hidden.shape[-1] // parts
    sds, f32 = jax.ShapeDtypeStruct, jnp.float32

    def call(h, o, cid):
        args = [m.reshape((2, 2 * B) + m.shape[1:]) for m in (weights, small)] + [h]
        shapes = [sds((2 * B,) + m.shape[1:], m.dtype) for m in (weights, small)]
        shapes += [sds(h.shape[1:], f32), sds(h.shape[1:], h.dtype)]
        scratch = PlaneScatter.scratch(U, B, h.shape[1], h.shape[2], h.dtype)
        if o is not None:
            args.append(o)
            shapes.append(sds(o.shape[1:], f32))
            scratch += Scatter.scratch(U, B, o.shape[2], o.shape[3], o.dtype, (0, 0))
        for m in (weights, small):
            scratch += PairExchange.scratch(U, B, m.shape[1], m.shape[2], m.dtype)
        return pl.pallas_call(
            functools.partial(finish_kernel, U, B, o is not None),
            out_shape=shapes,
            in_specs=any_specs(len(args)),
            out_specs=any_specs(len(shapes)),
            scratch_shapes=scratch + [pltpu.VMEM(h.shape[1:], h.dtype), pltpu.SemaphoreType.DMA((3,))],
            compiler_params=pltpu.CompilerParams(
                collective_id=cid, has_side_effects=True, vmem_limit_bytes=62 * 2**20),
        )(*args)

    if parts == 1:
        return call(hidden, out, cid)
    got = [call(hidden[..., n * D:(n + 1) * D], None, cid) for n in range(parts)]
    own, other = (jnp.concatenate([g[i] for g in got], axis=-1) for i in (2, 3))
    return got[0][0], got[0][1], own, other, scatter_by_permutes(out, U, B)


def scatter_by_permutes(v, U, B):
    X, Y, Z = U // 2, 2, B // 2
    f32 = jnp.float32
    u, b = lax.axis_index("ulysses"), lax.axis_index("blk")
    c, x, y, z = lax.rem(u, 2), lax.div(u, 2), lax.rem(b, Y), lax.div(b, Y)
    where = {"c": c, "x": x, "y": y, "z": z}
    size = {"c": 2, "x": X, "y": Y, "z": Z}

    def pairs(axis, by):
        out = []
        for f in range(U * B):
            at = {"x": f // B // 2, "c": f // B % 2, "z": f % B // Y, "y": f % Y}
            at[axis] = (at[axis] + by) % size[axis]
            out.append((f, (at["x"] * 2 + at["c"]) * B + at["z"] * Y + at["y"]))
        return out

    def fold(m, axis, dim):
        n = size[axis]
        total = lax.dynamic_index_in_dim(m, where[axis], dim, keepdims=False).astype(f32)
        for by in range(1, n):
            part = lax.dynamic_index_in_dim(m, lax.rem(where[axis] + by, n), dim, keepdims=False)
            total = total + lax.ppermute(part, ("ulysses", "blk"), pairs(axis, by)).astype(f32)
        return total

    rows, D = v.shape[-2:]
    m = fold(v.reshape(X, 2, Z, Y, 2, rows, D), "c", 1).astype(v.dtype)
    first = fold(m[:, :, :, 0], "x", 0).astype(v.dtype)
    first = fold(first, "y", 1).astype(v.dtype)
    second = fold(m[:, :, :, 1], "y", 2).astype(v.dtype)
    second = fold(second, "x", 0).astype(v.dtype)
    return fold(jnp.stack([first, second], axis=1), "z", 0)


def rms_norm(values, gains):
    return values * lax.rsqrt(jnp.mean(values * values, axis=-1, keepdims=True) + EPSILON) * gains


def dot(a, b, ca, cb):
    return lax.dot_general(a, b, (((ca,), (cb,)), ((), ())), preferred_element_type=jnp.float32)


def attend_kernel(U, B, bq, scale, q_ref, k_ref, vt_ref, out_ref, lse_ref, rows_ref, send, recv):
    p = Place(U, B)
    p.barrier("every")
    per = bq // rows_ref.shape[1]
    n = q_ref.shape[0] // bq

    def away(f):
        return remote(rows_ref.at[f], out_ref.at[p.me], send.at[f], recv.at[p.me], p.flat_dev(f))

    @pl.loop(0, n)
    def _(t):
        i = lax.rem(t + lax.div(p.me, per), n)
        rows = pl.ds(pl.multiple_of(i * bq, bq), bq)
        s = dot(k_ref[...], q_ref[rows, :], 1, 1) * scale
        top = jnp.max(s, axis=0, keepdims=True)
        e = jnp.exp(s - top)
        total = jnp.sum(e, axis=0, keepdims=True)
        o = dot(vt_ref[...], e.astype(jnp.bfloat16), 1, 0) / total
        lse_ref[:, rows] = top + jnp.log(total)
        rows_ref[pl.ds(i * per, per)] = o.T.astype(rows_ref.dtype).reshape((per,) + rows_ref.shape[1:])
        for d in range(per):
            f = i * per + d

            @pl.when(f != p.me)
            def _():
                away(f).start()

    cp = pltpu.make_async_copy(rows_ref.at[p.me], out_ref.at[p.me], recv.at[p.me])
    cp.start()
    cp.wait()

    @pl.loop(1, p.F)
    def _(o):
        f = lax.rem(p.me + o, p.F)
        remote(out_ref.at[f], out_ref.at[f], send.at[f], recv.at[f], p.flat_dev(f)).wait_recv()
        away(f).wait_send()


def attend(q, k, vt, positions, U, B, cid):
    n = q.shape[0]
    F = U * B
    bq = 256 if n <= 2048 else 128
    vmem = pl.BlockSpec(memory_space=pltpu.VMEM)
    dma = pltpu.SemaphoreType.DMA
    return pl.pallas_call(
        functools.partial(attend_kernel, U, B, bq, 1.0 / math.sqrt(HD)),
        in_specs=[vmem] * 3,
        out_specs=any_specs(1) + [vmem],
        out_shape=[jax.ShapeDtypeStruct((F, positions, HD), jnp.bfloat16), jax.ShapeDtypeStruct((1, n), jnp.float32)],
        scratch_shapes=[pltpu.VMEM((F, positions, HD), jnp.bfloat16), dma((F,)), dma((F,))],
        compiler_params=pltpu.CompilerParams(
            collective_id=cid, has_side_effects=True, vmem_limit_bytes=40 * 2**20),
    )(q, k, vt)


def attend_back_kernel(scale, q_ref, do_ref, lse_ref, k_ref, kt_ref, v_ref, dq_ref, dk_ref, dv_ref):
    @pl.when(pl.program_id(0) == 0)
    def _():
        dk_ref[...] = jnp.zeros_like(dk_ref)
        dv_ref[...] = jnp.zeros_like(dv_ref)

    p = jnp.exp(dot(k_ref[...], q_ref[...], 1, 1) * scale - lse_ref[...])
    dp = dot(v_ref[...], do_ref[...], 1, 1)
    delta = jnp.sum(p * dp, axis=0, keepdims=True)
    ds = (p * (dp - delta)).astype(jnp.bfloat16)
    dv_ref[...] += dot(p.astype(jnp.bfloat16), do_ref[...], 1, 0)
    dk_ref[...] += dot(ds, q_ref[...], 1, 0) * scale
    dq_ref[...] = (dot(kt_ref[...], ds, 1, 0) * scale).T


def attend_back(q, do, lse, k, kt, v):
    n = q.shape[0]
    bq = 256 if n <= 2048 else 128
    row = lambda i: (i, 0)
    whole = lambda i: (0, 0)
    f32 = jax.ShapeDtypeStruct((n, HD), jnp.float32)
    return pl.pallas_call(
        functools.partial(attend_back_kernel, 1.0 / math.sqrt(HD)),
        grid=(n // bq,),
        in_specs=[
            pl.BlockSpec((bq, HD), row),
            pl.BlockSpec((bq, HD), row),
            pl.BlockSpec((1, bq), lambda i: (0, i)),
            pl.BlockSpec((n, HD), whole),
            pl.BlockSpec((HD, n), whole),
            pl.BlockSpec((n, HD), whole),
        ],
        out_specs=[pl.BlockSpec((bq, HD), row), pl.BlockSpec((n, HD), whole), pl.BlockSpec((n, HD), whole)],
        out_shape=[f32, f32, f32],
        compiler_params=pltpu.CompilerParams(vmem_limit_bytes=58 * 2**20),
    )(q, do, lse, k, kt, v)


def turn(v, cosine, sine):
    return v * cosine + pltpu.roll(v, HD // 2, 1) * sine


def project_kernel(tok_ref, gain_ref, w_ref, qk_ref, cos_ref, sin_ref,
                   q_ref, k_ref, v_ref, kt_ref, vt_ref, rq_ref, rk_ref):
    bf16 = jnp.bfloat16
    raw = dot(rms_norm(tok_ref[...].astype(jnp.float32), gain_ref[...]).astype(bf16), w_ref[...], 1, 0)
    rq, rk, v = raw[:, :HD], raw[:, HD:2 * HD], raw[:, 2 * HD:].astype(bf16)
    rq_ref[...] = rq
    rk_ref[...] = rk
    q_ref[...] = turn(rms_norm(rq, qk_ref[0:1]), cos_ref[...], sin_ref[...]).astype(bf16)
    k = turn(rms_norm(rk, qk_ref[1:2]), cos_ref[...], sin_ref[...])
    k_ref[...] = k.astype(bf16)
    kt_ref[...] = k.T.astype(bf16)
    v_ref[...] = v
    vt_ref[...] = raw[:, 2 * HD:].T.astype(bf16)


def project(tok, gain, w, qk, cosine, sine):
    n, D = tok.shape
    bm = 256
    row, whole = (lambda i: (i, 0)), (lambda i: (0, 0))
    head, across = pl.BlockSpec((bm, HD), row), pl.BlockSpec((HD, bm), lambda i: (0, i))
    sds = jax.ShapeDtypeStruct
    f32, bf16 = jnp.float32, jnp.bfloat16
    return pl.pallas_call(
        project_kernel,
        grid=(n // bm,),
        in_specs=[
            pl.BlockSpec((bm, D), row), pl.BlockSpec((1, D), whole), pl.BlockSpec((D, 3 * HD), whole),
            pl.BlockSpec((2, HD), whole), head, head,
        ],
        out_specs=[head, head, head, across, across, head, head],
        out_shape=[sds((n, HD), bf16)] * 3 + [sds((HD, n), bf16)] * 2 + [sds((n, HD), f32)] * 2,
        compiler_params=pltpu.CompilerParams(vmem_limit_bytes=58 * 2**20),
    )(tok, gain, w, qk, cosine, sine)


def head_back_kernel(dq_ref, dk_ref, dv_ref, rq_ref, rk_ref, cos_ref, sin_ref, qk_ref, tok_ref, gain_ref, w_ref,
                     part_ref, dwout_ref, dg_ref, da_ref, dw_ref):
    f32, bf16 = jnp.float32, jnp.bfloat16

    @pl.when(pl.program_id(0) == 0)
    def _():
        dw_ref[...] = jnp.zeros_like(dw_ref)
        dg_ref[...] = jnp.zeros_like(dg_ref)
        da_ref[...] = jnp.zeros_like(da_ref)

    grads = []
    for n, (g_ref, raw_ref) in enumerate(((dq_ref, rq_ref), (dk_ref, rk_ref))):
        w = turn(g_ref[...].astype(bf16).astype(f32), cos_ref[...], -sin_ref[...])
        u = raw_ref[...]
        r = lax.rsqrt(jnp.mean(u * u, axis=-1, keepdims=True) + EPSILON)
        norm = u * r
        dg_ref[n:n + 1, :] += jnp.sum(w * norm, axis=0, keepdims=True)
        m = w * qk_ref[n:n + 1]
        grads.append((r * (m - norm * jnp.mean(m * norm, axis=-1, keepdims=True))).astype(bf16))
    grads.append(dv_ref[...].astype(bf16))
    grad = jnp.concatenate(grads, axis=1)
    tok = tok_ref[...].astype(f32)
    norm = tok * lax.rsqrt(jnp.mean(tok * tok, axis=-1, keepdims=True) + EPSILON)
    hidden = (norm * gain_ref[...]).astype(bf16)
    D = tok.shape[1]
    cut = min(D, 512)
    for n in range(0, D, cut):
        part = dot(grad, w_ref[n:n + cut, :], 1, 1)
        part_ref[:, n:n + cut] = part.astype(bf16)
        da_ref[0:1, n:n + cut] += jnp.sum(part * norm[:, n:n + cut], axis=0, keepdims=True)
        dw_ref[n:n + cut, :] += dot(hidden[:, n:n + cut], grad, 0, 0)

    @pl.when(pl.program_id(0) == pl.num_programs(0) - 1)
    def _():
        dwout_ref[...] = dw_ref[...].astype(bf16)


def head_back(dq, dk, dv, rq, rk, cosine, sine, qk, tok, gain, w):
    n, D = tok.shape
    bm = 512
    row, whole = (lambda i: (i, 0)), (lambda i: (0, 0))
    head = pl.BlockSpec((bm, HD), row)
    sds = jax.ShapeDtypeStruct
    return pl.pallas_call(
        head_back_kernel,
        grid=(n // bm,),
        in_specs=[head] * 7 + [
            pl.BlockSpec((2, HD), whole), pl.BlockSpec((bm, D), row), pl.BlockSpec((1, D), whole),
            pl.BlockSpec((D, 3 * HD), whole)],
        out_specs=[
            pl.BlockSpec((bm, D), row), pl.BlockSpec((D, 3 * HD), whole), pl.BlockSpec((8, HD), whole),
            pl.BlockSpec((8, D), whole)],
        out_shape=[sds((n, D), jnp.bfloat16), sds((D, 3 * HD), jnp.bfloat16), sds((8, HD), jnp.float32),
                   sds((8, D), jnp.float32)],
        scratch_shapes=[pltpu.VMEM((D, 3 * HD), jnp.float32)],
        compiler_params=pltpu.CompilerParams(vmem_limit_bytes=58 * 2**20),
    )(dq, dk, dv, rq, rk, cosine, sine, qk, tok, gain, w)


def dispatch_kernel(hot_ref, rg_ref, norm_ref, cot_ref, x_ref, pg_ref):
    bf16 = jnp.bfloat16
    experts, RB, D = x_ref.shape
    hot = hot_ref[0]
    KB = hot.shape[1]
    weight = rg_ref[:, :, 0:1].reshape(experts * RB, 1)
    cut = min(D, 512)
    norm = norm_ref[...].reshape(KB, D)
    cot = cot_ref[...].reshape(KB, D)
    for n in range(0, D, cut):
        x = dot(hot, norm[:, n:n + cut], 1, 0).astype(bf16)
        x_ref[:, :, n:n + cut] = x.reshape(experts, RB, cut)
        g = (dot(hot, cot[:, n:n + cut], 1, 0) * weight).astype(bf16)
        pg_ref[:, :, n:n + cut] = g.reshape(experts, RB, cut)


def group_spec(shape, Z):
    X, two, _, Y, T, D = shape
    return pl.BlockSpec((1, two, 1, Y, T, D), lambda g: (g // Z, 0, g % Z, 0, 0, 0))


def dispatch(hot, rg, normed, cot):
    G, rows, KB = hot.shape
    experts, D, Z = rg.shape[0], normed.shape[-1], normed.shape[2]
    RB = rows // experts
    out = pl.BlockSpec((experts, RB, D), lambda g: (0, g, 0))
    return pl.pallas_call(
        dispatch_kernel,
        grid=(G,),
        in_specs=[pl.BlockSpec((1, rows, KB), lambda g: (g, 0, 0)), pl.BlockSpec((experts, RB, 128), lambda g: (0, g, 0)),
                  group_spec(normed.shape, Z), group_spec(cot.shape, Z)],
        out_specs=[out, out],
        out_shape=[jax.ShapeDtypeStruct((experts, G * RB, D), jnp.bfloat16)] * 2,
        compiler_params=pltpu.CompilerParams(vmem_limit_bytes=58 * 2**20),
    )(hot, rg, normed, cot)


def expert_kernel(x_ref, pg_ref, rg_ref, wg_ref, wu_ref, wd_ref, y_ref, dx_ref, dwg_ref, dwu_ref, dwd_ref):
    bf16 = jnp.bfloat16
    x, pg = x_ref[0], pg_ref[0]
    D = x.shape[1]
    gate, up = dot(x, wg_ref[0], 1, 0), dot(x, wu_ref[0], 1, 0)
    sigma = jax.nn.sigmoid(gate)
    silu = gate * sigma
    inner = (silu * up).astype(bf16)
    back = dot(pg, wd_ref[0], 1, 1)
    dgate = (back * up * sigma * (1.0 + gate * (1.0 - sigma))).astype(bf16)
    dup = (back * silu).astype(bf16)
    cut = min(D, 512)
    weight = rg_ref[0, :, 0:1]
    first = pl.program_id(1) == 0

    def gather_in(ref, ix, value):
        if pl.num_programs(1) == 1:
            ref[ix] = value
        else:
            ref[ix] = value + jnp.where(first, 0.0, ref[ix])

    for n in range(0, D, cut):
        c = slice(n, n + cut)
        y_ref[0, :, c] = (dot(inner, wd_ref[0, :, c], 1, 0) * weight).astype(bf16)
        dx_ref[0, :, c] = (dot(dgate, wg_ref[0, c, :], 1, 1) + dot(dup, wu_ref[0, c, :], 1, 1)).astype(bf16)
        gather_in(dwg_ref, (0, c, slice(None)), dot(x_ref[0, :, c], dgate, 0, 0))
        gather_in(dwu_ref, (0, c, slice(None)), dot(x_ref[0, :, c], dup, 0, 0))
        gather_in(dwd_ref, (0, slice(None), c), dot(inner, pg_ref[0, :, c], 0, 0))


def expert_layer(x, pg, rg, wg, wu, wd):
    rows = x.shape[1]
    step = 640 if rows % 640 == 0 else rows
    some = lambda a: pl.BlockSpec((1, step) + a.shape[2:], lambda e, i: (e, i, 0))
    whole = lambda a: pl.BlockSpec((1,) + a.shape[1:], lambda e, i: (e, 0, 0))
    sds = jax.ShapeDtypeStruct
    return pl.pallas_call(
        expert_kernel,
        grid=(x.shape[0], rows // step),
        in_specs=[some(a) for a in (x, pg, rg)] + [whole(a) for a in (wg, wu, wd)],
        out_specs=[some(a) for a in (x, x)] + [whole(a) for a in (wg, wu, wd)],
        out_shape=[sds(x.shape, x.dtype)] * 2 + [sds(a.shape, jnp.float32) for a in (wg, wu, wd)],
        compiler_params=pltpu.CompilerParams(vmem_limit_bytes=60 * 2**20),
    )(x, pg, rg, wg, wu, wd)


def close_kernel(x_ref, w_ref, own_ref, other_ref, back_ref, tok_ref, gain_ref, q_ref, k_ref, v_ref, in_ref):
    f32 = jnp.float32
    for h in range(w_ref.shape[0]):
        for n, ref in enumerate((q_ref, k_ref, v_ref)):
            ref[:, h * HD:(h + 1) * HD] = w_ref[h, :, n * HD:(n + 1) * HD].astype(f32)
    here = x_ref[0]
    for s in (0, 1):
        grad = jnp.where(here == s, own_ref[...], other_ref[...].astype(f32))
        tok = tok_ref[s].astype(f32)
        inv = lax.rsqrt(jnp.mean(tok * tok, axis=-1, keepdims=True) + EPSILON)
        norm = tok * inv
        m = grad * gain_ref[...]
        in_ref[s] = back_ref[s] + inv * (m - norm * jnp.mean(m * norm, axis=-1, keepdims=True))


def close(here, weight_grad, own, other, back, tok, gain):
    heads, W, _ = weight_grad.shape
    vmem = pl.BlockSpec(memory_space=pltpu.VMEM)
    sds = jax.ShapeDtypeStruct
    return pl.pallas_call(
        close_kernel,
        in_specs=[pl.BlockSpec(memory_space=pltpu.SMEM)] + [vmem] * 6,
        out_specs=[vmem] * 4,
        out_shape=[sds((W, heads * HD), jnp.float32)] * 3 + [sds(tok.shape, jnp.float32)],
        compiler_params=pltpu.CompilerParams(vmem_limit_bytes=32 * 2**20),
    )(here, weight_grad, own, other, back, tok, gain)


def body(tokens, w_query, w_key, w_value, w_out, attn_gain, ffn_gain, qk_gain,
         expert_gate, expert_up, expert_down, routes, gates, order, cotangent):
    f32, bf16 = jnp.float32, jnp.bfloat16
    positions, seqs, D = tokens.shape
    U, B = lax.axis_size("ulysses"), lax.axis_size("blk")
    F = U * B
    u, b = lax.axis_index("ulysses"), lax.axis_index("blk")
    H = w_query.shape[1] // HD
    W = w_query.shape[0]
    L = F * positions
    T = seqs * positions
    top_count = routes.shape[-1]
    local_experts = expert_gate.shape[0]
    E = local_experts * B
    R = 2 * B // H
    x_here = u // 2
    first_copy = lax.rem((u % 2) * B + b, R) == 0

    tok = tokens.transpose(1, 0, 2)
    cot = cotangent.transpose(1, 0, 2)
    rows_f = tok.reshape(T, D).astype(f32)

    expert_of = routes.transpose(1, 0, 2).reshape(-1)
    prio = order.reshape(positions, seqs, top_count).transpose(1, 0, 2).reshape(-1)
    same = expert_of[:, None] == expert_of[None, :]
    ranks = jnp.sum((same & (prio[None, :] < prio[:, None])).astype(jnp.int32), axis=1)
    slot = jnp.where(ranks < CAP, expert_of * CAP + ranks, -1).astype(f32)
    pairs = slot.shape[0]

    nq = qk_gain.shape[1]
    small = jnp.concatenate(
        [slot, gates.transpose(1, 0, 2).reshape(-1)]
        + [g.astype(f32) for g in (attn_gain, ffn_gain, qk_gain[0], qk_gain[1])])
    small = jnp.pad(small, (0, -small.shape[0] % 1024)).reshape(-1, 128)
    heads_w = jnp.stack([w_query, w_key, w_value]).reshape(3, W, H, HD).transpose(2, 1, 0, 3).reshape(H, W, 3 * HD)
    if R > 1:
        heads_w = heads_w[np.arange(2 * B) // R]
    seq_tok, table, head_w = front(tok, small, heads_w, U, B, 1)
    seq_tok, head_w = seq_tok.reshape(L, D), head_w.reshape(D, 3 * HD)
    out_w = lax.all_gather(w_out, AXES, axis=0, tiled=True)
    cot_all = lax.all_gather(cot, AXES, axis=0)
    table = table.reshape(F, -1)
    cut = 2 * pairs
    attn_g = table[:, cut:cut + W].reshape(1, D)
    ffn_g = table[:, cut + W:cut + 2 * W].reshape(1, D)
    cut = cut + 2 * W
    qk_g = jnp.stack([table[:, cut:cut + nq].reshape(-1), table[:, cut + nq:cut + 2 * nq].reshape(-1)])

    groups = (U // 2, 2, B // 2, 2)
    GB = 4
    G, KB = F // GB, GB * T
    RB = -(-GB * CAP // 16) * 16
    slot_all = table[:, :pairs].astype(jnp.int32).reshape(F, T, top_count)
    gate_all = table[:, pairs:2 * pairs].reshape(F, T, top_count)
    place = ((np.arange(F) // B % 2) * 2 + np.arange(F) % 2).astype(np.int32)
    base = (b * local_experts + jnp.arange(local_experts, dtype=jnp.int32)) * CAP
    off = slot_all[:, :, :, None] - base
    mine = (off >= 0) & (off < CAP)
    val = jnp.sum(jnp.where(mine, off + 1, 0), axis=2)
    val = jnp.where(val > 0, val - 1 + jnp.asarray(place)[:, None, None] * CAP, -1)
    gate_of = jnp.sum(jnp.where(mine, gate_all[:, :, :, None], 0.0), axis=2)

    def by_group(m):
        return m.reshape(groups + (T, local_experts)).transpose(0, 2, 5, 1, 3, 4).reshape(G, local_experts, KB)

    val, gate_of = by_group(val), by_group(gate_of)

    inverse = (ROPE_BASE ** (-2.0 * np.arange(HD // 2) / HD)).astype(np.float32)
    angles = np.arange(L).astype(np.float32)[:, None] * inverse[None, :]
    cosine = jnp.asarray(np.concatenate([np.cos(angles)] * 2, axis=1).astype(np.float32))
    sine = jnp.asarray(np.concatenate([-np.sin(angles), np.sin(angles)], axis=1).astype(np.float32))
    q, k, v, kt, vt, raw_q, raw_k = project(seq_tok, attn_g, head_w, qk_g, cosine, sine)
    att_rows, lse = attend(q, k, vt, positions, U, B, 5)

    def from_heads(m):
        m = m.reshape(2, 2 * B, positions, HD).transpose(0, 2, 1, 3)
        return m.reshape(2, positions, H, R, HD)[:, :, :, 0].reshape(T, H * HD)

    attended = from_heads(att_rows)
    residual = rows_f + jnp.dot(attended, out_w, preferred_element_type=f32)
    normed_full, ffn_back = jax.vjp(rms_norm, residual, ffn_g)
    normed = normed_full.astype(bf16).reshape(2, positions, D)

    normed_all, hot, row_gate = gather_blocks(normed, val, gate_of, RB, U, B, 2)
    shape = groups + (T, D)
    x, pair_grad = dispatch(hot, row_gate, normed_all.reshape(shape), cot_all.reshape(shape))
    y, dx, gate_grad, up_grad, down_grad = expert_layer(x, pair_grad, row_gate, expert_gate, expert_up, expert_down)
    normed_grad, mixed_sum = scatter_pair(dx, y, hot, positions, U, B, 3)
    mixed = (residual + mixed_sum.reshape(T, D)).reshape(2, positions, D).transpose(1, 0, 2).astype(bf16)
    normed_grad = normed_grad.reshape(T, D)

    residual_norm_grad, ffn_gain_part = ffn_back(normed_grad)
    residual_grad = cot.reshape(T, D).astype(f32) + residual_norm_grad
    attn_out_grad = residual_grad.astype(bf16)
    att_grad = dot(attn_out_grad, out_w, 1, 1).astype(bf16)
    att_grad = jnp.repeat(att_grad.reshape(2, positions, H, HD).transpose(0, 2, 1, 3), R, axis=1)
    att_grad = att_grad.reshape(F, positions, HD)
    do = exchange(att_grad, U, B, 6).reshape(L, HD)
    out_part = dot(attended, attn_out_grad, 0, 0).astype(bf16)
    out_part = out_part.reshape(F, 2, W // 2, D)
    dq, dk, dv = attend_back(q, do, lse, k, kt, v)
    if R > 1:
        dq, dk, dv = (jnp.where(first_copy, m, 0.0) for m in (dq, dk, dv))
    hidden_part, weight_part, qk_part, attn_gain_part = head_back(
        dq, dk, dv, raw_q, raw_k, cosine, sine, qk_g, seq_tok, attn_g, head_w)
    weight_part = weight_part.reshape(F, W, 3 * HD)
    small = jnp.concatenate(
        [attn_gain_part[0].reshape(F, W), ffn_gain_part.reshape(F, W),
         qk_part[0].reshape(F, nq), qk_part[1].reshape(F, nq)], axis=1)
    small = jnp.pad(small, ((0, 0), (0, -small.shape[1] % 1024))).reshape(F, -1, 128)
    weight_grad, small, own, other, out_grad = finish(
        weight_part, small, hidden_part.reshape(F, positions, D), out_part, U, B, 4)
    small = jnp.sum(small, axis=0).reshape(-1)
    if R > 1:
        weight_grad = weight_grad.reshape(H, R, W, 3 * HD).astype(f32).sum(axis=1)
    query_grad, key_grad, value_grad, input_grad = close(
        x_here.reshape(1), weight_grad, own, other, residual_grad.reshape(2, positions, D), tok, attn_g)
    input_grad = input_grad.transpose(1, 0, 2)
    out_grad = out_grad.reshape(W, D)
    return (
        mixed, input_grad, query_grad, key_grad, value_grad, out_grad,
        small[:W], small[W:2 * W], small[2 * W:2 * W + 2 * nq].reshape(2, nq),
        gate_grad, up_grad, down_grad,
    )


def solution(mesh):
    rows = P(AXES, None, None)
    flat = P(AXES, None)
    by_expert = (P("blk", None, "ulysses"), P("blk", None, "ulysses"), P("blk", "ulysses", None))
    in_specs = (rows, flat, flat, flat, flat, P(AXES), P(AXES), P(None, AXES)) + by_expert + (rows, rows, flat, rows)
    out_specs = (rows, rows, flat, flat, flat, flat, P(AXES), P(AXES), P(None, AXES)) + by_expert
    return jax.shard_map(body, mesh=mesh, in_specs=in_specs, out_specs=out_specs, check_vma=False)
```

```python
import functools
import math

import jax
import jax.numpy as jnp
import numpy as np
from jax import lax
from jax.experimental import pallas as pl
from jax.experimental.pallas import tpu as pltpu
from jax.sharding import PartitionSpec as P

HD = 128
CAP = 18
EPSILON = 1e-06
ROPE_BASE = 10000.0
AXES = ("ulysses", "blk")
MESH = pl.DeviceIdType.MESH


class Place:
    def __init__(self, U, B):
        self.U, self.B = U, B
        self.X, self.Y = U // 2, 2
        self.Z = B // self.Y
        self.Q, self.F = self.X * B, U * B
        u, b = lax.axis_index("ulysses"), lax.axis_index("blk")
        self.c, self.x = lax.rem(u, 2), lax.div(u, 2)
        self.y, self.z = lax.rem(b, self.Y), lax.div(b, self.Y)
        self.r = self.c * B + b
        self.me = u * B + b
        self.core_peer = self.dev(self.x, self.y, self.z, 1 - self.c)
        self.x_peer = self.dev(1 - self.x, self.y, self.z, self.c)

    def dev(self, x, y, z, c):
        return (x * 2 + c, z * self.Y + y)

    def block(self, x, y, z, c):
        return (x * 2 + c) * self.B + z * self.Y + y

    def chip(self, x, y, z):
        return x * self.B + z * self.Y + y

    def at(self, r, x):
        return x * 2 * self.B + r

    def plane_dev(self, r):
        return (self.x * 2 + lax.div(r, self.B), lax.rem(r, self.B))

    def flat_dev(self, f):
        return (lax.div(f, self.B), lax.rem(f, self.B))

    def others(self, axis):
        n = {"x": self.X, "y": self.Y, "z": self.Z}[axis]
        i = {"x": self.x, "y": self.y, "z": self.z}[axis]
        return [lax.rem(i + o, n) for o in range(1, n)]

    def far_first(self):
        table = [sorted((k for k in range(self.Z) if k != z), key=lambda k: (-abs(k - z), -k)) for z in range(self.Z)]
        out = []
        for n in range(self.Z - 1):
            k = 0
            for z in range(self.Z):
                k = k + jnp.where(self.z == z, table[z][n], 0)
            out.append(k)
        return out + [self.z]

    def barrier(self, reach):
        sem = pltpu.get_barrier_semaphore()

        def greet(d):
            pl.semaphore_signal(sem, inc=1, device_id=d, device_id_type=MESH)

        if reach == "every":
            @pl.loop(1, self.F)
            def _(o):
                greet(self.flat_dev(lax.rem(self.me + o, self.F)))

            pl.semaphore_wait(sem, self.F - 1)
            return
        if reach == "plane":
            greet(self.x_peer)

            @pl.loop(1, 2 * self.B)
            def _(o):
                greet(self.plane_dev(lax.rem(self.r + o, 2 * self.B)))

            pl.semaphore_wait(sem, 2 * self.B)
            return
        greet(self.core_peer)
        for k in self.others("x"):
            greet(self.dev(k, self.y, self.z, self.c))
        for k in self.others("y"):
            greet(self.dev(self.x, k, self.z, self.c))
        count = self.X + self.Y - 1
        if reach == "chain":
            below, above = self.z > 0, self.z < self.Z - 1

            @pl.when(below)
            def _():
                greet(self.dev(self.x, self.y, self.z - 1, self.c))

            @pl.when(above)
            def _():
                greet(self.dev(self.x, self.y, self.z + 1, self.c))

            count = count + jnp.where(below, 1, 0) + jnp.where(above, 1, 0)
        else:
            for k in self.others("z"):
                greet(self.dev(self.x, self.y, k, self.c))
            count += self.Z - 1
        pl.semaphore_wait(sem, count)


def remote(src, dst, send, recv, dev):
    return pltpu.make_async_remote_copy(
        src_ref=src, dst_ref=dst, send_sem=send, recv_sem=recv, device_id=dev, device_id_type=MESH)


class Gather:
    def __init__(self, p, src, out, send_sem, recv_sem, local_sem, like=(0, 1)):
        self.p, self.src, self.out, self.like = p, src, out, like
        self.send_sem, self.recv_sem, self.local_sem = send_sem, recv_sem, local_sem
        self.steps = p.Z + 2
        self.started = []
        self.always = p.z >= 0

    @staticmethod
    def semaphores(U, B):
        dma = pltpu.SemaphoreType.DMA
        return [dma((4 + U // 2, 2, U * B)), dma((2, U * B)), dma((1,))]

    def where(self, half, x, y, z):
        f = self.p.block(x, y, z, self.p.c)
        return self.out.at[f, half], (half, f)

    def send(self, cond, src_ref, dst_ref, ix, way, dev):
        cp = remote(src_ref, dst_ref, self.send_sem.at[(way,) + ix], self.recv_sem.at[ix], dev)

        @pl.when(cond)
        def _():
            cp.start()

        self.started.append((cond, cp))

    def wait(self, ref, ix):
        remote(ref, ref, self.send_sem.at[(0,) + ix], self.recv_sem.at[ix], self.p.core_peer).wait_recv()

    def along(self, cond, half, x, y, z, axes):
        p = self.p
        ref, ix = self.where(half, x, y, z)
        for ax in axes:
            if ax == "core":
                self.send(cond, ref, ref, ix, 0, p.core_peer)
            elif ax == "up":
                self.send(cond & (p.z < p.Z - 1), ref, ref, ix, 1, p.dev(p.x, p.y, p.z + 1, p.c))
            elif ax == "down":
                self.send(cond & (p.z > 0), ref, ref, ix, 2, p.dev(p.x, p.y, p.z - 1, p.c))
            elif ax == "y":
                for i, k in enumerate(p.others("y")):
                    self.send(cond, ref, ref, ix, 3 + i, p.dev(p.x, k, p.z, p.c))
            else:
                for i, k in enumerate(p.others("x")):
                    self.send(cond, ref, ref, ix, 2 + p.Y + i, p.dev(k, p.y, p.z, p.c))

    def zs(self, step):
        p = self.p
        if step == 0:
            return [(self.always, p.z, ())]
        return [(p.z - step >= 0, p.z - step, ("up",)), (p.z + step < p.Z, p.z + step, ("down",))]

    def arrive(self, cond, half, x, y, z, axes):
        ref, ix = self.where(half, x, y, z)

        @pl.when(cond)
        def _():
            self.wait(ref, ix)

        self.along(cond, half, x, y, z, axes)

    def step(self, n):
        p = self.p
        if n == 0:
            cp = pltpu.make_async_copy(self.src, self.out.at[p.me], self.local_sem.at[0])
            cp.start()
            cp.wait()
            for half in (0, 1):
                self.along(self.always, half, p.x, p.y, p.z, ("up", "down", "y", "x"))
            for half in (0, 1):
                self.along(self.always, half, p.x, p.y, p.z, ("core",))
            return
        if n < p.Z:
            for half in (0, 1):
                for cond, k, on in self.zs(n):
                    self.arrive(cond, half, p.x, p.y, k, on + ("y", "x", "core"))
        if n <= p.Z:
            for cond, k, _ in self.zs(n - 1):
                for half, way in enumerate(self.like):
                    if way == 0:
                        for i in p.others("y"):
                            self.arrive(cond, half, p.x, i, k, ("x", "core"))
                    else:
                        for j in p.others("x"):
                            self.arrive(cond, half, j, p.y, k, ("y", "core"))
        if n >= 2:
            for cond, k, _ in self.zs(n - 2):
                for half, way in enumerate(self.like):
                    if way == 0:
                        for j in p.others("x"):
                            self.arrive(cond, half, j, p.y, k, ("core",))
                    else:
                        for i in p.others("y"):
                            self.arrive(cond, half, p.x, i, k, ("core",))
                for half in (0, 1):
                    for j in p.others("x"):
                        for i in p.others("y"):
                            self.arrive(cond, half, j, i, k, ("core",))

    def end(self):
        p = self.p
        for k in range(p.Z):
            for j in range(p.X):
                for i in range(p.Y):
                    f = p.block(j, i, k, 1 - p.c)
                    for half in (0, 1):
                        self.wait(self.out.at[f, half], (half, f))
        for cond, cp in self.started:
            @pl.when(cond)
            def _(cp=cp):
                cp.wait_send()


class PlaneGather(Gather):
    def __init__(self, *a):
        super().__init__(*a)
        self.steps = self.p.Z + 1

    @staticmethod
    def semaphores(U, B):
        dma = pltpu.SemaphoreType.DMA
        return [dma((5, 1, U * B)), dma((1, U * B)), dma((1,))]

    def where(self, half, x, y, z):
        f = self.p.block(half, y, z, self.p.c)
        return self.out.at[f], (0, f)

    def step(self, n):
        p = self.p
        if n == 0:
            cp = pltpu.make_async_copy(self.src.at[p.x], self.out.at[p.me], self.local_sem.at[0])
            cp.start()
            self.send(self.always, self.src.at[1 - p.x], self.out.at[p.me], (0, p.me), 4, p.x_peer)
            cp.wait()
            self.along(self.always, p.x, p.x, p.y, p.z, ("up", "down", "y", "core"))
            self.arrive(self.always, 1 - p.x, p.x, p.y, p.z, ("up", "down", "y", "core"))
            return
        if n < p.Z:
            for half in (0, 1):
                for cond, k, on in self.zs(n):
                    self.arrive(cond, half, p.x, p.y, k, on + ("y", "core"))
        for half in (0, 1):
            for cond, k, _ in self.zs(n - 1):
                for i in p.others("y"):
                    self.arrive(cond, half, p.x, i, k, ("core",))

    def end(self):
        p = self.p
        for k in range(p.Z):
            for i in range(p.Y):
                for half in (0, 1):
                    f = p.block(half, i, k, 1 - p.c)
                    self.wait(self.out.at[f], (0, f))
        for cond, cp in self.started:
            @pl.when(cond)
            def _(cp=cp):
                cp.wait_send()


class Spread:
    def __init__(self, p, parts, out, send_sem, recv_sem, over_sem):
        self.p, self.parts, self.out = p, parts, out
        self.send_sem, self.recv_sem, self.over_sem = send_sem, recv_sem, over_sem

    @staticmethod
    def semaphores(U, B, n):
        dma = pltpu.SemaphoreType.DMA
        return [dma((n, 2 * B)), dma((n, 2 * B)), dma((2, 2 * B))]

    def out_to(self, o):
        p = self.p
        r = lax.rem(p.r + o, 2 * p.B)
        return [remote(src, self.out.at[(p.me,) + at], self.send_sem.at[n, r], self.recv_sem.at[n, p.r], p.plane_dev(r))
                for n, (src, at) in enumerate(self.parts(r))]

    def across(self, r):
        f = self.p.at(r, self.p.x)
        return remote(self.out.at[f], self.out.at[f], self.over_sem.at[0, r], self.over_sem.at[1, r], self.p.x_peer)

    def begin(self):
        p = self.p

        @pl.loop(1, 2 * p.B)
        def _(o):
            for cp in self.out_to(o):
                cp.start()

        mine = [pltpu.make_async_copy(src, self.out.at[(p.me,) + at], self.send_sem.at[n, p.r])
                for n, (src, at) in enumerate(self.parts(p.r))]
        for cp in mine:
            cp.start()
        for cp in mine:
            cp.wait()
        self.across(p.r).start()

    def middle(self):
        p = self.p

        @pl.loop(1, 2 * p.B)
        def _(o):
            r = lax.rem(p.r + o, 2 * p.B)
            for n, (_, at) in enumerate(self.parts(r)):
                ref = self.out.at[(p.at(r, p.x),) + at]
                remote(ref, ref, self.send_sem.at[n, 0], self.recv_sem.at[n, r], p.x_peer).wait_recv()
            self.across(r).start()

    def end(self):
        p = self.p

        @pl.loop(0, 2 * p.B)
        def _(r):
            f = p.at(r, 1 - p.x)
            remote(self.out.at[f], self.out.at[f], self.over_sem.at[0, 0], self.over_sem.at[1, r], p.x_peer).wait_recv()
            self.across(r).wait_send()

        @pl.loop(1, 2 * p.B)
        def _(o):
            for cp in self.out_to(o):
                cp.wait_send()


def any_specs(n):
    return [pl.BlockSpec(memory_space=pl.ANY)] * n


def gather_kernel(U, B, experts, RB, src, val, gate, out, hot_out, rg_out, send, recv, local, hot, rg, store):
    p = Place(U, B)
    p.barrier("chain")
    g = Gather(p, src, out, send, recv, local)
    G, _, KB = val.shape
    per = -(-G // (g.steps - 2))
    at = lax.broadcasted_iota(jnp.int32, (RB, KB), 0)
    saves = [pltpu.make_async_copy(hot, hot_out, store.at[0]), pltpu.make_async_copy(rg, rg_out, store.at[1])]
    for n in range(g.steps):
        g.step(n)

        @pl.loop(min(n * per, G), min((n + 1) * per, G))
        def _(m):
            for e in range(experts):
                hit = at == val[m, e:e + 1, :]
                hot[m, e * RB:(e + 1) * RB, :] = jnp.where(hit, 1.0, 0.0).astype(hot.dtype)
                w = jnp.sum(jnp.where(hit, gate[m, e:e + 1, :], 0.0), axis=1, keepdims=True)
                rg[e, pl.ds(pl.multiple_of(m * RB, RB), RB), :] = jnp.broadcast_to(w, (RB, 128))

        if n == g.steps - 2:
            for cp in saves:
                cp.start()
    g.end()
    for cp in saves:
        cp.wait()


def gather_blocks(v, val, gate, RB, U, B, cid):
    G, experts, KB = val.shape
    sds = jax.ShapeDtypeStruct
    vmem = pl.BlockSpec(memory_space=pltpu.VMEM)
    hot, rg = sds((G, experts * RB, KB), jnp.bfloat16), sds((experts, G * RB, 128), jnp.float32)
    return pl.pallas_call(
        functools.partial(gather_kernel, U, B, experts, RB),
        out_shape=[sds((U * B,) + v.shape, v.dtype), hot, rg],
        in_specs=any_specs(1) + [vmem, vmem],
        out_specs=any_specs(3),
        scratch_shapes=Gather.semaphores(U, B) + [
            pltpu.VMEM(hot.shape, hot.dtype), pltpu.VMEM(rg.shape, rg.dtype), pltpu.SemaphoreType.DMA((2,))],
        compiler_params=pltpu.CompilerParams(
            collective_id=cid, has_side_effects=True, vmem_limit_bytes=32 * 2**20),
    )(v, val, gate)


def front_kernel(U, B, width, copies, tok, small, wq, wk, wv, tok_out, small_out, weights_out, *sems):
    p = Place(U, B)
    p.barrier("plane")
    g = PlaneGather(p, tok, tok_out, *sems[:3])
    s = Spread(p, lambda r: [(small, ())], small_out, *sems[3:6])
    every = slice(None)

    def columns(r):
        h = lax.div(r, copies)
        cols = pl.ds(pl.multiple_of(h * width, width), width)
        return [(m.at[:, cols], (every, slice(n * width, (n + 1) * width))) for n, m in enumerate((wq, wk, wv))]

    w = Spread(p, columns, weights_out, *sems[6:9])
    s.begin()
    g.step(0)
    w.begin()
    for n in range(1, g.steps):
        g.step(n)
        if n == 1:
            s.middle()
            w.middle()
    s.end()
    w.end()
    g.end()


def front(tok, small, weights, width, copies, U, B, cid):
    F = U * B
    rows = weights[0].shape[0]
    shapes = [((F,) + tok.shape[1:], tok.dtype), ((F,) + small.shape, small.dtype), ((F, rows, 3 * width), weights[0].dtype)]
    return pl.pallas_call(
        functools.partial(front_kernel, U, B, width, copies),
        out_shape=[jax.ShapeDtypeStruct(*m) for m in shapes],
        in_specs=any_specs(5),
        out_specs=any_specs(3),
        scratch_shapes=PlaneGather.semaphores(U, B) + Spread.semaphores(U, B, 1) + Spread.semaphores(U, B, 3),
        compiler_params=pltpu.CompilerParams(collective_id=cid, has_side_effects=True),
    )(tok, small, *weights)


class Scatter:
    def __init__(self, p, acc, rc, rx0, rx1, ry0, ry1, rz, fin, loc, cs, cr, xs, xr, ys, yr, zs, zr, like=(0, 1), chain=False):
        self.p, self.like, self.chain = p, like, chain
        self.acc, self.rc, self.rx, self.ry, self.rz, self.fin = acc, rc, (rx0, rx1), (ry0, ry1), rz, fin
        self.loc, self.cs, self.cr = loc, cs, cr
        self.xs, self.xr, self.ys, self.yr, self.zs, self.zr = xs, xr, ys, yr, zs, zr
        self.order = p.far_first() if chain else p.others("z") + [p.z]
        self.steps = p.Z + 2
        self.started, self.maybe = [], []
        self.local = True

    @staticmethod
    def scratch(U, B, rows, D, t, like=(0, 1), chain=False):
        X, Y, Z, Q = U // 2, 2, B // 2, U * B // 2
        dma = pltpu.SemaphoreType.DMA
        x, y = max(X - 1, 1), Y - 1
        return [
            pltpu.VMEM((Q, 2, rows, D), t),
            pltpu.VMEM((Q, 2, rows, D), t),
            pltpu.VMEM((x, Z * Y, rows, D), t),
            pltpu.VMEM((x, Z if like[1] else Z * Y, rows, D), t),
            pltpu.VMEM((y, Z, rows, D), t),
            pltpu.VMEM((y, Z * X if like[1] else Z, rows, D), t),
            pltpu.VMEM((2, 2, Z, rows, D) if chain else (2, Z, rows, D), t),
            pltpu.VMEM((2, rows, D), jnp.float32),
            dma((Q, 2)),
            dma((Q, 2)),
            dma((Q, 2)),
            dma((2, x, Z * Y)),
            dma((2, x, Z * Y)),
            dma((2, y, Z * X)),
            dma((2, y, Z * X)),
            dma((2, Z)),
            dma((2, 2, Z) if chain else (2, Z)),
        ]

    SCRATCH = 17

    def start(self, *a):
        cp = remote(*a)
        cp.start()
        self.started.append(cp)

    def got(self, ref, sem):
        remote(ref, ref, sem, sem, self.p.core_peer).wait_recv()

    def load(self, src):
        p = self.p
        for k in self.order:
            for j in p.others("x") + [p.x]:
                for i in range(p.Y):
                    for h in (0, 1):
                        q = p.chip(j, i, k)
                        cp = self.across(src.at[p.block(j, i, k, 1 - p.c), h], q, h)
                        cp.start()
                        self.started.append(cp)
                        self.keep(src.at[p.block(j, i, k, p.c), h], q, h).start()

    def keep(self, src, q, h):
        return pltpu.make_async_copy(src, self.acc.at[q, h], self.loc.at[q, h])

    def across(self, src, q, h):
        return remote(src, self.rc.at[q, h], self.cs.at[q, h], self.cr.at[q, h], self.p.core_peer)

    def ready(self, h, j, i, k):
        q = self.p.chip(j, i, k)
        if self.local:
            self.keep(self.acc.at[q, h], q, h).wait()
        self.got(self.rc.at[q, h], self.cr.at[q, h])
        return [self.rc.at[q, h]]

    def send_x(self, h, q, j, s):
        p = self.p
        o = lax.rem(j - p.x + p.X, p.X) - 1
        self.start(self.acc.at[q, h], self.rx[h].at[o, s], self.xs.at[h, o, s], self.xr.at[h, o, s],
                   p.dev(j, p.y, p.z, p.c))

    def send_y(self, h, q, i, s):
        p = self.p
        o = lax.rem(i - p.y + p.Y, p.Y) - 1
        self.start(self.acc.at[q, h], self.ry[h].at[o, s], self.ys.at[h, o, s], self.yr.at[h, o, s],
                   p.dev(p.x, i, p.z, p.c))

    def from_x(self, h, s):
        out = []
        for o in range(self.p.X - 1):
            self.got(self.rx[h].at[o, s], self.xr.at[h, o, s])
            out.append(self.rx[h].at[o, s])
        return out

    def from_y(self, h, s):
        out = []
        for o in range(self.p.Y - 1):
            self.got(self.ry[h].at[o, s], self.yr.at[h, o, s])
            out.append(self.ry[h].at[o, s])
        return out

    def along_z(self, n, h, q, extra):
        p = self.p
        k = self.order[n]
        here = self.acc.at[q, h]
        add(here, extra)
        for way, cond in enumerate(((k >= p.z) & (p.z > 0), (k <= p.z) & (p.z < p.Z - 1))):
            @pl.when(cond)
            def _(way=way):
                self.got(self.rz.at[way, h, k], self.zr.at[way, h, k])
                add(here, [self.rz.at[way, h, k]])
        if n == p.Z - 1:
            add(here, [], self.fin.at[h])
            return
        for way, cond, z in ((0, k > p.z, p.z + 1), (1, k < p.z, p.z - 1)):
            cp = remote(here, self.rz.at[way, h, k], self.zs.at[h, k], self.zr.at[way, h, k], p.dev(p.x, p.y, z, p.c))

            @pl.when(cond)
            def _(cp=cp):
                cp.start()

            self.maybe.append((cond, cp))

    def last(self, n, h, q, extra):
        p = self.p
        if self.chain:
            self.along_z(n, h, q, extra)
            return
        k = self.order[n]
        if n < p.Z - 1:
            add(self.acc.at[q, h], extra)
            self.start(self.acc.at[q, h], self.rz.at[h, p.z], self.zs.at[h, k], self.zr.at[h, p.z],
                       p.dev(p.x, p.y, k, p.c))
        else:
            for a in p.others("z"):
                self.got(self.rz.at[h, a], self.zr.at[h, a])
                extra.append(self.rz.at[h, a])
            add(self.acc.at[q, h], extra, self.fin.at[h])

    def first(self, n, j):
        p = self.p
        k = self.order[n]
        for h, way in enumerate(self.like):
            if way == 0 and j is not p.x:
                for i in range(p.Y):
                    q = p.chip(j, i, k)
                    add(self.acc.at[q, h], self.ready(h, j, i, k))
                    self.send_x(h, q, j, k * p.Y + i)
            if way == 1:
                for i in p.others("y"):
                    q = p.chip(j, i, k)
                    add(self.acc.at[q, h], self.ready(h, j, i, k))
                    self.send_y(h, q, i, k * p.X + j)

    def rest(self, n):
        p = self.p
        X, Y, Z = p.X, p.Y, p.Z
        if 1 <= n <= Z:
            k = self.order[n - 1]
            for h, way in enumerate(self.like):
                if way == 0:
                    for i in p.others("y"):
                        q = p.chip(p.x, i, k)
                        add(self.acc.at[q, h], self.ready(h, p.x, i, k) + self.from_x(h, k * Y + i))
                        self.send_y(h, q, i, k)
                else:
                    for j in p.others("x"):
                        q = p.chip(j, p.y, k)
                        add(self.acc.at[q, h], self.ready(h, j, p.y, k) + self.from_y(h, k * X + j))
                        self.send_x(h, q, j, k)
        if n >= 2:
            k = self.order[n - 2]
            q = p.chip(p.x, p.y, k)
            for h, way in enumerate(self.like):
                extra = self.ready(h, p.x, p.y, k)
                if way == 0:
                    extra = extra + self.from_x(h, k * Y + p.y) + self.from_y(h, k)
                else:
                    extra = extra + self.from_y(h, k * X + p.x) + self.from_x(h, k)
                self.last(n - 2, h, q, extra)

    def step(self, n):
        if n < self.p.Z:
            for j in self.p.others("x") + [self.p.x]:
                self.first(n, j)
        self.rest(n)

    def sent(self):
        for cp in self.started:
            cp.wait_send()
        for cond, cp in self.maybe:
            @pl.when(cond)
            def _(cp=cp):
                cp.wait_send()


def add(dst, srcs, f32_out=None):
    step = 16

    def one(n, _):
        r = pl.ds(pl.multiple_of(n * step, step), step)
        t = dst[r, :].astype(jnp.float32)
        for s in srcs:
            t = t + s[r, :].astype(jnp.float32)
        if f32_out is None:
            dst[r, :] = t.astype(dst.dtype)
        else:
            f32_out[r, :] = t
        return 0

    lax.fori_loop(0, dst.shape[0] // step, one, 0)


class PlaneScatter(Scatter):
    def __init__(self, p, acc, rc, ry, rz, fin, loc, cs, cr, ys, yr, zs, zr):
        self.p = p
        self.acc, self.rc, self.rz, self.fin, self.ry = acc, rc, rz, fin, (ry.at[0], ry.at[1])
        self.loc, self.cs, self.cr = loc, cs, cr
        self.ys, self.yr, self.zs, self.zr = ys, yr, zs, zr
        self.chain = True
        self.order = p.far_first()
        self.steps = p.Z + 1
        self.started, self.maybe = [], []
        self.local = True

    @staticmethod
    def scratch(U, B, rows, D, t):
        Y, Z = 2, B // 2
        dma = pltpu.SemaphoreType.DMA
        return [
            pltpu.VMEM((B, 2, rows, D), t),
            pltpu.VMEM((B, 2, rows, D), t),
            pltpu.VMEM((2, Y - 1, Z, rows, D), t),
            pltpu.VMEM((2, 2, Z, rows, D), t),
            pltpu.VMEM((2, rows, D), jnp.float32),
            dma((B, 2)),
            dma((B, 2)),
            dma((B, 2)),
            dma((2, Y - 1, Z)),
            dma((2, Y - 1, Z)),
            dma((2, Z)),
            dma((2, 2, Z)),
        ]

    SCRATCH = 12

    def load(self, src):
        p = self.p
        for k in self.order:
            for i in p.others("y") + [p.y]:
                for h in (0, 1):
                    q = p.chip(0, i, k)
                    cp = self.across(src.at[p.block(h, i, k, 1 - p.c)], q, h)
                    cp.start()
                    self.started.append(cp)
                    self.keep(src.at[p.block(h, i, k, p.c)], q, h).start()

    def step(self, n):
        p = self.p
        if n < p.Z:
            k = self.order[n]
            for i in p.others("y"):
                q = p.chip(0, i, k)
                for h in (0, 1):
                    add(self.acc.at[q, h], self.ready(h, 0, i, k))
                    self.send_y(h, q, i, k)
        if n >= 1:
            k = self.order[n - 1]
            q = p.chip(0, p.y, k)
            for h in (0, 1):
                self.last(n - 1, h, q, self.ready(h, 0, p.y, k) + self.from_y(h, k))


def keep_sum(fin, out, sem):
    cp = pltpu.make_async_copy(fin, out, sem)
    cp.start()
    cp.wait()


class Combine:
    def __init__(self, s, rows_in, hot_in, cols, rows_buf, hot_buf, stage, sems):
        self.s, self.p = s, s.p
        self.rows_in, self.hot_in, self.cols = rows_in, hot_in, cols
        self.rows_buf, self.hot_buf, self.stage, self.sems = rows_buf, hot_buf, stage, sems
        self.sent = []
        s.local = False

    def loads(self, j, k):
        g = j * self.p.Z + k
        RB = self.rows_buf.shape[1]
        rows = pl.ds(pl.multiple_of(g * RB, RB), RB)
        return (
            pltpu.make_async_copy(self.rows_in.at[:, rows, self.cols], self.rows_buf, self.sems.at[0]),
            pltpu.make_async_copy(self.hot_in.at[g], self.hot_buf, self.sems.at[1]),
        )

    def fetch(self, j, k):
        for cp in self.loads(j, k):
            cp.start()

    def make(self, j, k):
        p, s = self.p, self.s
        for cp in self.loads(j, k):
            cp.wait()
        for cp in self.sent:
            cp.wait_send()
        self.sent.clear()
        experts, RB, D = self.rows_buf.shape
        KB = self.hot_buf.shape[1]
        cut = min(D, 512)

        half = KB // 2
        t = s.acc.shape[2]

        def blocks(core, put):
            hot = self.hot_buf[:, pl.ds(pl.multiple_of(core * half, half), half)]
            for n in range(0, D, cut):
                m = lax.dot_general(hot, self.rows_buf[:, :, n:n + cut].reshape(experts * RB, cut),
                                    (((0,), (0,)), ((), ())), preferred_element_type=jnp.float32).astype(s.acc.dtype)
                for i in range(p.Y):
                    for h in (0, 1):
                        at = (i * 2 + h) * t
                        put(i, h, n, m[at:at + t])

        def away(i, h, n, m):
            self.stage[i, h, :, n:n + cut] = m

        def own(i, h, n, m):
            s.acc[p.chip(j, i, k), h, :, n:n + cut] = m

        blocks(1 - p.c, away)
        for i in range(p.Y):
            for h in (0, 1):
                cp = s.across(self.stage.at[i, h], p.chip(j, i, k), h)
                cp.start()
                self.sent.append(cp)
        blocks(p.c, own)

    def end(self):
        for cp in self.sent:
            cp.wait_send()


def pair_kernel(U, B, cols, a, b, hot, out_a, out_b, *scratch):
    p = Place(U, B)
    p.barrier("lines")
    k = Scatter.SCRATCH
    work = [Scatter(p, *scratch[k * i:k * (i + 1)]) for i in range(2)]
    feed = [Combine(s, m, hot, cols, *scratch[2 * k:2 * k + 4]) for s, m in zip(work, (a, b))]
    feed[1].sent = feed[0].sent
    xs = p.others("x") + [p.x]
    todo = [(f, j, z) for z in work[0].order for f in feed for j in xs]
    todo[0][0].fetch(*todo[0][1:])
    at = 0
    for n in range(work[0].steps):
        for s in work:
            if n < p.Z:
                for x in xs:
                    f, j, z = todo[at]
                    f.make(j, z)
                    at += 1
                    if at < len(todo):
                        todo[at][0].fetch(*todo[at][1:])
                    s.first(n, x)
            s.rest(n)
    feed[0].end()
    for s, out in zip(work, (out_a, out_b)):
        keep_sum(s.fin, out, scratch[-1].at[0])
        s.sent()


def scatter_pair(a, b, hot, rows, U, B, cid):
    F = U * B
    experts, _, D = a.shape
    G, n, KB = hot.shape
    RB = n // experts
    parts = max(1, F // 32)
    D = D // parts
    dma = pltpu.SemaphoreType.DMA

    def call(c):
        return pl.pallas_call(
            functools.partial(pair_kernel, U, B, pl.ds(c * D, D)),
            out_shape=[jax.ShapeDtypeStruct((2, rows, D), jnp.float32)] * 2,
            in_specs=any_specs(3),
            out_specs=any_specs(2),
            scratch_shapes=Scatter.scratch(U, B, rows, D, a.dtype) * 2 + [
                pltpu.VMEM((experts, RB, D), a.dtype), pltpu.VMEM((n, KB), hot.dtype),
                pltpu.VMEM((2, 2, rows, D), a.dtype), dma((2,)), dma((1,))],
            compiler_params=pltpu.CompilerParams(
                collective_id=cid, has_side_effects=True, vmem_limit_bytes=62 * 2**20),
        )(a, b, hot)

    got = [call(c) for c in range(parts)]
    return tuple(jnp.concatenate([g[i] for g in got], axis=-1) for i in range(2))


class PairExchange:
    def __init__(self, p, src, out, acc, rc, local, send, recv):
        self.p, self.src, self.out, self.acc, self.rc = p, src, out, acc, rc
        self.local, self.send, self.recv = local, send, recv

    @staticmethod
    def scratch(U, B, rows, w, t):
        dma = pltpu.SemaphoreType.DMA
        return [pltpu.VMEM((2 * B, rows, w), t), pltpu.VMEM((2 * B, rows, w), t),
                dma((1,)), dma((1 + 2 * B,)), dma((1 + 2 * B,))]

    SCRATCH = 5

    def across(self):
        p = self.p
        return remote(self.src.at[1 - p.x], self.rc, self.send.at[0], self.recv.at[0], p.x_peer)

    def own(self):
        return pltpu.make_async_copy(self.src.at[self.p.x], self.acc, self.local.at[0])

    def away(self, o):
        p = self.p
        r = lax.rem(p.r + o, 2 * p.B)
        return remote(self.acc.at[r], self.out.at[p.r], self.send.at[1 + r], self.recv.at[1 + p.r], p.plane_dev(r))

    def begin(self):
        self.across().start()
        self.own().start()

    def middle(self):
        p = self.p
        self.own().wait()
        self.across().wait_recv()

        @pl.loop(0, 2 * p.B)
        def _(r):
            t = self.acc[r].astype(jnp.float32) + self.rc[r].astype(jnp.float32)
            self.acc[r] = t.astype(self.acc.dtype)

        @pl.loop(1, 2 * p.B)
        def _(o):
            self.away(o).start()

        cp = pltpu.make_async_copy(self.acc.at[p.r], self.out.at[p.r], self.local.at[0])
        cp.start()
        cp.wait()

    def end(self):
        p = self.p
        self.across().wait_send()

        @pl.loop(1, 2 * p.B)
        def _(o):
            r = lax.rem(p.r + o, 2 * p.B)
            part = self.out.at[r]
            remote(part, part, self.send.at[0], self.recv.at[1 + r], p.x_peer).wait_recv()
            self.away(o).wait_send()


def finish_kernel(U, B, more, *refs):
    p = Place(U, B)
    p.barrier("plane")
    n = 4 if more else 3
    srcs, outs, scratch = refs[:n], refs[n:2 * n + 1], refs[2 * n + 1:]
    at = PlaneScatter.SCRATCH
    work = [PlaneScatter(p, *scratch[:at])]
    if more:
        work.append(Scatter(p, *scratch[at:at + Scatter.SCRATCH], like=(0, 0), chain=True))
        at += Scatter.SCRATCH
    ex = []
    for i in range(2):
        ex.append(PairExchange(p, srcs[i], outs[i], *scratch[at:at + PairExchange.SCRATCH]))
        at += PairExchange.SCRATCH
    stage, sems = scratch[at:]
    for s, src in zip(work, srcs[2:]):
        s.load(src)
    for e in ex:
        e.begin()
    work[0].step(0)
    for e in ex:
        e.middle()
    for s in work[1:]:
        s.step(0)
    for j in range(1, p.Z + 1):
        for s in work:
            s.step(j)
    fin = work[0].fin
    rows = fin.shape[1]

    def one(m, _):
        r = pl.ds(pl.multiple_of(m * 16, 16), 16)
        stage[r, :] = fin[1 - p.x, r, :].astype(stage.dtype)
        return 0

    lax.fori_loop(0, rows // 16, one, 0)
    away = remote(stage, outs[3], sems.at[0], sems.at[1], p.x_peer)
    away.start()
    keep_sum(fin.at[p.x], outs[2], sems.at[2])
    if more:
        work[1].step(p.Z + 1)
        keep_sum(work[1].fin, outs[4], sems.at[2])
    away.wait_recv()
    away.wait_send()
    for s in work:
        s.sent()
    for e in ex:
        e.end()


def finish(weights, small, hidden, out, U, B, cid):
    F = U * B
    parts = max(1, F // 32)
    D = hidden.shape[-1] // parts
    sds, f32 = jax.ShapeDtypeStruct, jnp.float32

    def call(h, o, cid):
        args = [m.reshape((2, 2 * B) + m.shape[1:]) for m in (weights, small)] + [h]
        shapes = [sds((2 * B,) + m.shape[1:], m.dtype) for m in (weights, small)]
        shapes += [sds(h.shape[1:], f32), sds(h.shape[1:], h.dtype)]
        scratch = PlaneScatter.scratch(U, B, h.shape[1], h.shape[2], h.dtype)
        if o is not None:
            args.append(o)
            shapes.append(sds(o.shape[1:], f32))
            scratch += Scatter.scratch(U, B, o.shape[2], o.shape[3], o.dtype, (0, 0), True)
        for m in (weights, small):
            scratch += PairExchange.scratch(U, B, m.shape[1], m.shape[2], m.dtype)
        return pl.pallas_call(
            functools.partial(finish_kernel, U, B, o is not None),
            out_shape=shapes,
            in_specs=any_specs(len(args)),
            out_specs=any_specs(len(shapes)),
            scratch_shapes=scratch + [pltpu.VMEM(h.shape[1:], h.dtype), pltpu.SemaphoreType.DMA((3,))],
            compiler_params=pltpu.CompilerParams(
                collective_id=cid, has_side_effects=True, vmem_limit_bytes=62 * 2**20),
        )(*args)

    if parts == 1:
        return call(hidden, out, cid)
    got = [call(hidden[..., n * D:(n + 1) * D], None, cid) for n in range(parts)]
    own, other = (jnp.concatenate([g[i] for g in got], axis=-1) for i in (2, 3))
    return got[0][0], got[0][1], own, other, scatter_by_permutes(out, U, B)


def scatter_by_permutes(v, U, B):
    X, Y, Z = U // 2, 2, B // 2
    f32 = jnp.float32
    u, b = lax.axis_index("ulysses"), lax.axis_index("blk")
    c, x, y, z = lax.rem(u, 2), lax.div(u, 2), lax.rem(b, Y), lax.div(b, Y)
    where = {"c": c, "x": x, "y": y, "z": z}
    size = {"c": 2, "x": X, "y": Y, "z": Z}

    def pairs(axis, by):
        out = []
        for f in range(U * B):
            at = {"x": f // B // 2, "c": f // B % 2, "z": f % B // Y, "y": f % Y}
            at[axis] = (at[axis] + by) % size[axis]
            out.append((f, (at["x"] * 2 + at["c"]) * B + at["z"] * Y + at["y"]))
        return out

    def fold(m, axis, dim):
        n = size[axis]
        total = lax.dynamic_index_in_dim(m, where[axis], dim, keepdims=False).astype(f32)
        for by in range(1, n):
            part = lax.dynamic_index_in_dim(m, lax.rem(where[axis] + by, n), dim, keepdims=False)
            total = total + lax.ppermute(part, ("ulysses", "blk"), pairs(axis, by)).astype(f32)
        return total

    rows, D = v.shape[-2:]
    m = fold(v.reshape(X, 2, Z, Y, 2, rows, D), "c", 1).astype(v.dtype)
    first = fold(m[:, :, :, 0], "x", 0).astype(v.dtype)
    first = fold(first, "y", 1).astype(v.dtype)
    second = fold(m[:, :, :, 1], "y", 2).astype(v.dtype)
    second = fold(second, "x", 0).astype(v.dtype)
    return fold(jnp.stack([first, second], axis=1), "z", 0)


def rms_norm(values, gains):
    return values * lax.rsqrt(jnp.mean(values * values, axis=-1, keepdims=True) + EPSILON) * gains


def dot(a, b, ca, cb):
    return lax.dot_general(a, b, (((ca,), (cb,)), ((), ())), preferred_element_type=jnp.float32)


def attend_kernel(U, B, bq, scale, q_ref, k_ref, vt_ref, out_ref, lse_ref, rows_ref, send, recv):
    p = Place(U, B)
    p.barrier("every")
    per = bq // rows_ref.shape[1]
    n = q_ref.shape[0] // bq

    def away(f):
        return remote(rows_ref.at[f], out_ref.at[p.me], send.at[f], recv.at[p.me], p.flat_dev(f))

    @pl.loop(0, n)
    def _(t):
        i = lax.rem(t + lax.div(p.me, per), n)
        rows = pl.ds(pl.multiple_of(i * bq, bq), bq)
        s = dot(k_ref[...], q_ref[rows, :], 1, 1) * scale
        top = jnp.max(s, axis=0, keepdims=True)
        e = jnp.exp(s - top)
        total = jnp.sum(e, axis=0, keepdims=True)
        o = dot(vt_ref[...], e.astype(jnp.bfloat16), 1, 0) / total
        lse_ref[:, rows] = top + jnp.log(total)
        rows_ref[pl.ds(i * per, per)] = o.T.astype(rows_ref.dtype).reshape((per,) + rows_ref.shape[1:])
        for d in range(per):
            f = i * per + d

            @pl.when(f != p.me)
            def _():
                away(f).start()

    cp = pltpu.make_async_copy(rows_ref.at[p.me], out_ref.at[p.me], recv.at[p.me])
    cp.start()
    cp.wait()

    @pl.loop(1, p.F)
    def _(o):
        f = lax.rem(p.me + o, p.F)
        remote(out_ref.at[f], out_ref.at[f], send.at[f], recv.at[f], p.flat_dev(f)).wait_recv()
        away(f).wait_send()


def attend(q, k, vt, positions, U, B, cid):
    n = q.shape[0]
    F = U * B
    bq = 256 if n <= 2048 else 128
    vmem = pl.BlockSpec(memory_space=pltpu.VMEM)
    dma = pltpu.SemaphoreType.DMA
    return pl.pallas_call(
        functools.partial(attend_kernel, U, B, bq, 1.0 / math.sqrt(HD)),
        in_specs=[vmem] * 3,
        out_specs=any_specs(1) + [vmem],
        out_shape=[jax.ShapeDtypeStruct((F, positions, HD), jnp.bfloat16), jax.ShapeDtypeStruct((1, n), jnp.float32)],
        scratch_shapes=[pltpu.VMEM((F, positions, HD), jnp.bfloat16), dma((F,)), dma((F,))],
        compiler_params=pltpu.CompilerParams(
            collective_id=cid, has_side_effects=True, vmem_limit_bytes=40 * 2**20),
    )(q, k, vt)


def attend_back_kernel(U, B, bq, scale, src_ref, q_ref, lse_ref, k_ref, kt_ref, v_ref,
                       dq_ref, dk_ref, dv_ref, do_ref, send, recv, local):
    p = Place(U, B)
    p.barrier("every")
    per = bq // do_ref.shape[1]
    n = q_ref.shape[0] // bq

    def away(f):
        return remote(src_ref.at[f], do_ref.at[p.me], send.at[f], recv.at[p.me], p.flat_dev(f))

    @pl.loop(1, p.F)
    def _(o):
        away(lax.rem(p.me + o, p.F)).start()

    cp = pltpu.make_async_copy(src_ref.at[p.me], do_ref.at[p.me], local.at[0])
    cp.start()
    dk_ref[...] = jnp.zeros_like(dk_ref)
    dv_ref[...] = jnp.zeros_like(dv_ref)
    cp.wait()

    @pl.loop(0, n)
    def _(t):
        i = lax.rem(n - t + lax.div(p.me, per), n)
        rows = pl.ds(pl.multiple_of(i * bq, bq), bq)
        e = jnp.exp(dot(k_ref[...], q_ref[rows, :], 1, 1) * scale - lse_ref[:, rows])
        for d in range(per):
            f = i * per + d

            @pl.when(f != p.me)
            def _():
                remote(do_ref.at[f], do_ref.at[f], send.at[f], recv.at[f], p.flat_dev(f)).wait_recv()

        do = do_ref[pl.ds(i * per, per)].reshape(bq, HD)
        dp = dot(v_ref[...], do, 1, 1)
        delta = jnp.sum(e * dp, axis=0, keepdims=True)
        ds = (e * (dp - delta)).astype(jnp.bfloat16)
        dv_ref[...] += dot(e.astype(jnp.bfloat16), do, 1, 0)
        dk_ref[...] += dot(ds, q_ref[rows, :], 1, 0) * scale
        dq_ref[rows, :] = (dot(kt_ref[...], ds, 1, 0) * scale).T

    @pl.loop(1, p.F)
    def _(o):
        away(lax.rem(p.me + o, p.F)).wait_send()


def attend_back(grads, q, lse, k, kt, v, U, B, cid):
    n = q.shape[0]
    F = U * B
    bq = 256 if n <= 2048 else 128
    vmem = pl.BlockSpec(memory_space=pltpu.VMEM)
    dma = pltpu.SemaphoreType.DMA
    return pl.pallas_call(
        functools.partial(attend_back_kernel, U, B, bq, 1.0 / math.sqrt(HD)),
        in_specs=any_specs(1) + [vmem] * 5,
        out_specs=[vmem] * 3,
        out_shape=[jax.ShapeDtypeStruct((n, HD), jnp.float32)] * 3,
        scratch_shapes=[pltpu.VMEM(grads.shape, grads.dtype), dma((F,)), dma((F,)), dma((1,))],
        compiler_params=pltpu.CompilerParams(
            collective_id=cid, has_side_effects=True, vmem_limit_bytes=58 * 2**20),
    )(grads, q, lse, k, kt, v)


def turn(v, cosine, sine):
    return v * cosine + pltpu.roll(v, HD // 2, 1) * sine


def project_kernel(tok_ref, gain_ref, w_ref, qk_ref, cos_ref, sin_ref,
                   q_ref, k_ref, v_ref, kt_ref, vt_ref, rq_ref, rk_ref):
    bf16 = jnp.bfloat16
    raw = dot(rms_norm(tok_ref[...].astype(jnp.float32), gain_ref[...]).astype(bf16), w_ref[...], 1, 0)
    rq, rk, v = raw[:, :HD], raw[:, HD:2 * HD], raw[:, 2 * HD:].astype(bf16)
    rq_ref[...] = rq
    rk_ref[...] = rk
    q_ref[...] = turn(rms_norm(rq, qk_ref[0:1]), cos_ref[...], sin_ref[...]).astype(bf16)
    k = turn(rms_norm(rk, qk_ref[1:2]), cos_ref[...], sin_ref[...])
    k_ref[...] = k.astype(bf16)
    kt_ref[...] = k.T.astype(bf16)
    v_ref[...] = v
    vt_ref[...] = raw[:, 2 * HD:].T.astype(bf16)


def project(tok, gain, w, qk, cosine, sine):
    n, D = tok.shape
    bm = 512
    row, whole = (lambda i: (i, 0)), (lambda i: (0, 0))
    head, across = pl.BlockSpec((bm, HD), row), pl.BlockSpec((HD, bm), lambda i: (0, i))
    sds = jax.ShapeDtypeStruct
    f32, bf16 = jnp.float32, jnp.bfloat16
    return pl.pallas_call(
        project_kernel,
        grid=(n // bm,),
        in_specs=[
            pl.BlockSpec((bm, D), row), pl.BlockSpec((1, D), whole), pl.BlockSpec((D, 3 * HD), whole),
            pl.BlockSpec((2, HD), whole), head, head,
        ],
        out_specs=[head, head, head, across, across, head, head],
        out_shape=[sds((n, HD), bf16)] * 3 + [sds((HD, n), bf16)] * 2 + [sds((n, HD), f32)] * 2,
        compiler_params=pltpu.CompilerParams(vmem_limit_bytes=58 * 2**20),
    )(tok, gain, w, qk, cosine, sine)


def head_back_kernel(dq_ref, dk_ref, dv_ref, rq_ref, rk_ref, cos_ref, sin_ref, qk_ref, tok_ref, gain_ref, w_ref,
                     part_ref, dwout_ref, dg_ref, da_ref, dw_ref):
    f32, bf16 = jnp.float32, jnp.bfloat16

    @pl.when(pl.program_id(0) == 0)
    def _():
        dw_ref[...] = jnp.zeros_like(dw_ref)
        dg_ref[...] = jnp.zeros_like(dg_ref)
        da_ref[...] = jnp.zeros_like(da_ref)

    grads = []
    for n, (g_ref, raw_ref) in enumerate(((dq_ref, rq_ref), (dk_ref, rk_ref))):
        w = turn(g_ref[...].astype(bf16).astype(f32), cos_ref[...], -sin_ref[...])
        u = raw_ref[...]
        r = lax.rsqrt(jnp.mean(u * u, axis=-1, keepdims=True) + EPSILON)
        norm = u * r
        dg_ref[n:n + 1, :] += jnp.sum(w * norm, axis=0, keepdims=True)
        m = w * qk_ref[n:n + 1]
        grads.append((r * (m - norm * jnp.mean(m * norm, axis=-1, keepdims=True))).astype(bf16))
    grads.append(dv_ref[...].astype(bf16))
    grad = jnp.concatenate(grads, axis=1)
    across = grad.T
    tok = tok_ref[...].astype(f32)
    norm = tok * lax.rsqrt(jnp.mean(tok * tok, axis=-1, keepdims=True) + EPSILON)
    hidden = (norm * gain_ref[...]).astype(bf16)
    D = tok.shape[1]
    cut = min(D, 512)
    for n in range(0, D, cut):
        part = dot(grad, w_ref[n:n + cut, :], 1, 1)
        part_ref[:, n:n + cut] = part.astype(bf16)
        da_ref[0:1, n:n + cut] += jnp.sum(part * norm[:, n:n + cut], axis=0, keepdims=True)
        dw_ref[:, n:n + cut] += dot(across, hidden[:, n:n + cut], 1, 0)

    @pl.when(pl.program_id(0) == pl.num_programs(0) - 1)
    def _():
        for n in range(0, D, cut):
            dwout_ref[n:n + cut, :] = dw_ref[:, n:n + cut].T.astype(bf16)


def head_back(dq, dk, dv, rq, rk, cosine, sine, qk, tok, gain, w):
    n, D = tok.shape
    bm = 512
    row, whole = (lambda i: (i, 0)), (lambda i: (0, 0))
    head = pl.BlockSpec((bm, HD), row)
    sds = jax.ShapeDtypeStruct
    return pl.pallas_call(
        head_back_kernel,
        grid=(n // bm,),
        in_specs=[head] * 7 + [
            pl.BlockSpec((2, HD), whole), pl.BlockSpec((bm, D), row), pl.BlockSpec((1, D), whole),
            pl.BlockSpec((D, 3 * HD), whole)],
        out_specs=[
            pl.BlockSpec((bm, D), row), pl.BlockSpec((D, 3 * HD), whole), pl.BlockSpec((8, HD), whole),
            pl.BlockSpec((8, D), whole)],
        out_shape=[sds((n, D), jnp.bfloat16), sds((D, 3 * HD), jnp.bfloat16), sds((8, HD), jnp.float32),
                   sds((8, D), jnp.float32)],
        scratch_shapes=[pltpu.VMEM((3 * HD, D), jnp.float32)],
        compiler_params=pltpu.CompilerParams(vmem_limit_bytes=58 * 2**20),
    )(dq, dk, dv, rq, rk, cosine, sine, qk, tok, gain, w)


def dispatch_kernel(hot_ref, rg_ref, norm_ref, cot_ref, x_ref, pg_ref):
    bf16 = jnp.bfloat16
    experts, RB, D = x_ref.shape
    hot = hot_ref[0]
    KB = hot.shape[1]
    weight = rg_ref[:, :, 0:1].reshape(experts * RB, 1)
    cut = min(D, 512)
    norm = norm_ref[...].reshape(KB, D)
    cot = cot_ref[...].reshape(KB, D)
    for n in range(0, D, cut):
        x = dot(hot, norm[:, n:n + cut], 1, 0).astype(bf16)
        x_ref[:, :, n:n + cut] = x.reshape(experts, RB, cut)
        g = (dot(hot, cot[:, n:n + cut], 1, 0) * weight).astype(bf16)
        pg_ref[:, :, n:n + cut] = g.reshape(experts, RB, cut)


def group_spec(shape, Z):
    X, two, _, Y, T, D = shape
    return pl.BlockSpec((1, two, 1, Y, T, D), lambda g: (g // Z, 0, g % Z, 0, 0, 0))


def dispatch(hot, rg, normed, cot):
    G, rows, KB = hot.shape
    experts, D, Z = rg.shape[0], normed.shape[-1], normed.shape[2]
    RB = rows // experts
    out = pl.BlockSpec((experts, RB, D), lambda g: (0, g, 0))
    return pl.pallas_call(
        dispatch_kernel,
        grid=(G,),
        in_specs=[pl.BlockSpec((1, rows, KB), lambda g: (g, 0, 0)), pl.BlockSpec((experts, RB, 128), lambda g: (0, g, 0)),
                  group_spec(normed.shape, Z), group_spec(cot.shape, Z)],
        out_specs=[out, out],
        out_shape=[jax.ShapeDtypeStruct((experts, G * RB, D), jnp.bfloat16)] * 2,
        compiler_params=pltpu.CompilerParams(vmem_limit_bytes=62 * 2**20),
    )(hot, rg, normed, cot)


def expert_kernel(x_ref, pg_ref, rg_ref, wg_ref, wu_ref, wd_ref, y_ref, dx_ref, dwg_ref, dwu_ref, dwd_ref):
    bf16 = jnp.bfloat16
    x, pg = x_ref[0], pg_ref[0]
    D = x.shape[1]
    gate, up = dot(x, wg_ref[0], 1, 0), dot(x, wu_ref[0], 1, 0)
    sigma = jax.nn.sigmoid(gate)
    silu = gate * sigma
    inner = (silu * up).astype(bf16)
    back = dot(pg, wd_ref[0], 1, 1)
    dgate = (back * up * sigma * (1.0 + gate * (1.0 - sigma))).astype(bf16)
    dup = (back * silu).astype(bf16)
    cut = min(D, 1024)
    weight = rg_ref[0, :, 0:1]
    both = jnp.concatenate([dgate, dup], axis=1)
    ff = dgate.shape[1]
    first = pl.program_id(1) == 0

    def put(ref, ix, value):
        if pl.num_programs(1) == 1:
            ref[ix] = value
        else:
            ref[ix] = value + jnp.where(first, 0.0, ref[ix])

    for n in range(0, D, cut):
        c = slice(n, n + cut)
        y_ref[0, :, c] = (dot(inner, wd_ref[0, :, c], 1, 0) * weight).astype(bf16)
        dx_ref[0, :, c] = (dot(dgate, wg_ref[0, c, :], 1, 1) + dot(dup, wu_ref[0, c, :], 1, 1)).astype(bf16)
        d = dot(x_ref[0, :, c], both, 0, 0)
        put(dwg_ref, (0, c, slice(None)), d[:, :ff])
        put(dwu_ref, (0, c, slice(None)), d[:, ff:])
        put(dwd_ref, (0, slice(None), c), dot(inner, pg_ref[0, :, c], 0, 0))


def expert_layer(x, pg, rg, wg, wu, wd):
    rows = x.shape[1]
    step = 640 if rows % 640 == 0 else rows
    some = lambda a: pl.BlockSpec((1, step) + a.shape[2:], lambda e, i: (e, i, 0))
    whole = lambda a: pl.BlockSpec((1,) + a.shape[1:], lambda e, i: (e, 0, 0))
    sds = jax.ShapeDtypeStruct
    return pl.pallas_call(
        expert_kernel,
        grid=(x.shape[0], rows // step),
        in_specs=[some(a) for a in (x, pg, rg)] + [whole(a) for a in (wg, wu, wd)],
        out_specs=[some(a) for a in (x, x)] + [whole(a) for a in (wg, wu, wd)],
        out_shape=[sds(x.shape, x.dtype)] * 2 + [sds(a.shape, jnp.float32) for a in (wg, wu, wd)],
        compiler_params=pltpu.CompilerParams(vmem_limit_bytes=62 * 2**20),
    )(x, pg, rg, wg, wu, wd)


def middle_kernel(res_ref, gain_ref, grad_ref, cot_ref, att_ref, w_ref, back_ref, gain_out_ref, heads_ref, part_ref, low_ref):
    f32, bf16 = jnp.float32, jnp.bfloat16

    @pl.when(pl.program_id(0) == 0)
    def _():
        u = res_ref[...]
        r = lax.rsqrt(jnp.mean(u * u, axis=-1, keepdims=True) + EPSILON)
        norm = u * r
        w = grad_ref[...]
        gain_out_ref[...] = jnp.broadcast_to(jnp.sum(w * norm, axis=0, keepdims=True), gain_out_ref.shape)
        m = w * gain_ref[...]
        back = cot_ref[...].astype(f32) + r * (m - norm * jnp.mean(m * norm, axis=-1, keepdims=True))
        back_ref[...] = back
        low_ref[...] = back.astype(bf16)

    low = low_ref[...]
    seqs, heads, positions, _ = heads_ref.shape
    grad = dot(low, w_ref[...], 1, 1).astype(bf16)
    for s in range(seqs):
        for h in range(heads):
            heads_ref[s, h] = grad[s * positions:(s + 1) * positions, h * HD:(h + 1) * HD]
    part_ref[...] = dot(att_ref[...], low, 0, 0).astype(bf16)


def middle(residual, gain, normed_grad, cot, attended, out_w, seqs):
    T, D = residual.shape
    features = attended.shape[1]
    cut = 512
    whole = lambda n: (0, 0)
    sds, f32, bf16 = jax.ShapeDtypeStruct, jnp.float32, jnp.bfloat16
    full = pl.BlockSpec((T, D), whole)
    rows = pl.BlockSpec((cut, D), lambda n: (n, 0))
    return pl.pallas_call(
        middle_kernel,
        grid=(features // cut,),
        in_specs=[full, pl.BlockSpec((1, D), whole), full, full, pl.BlockSpec((T, cut), lambda n: (0, n)), rows],
        out_specs=[full, pl.BlockSpec((8, D), whole),
                   pl.BlockSpec((seqs, cut // HD, T // seqs, HD), lambda n: (0, n, 0, 0)), rows],
        out_shape=[sds((T, D), f32), sds((8, D), f32), sds((seqs, features // HD, T // seqs, HD), bf16),
                   sds((features, D), bf16)],
        scratch_shapes=[pltpu.VMEM((T, D), bf16)],
        compiler_params=pltpu.CompilerParams(vmem_limit_bytes=58 * 2**20),
    )(residual, gain, normed_grad, cot, attended, out_w)


def close_kernel(x_ref, w_ref, own_ref, other_ref, back_ref, tok_ref, gain_ref, q_ref, k_ref, v_ref, in_ref):
    f32 = jnp.float32
    for h in range(w_ref.shape[0]):
        for n, ref in enumerate((q_ref, k_ref, v_ref)):
            ref[:, h * HD:(h + 1) * HD] = w_ref[h, :, n * HD:(n + 1) * HD].astype(f32)
    here = x_ref[0]
    for s in (0, 1):
        grad = jnp.where(here == s, own_ref[...], other_ref[...].astype(f32))
        tok = tok_ref[s].astype(f32)
        inv = lax.rsqrt(jnp.mean(tok * tok, axis=-1, keepdims=True) + EPSILON)
        norm = tok * inv
        m = grad * gain_ref[...]
        in_ref[s] = back_ref[s] + inv * (m - norm * jnp.mean(m * norm, axis=-1, keepdims=True))


def close(here, weight_grad, own, other, back, tok, gain):
    heads, W, _ = weight_grad.shape
    vmem = pl.BlockSpec(memory_space=pltpu.VMEM)
    sds = jax.ShapeDtypeStruct
    return pl.pallas_call(
        close_kernel,
        in_specs=[pl.BlockSpec(memory_space=pltpu.SMEM)] + [vmem] * 6,
        out_specs=[vmem] * 4,
        out_shape=[sds((W, heads * HD), jnp.float32)] * 3 + [sds(tok.shape, jnp.float32)],
        compiler_params=pltpu.CompilerParams(vmem_limit_bytes=32 * 2**20),
    )(here, weight_grad, own, other, back, tok, gain)


def body(tokens, w_query, w_key, w_value, w_out, attn_gain, ffn_gain, qk_gain,
         expert_gate, expert_up, expert_down, routes, gates, order, cotangent):
    f32, bf16 = jnp.float32, jnp.bfloat16
    positions, seqs, D = tokens.shape
    U, B = lax.axis_size("ulysses"), lax.axis_size("blk")
    F = U * B
    u, b = lax.axis_index("ulysses"), lax.axis_index("blk")
    H = w_query.shape[1] // HD
    W = w_query.shape[0]
    L = F * positions
    T = seqs * positions
    top_count = routes.shape[-1]
    local_experts = expert_gate.shape[0]
    E = local_experts * B
    R = 2 * B // H
    x_here = u // 2
    first_copy = lax.rem((u % 2) * B + b, R) == 0

    tok = tokens.transpose(1, 0, 2)
    cot = cotangent.transpose(1, 0, 2)
    rows_f = tok.reshape(T, D).astype(f32)

    expert_of = routes.transpose(1, 0, 2).reshape(-1)
    prio = order.reshape(positions, seqs, top_count).transpose(1, 0, 2).reshape(-1)
    same = expert_of[:, None] == expert_of[None, :]
    ranks = jnp.sum((same & (prio[None, :] < prio[:, None])).astype(jnp.int32), axis=1)
    slot = jnp.where(ranks < CAP, expert_of * CAP + ranks, -1).astype(f32)
    pairs = slot.shape[0]

    nq = qk_gain.shape[1]
    small = jnp.concatenate(
        [slot, gates.transpose(1, 0, 2).reshape(-1)]
        + [g.astype(f32) for g in (attn_gain, ffn_gain, qk_gain[0], qk_gain[1])])
    small = jnp.pad(small, (0, -small.shape[0] % 1024)).reshape(-1, 128)
    seq_tok, table, head_w = front(tok, small, (w_query, w_key, w_value), HD, R, U, B, 1)
    seq_tok, head_w = seq_tok.reshape(L, D), head_w.reshape(D, 3 * HD)
    out_w = lax.all_gather(w_out, AXES, axis=0, tiled=True)
    cot_all = lax.all_gather(cot, AXES, axis=0)
    table = table.reshape(F, -1)
    cut = 2 * pairs
    attn_g = table[:, cut:cut + W].reshape(1, D)
    ffn_g = table[:, cut + W:cut + 2 * W].reshape(1, D)
    cut = cut + 2 * W
    qk_g = jnp.stack([table[:, cut:cut + nq].reshape(-1), table[:, cut + nq:cut + 2 * nq].reshape(-1)])

    groups = (U // 2, 2, B // 2, 2)
    GB = 4
    G, KB = F // GB, GB * T
    RB = -(-GB * CAP // 16) * 16
    slot_all = table[:, :pairs].astype(jnp.int32).reshape(F, T, top_count)
    gate_all = table[:, pairs:2 * pairs].reshape(F, T, top_count)
    place = ((np.arange(F) // B % 2) * 2 + np.arange(F) % 2).astype(np.int32)
    base = (b * local_experts + jnp.arange(local_experts, dtype=jnp.int32)) * CAP
    off = slot_all[:, :, :, None] - base
    mine = (off >= 0) & (off < CAP)
    val = jnp.sum(jnp.where(mine, off + 1, 0), axis=2)
    val = jnp.where(val > 0, val - 1 + jnp.asarray(place)[:, None, None] * CAP, -1)
    gate_of = jnp.sum(jnp.where(mine, gate_all[:, :, :, None], 0.0), axis=2)

    def by_group(m):
        return m.reshape(groups + (T, local_experts)).transpose(0, 2, 5, 1, 3, 4).reshape(G, local_experts, KB)

    val, gate_of = by_group(val), by_group(gate_of)

    inverse = (ROPE_BASE ** (-2.0 * np.arange(HD // 2) / HD)).astype(np.float32)
    angles = np.arange(L).astype(np.float32)[:, None] * inverse[None, :]
    cosine = jnp.asarray(np.concatenate([np.cos(angles)] * 2, axis=1).astype(np.float32))
    sine = jnp.asarray(np.concatenate([-np.sin(angles), np.sin(angles)], axis=1).astype(np.float32))
    q, k, v, kt, vt, raw_q, raw_k = project(seq_tok, attn_g, head_w, qk_g, cosine, sine)
    att_rows, lse = attend(q, k, vt, positions, U, B, 5)

    def from_heads(m):
        m = m.reshape(2, 2 * B, positions, HD).transpose(0, 2, 1, 3)
        return m.reshape(2, positions, H, R, HD)[:, :, :, 0].reshape(T, H * HD)

    attended = from_heads(att_rows)
    residual = rows_f + jnp.dot(attended, out_w, preferred_element_type=f32)
    normed = rms_norm(residual, ffn_g).astype(bf16).reshape(2, positions, D)

    normed_all, hot, row_gate = gather_blocks(normed, val, gate_of, RB, U, B, 2)
    shape = groups + (T, D)
    normed_all, cot_all = normed_all.reshape(shape), cot_all.reshape(shape)
    weights = (expert_gate, expert_up, expert_down)
    x, pair_grad = dispatch(hot, row_gate, normed_all, cot_all)
    y, dx, gate_grad, up_grad, down_grad = expert_layer(x, pair_grad, row_gate, *weights)
    normed_grad, mixed_sum = scatter_pair(dx, y, hot, positions, U, B, 3)
    mixed = (residual + mixed_sum.reshape(T, D)).reshape(2, positions, D).transpose(1, 0, 2).astype(bf16)
    normed_grad = normed_grad.reshape(T, D)

    residual_grad, ffn_gain_part, att_grad, out_part = middle(
        residual, ffn_g, normed_grad, cot.reshape(T, D), attended, out_w, seqs)
    att_grad = jnp.repeat(att_grad, R, axis=1).reshape(F, positions, HD)
    out_part = out_part.reshape(F, 2, W // 2, D)
    dq, dk, dv = attend_back(att_grad, q, lse, k, kt, v, U, B, 6)
    if R > 1:
        dq, dk, dv = (jnp.where(first_copy, m, 0.0) for m in (dq, dk, dv))
    hidden_part, weight_part, qk_part, attn_gain_part = head_back(
        dq, dk, dv, raw_q, raw_k, cosine, sine, qk_g, seq_tok, attn_g, head_w)
    weight_part = weight_part.reshape(F, W, 3 * HD)
    small = jnp.concatenate(
        [attn_gain_part[0].reshape(F, W), ffn_gain_part[0].reshape(F, W),
         qk_part[0].reshape(F, nq), qk_part[1].reshape(F, nq)], axis=1)
    small = jnp.pad(small, ((0, 0), (0, -small.shape[1] % 1024))).reshape(F, -1, 128)
    weight_grad, small, own, other, out_grad = finish(
        weight_part, small, hidden_part.reshape(F, positions, D), out_part, U, B, 4)
    small = jnp.sum(small, axis=0).reshape(-1)
    if R > 1:
        weight_grad = weight_grad.reshape(H, R, W, 3 * HD).astype(f32).sum(axis=1)
    query_grad, key_grad, value_grad, input_grad = close(
        x_here.reshape(1), weight_grad, own, other, residual_grad.reshape(2, positions, D), tok, attn_g)
    input_grad = input_grad.transpose(1, 0, 2)
    out_grad = out_grad.reshape(W, D)
    return (
        mixed, input_grad, query_grad, key_grad, value_grad, out_grad,
        small[:W], small[W:2 * W], small[2 * W:2 * W + 2 * nq].reshape(2, nq),
        gate_grad, up_grad, down_grad,
    )


def solution(mesh):
    rows = P(AXES, None, None)
    flat = P(AXES, None)
    by_expert = (P("blk", None, "ulysses"), P("blk", None, "ulysses"), P("blk", "ulysses", None))
    in_specs = (rows, flat, flat, flat, flat, P(AXES), P(AXES), P(None, AXES)) + by_expert + (rows, rows, flat, rows)
    out_specs = (rows, rows, flat, flat, flat, flat, P(AXES), P(AXES), P(None, AXES)) + by_expert
    return jax.shard_map(body, mesh=mesh, in_specs=in_specs, out_specs=out_specs, check_vma=False)
```

```python
import functools
import math

import jax
import jax.numpy as jnp
import numpy as np
from jax import lax
from jax.experimental import pallas as pl
from jax.experimental.pallas import tpu as pltpu
from jax.sharding import PartitionSpec as P

HD = 128
CAP = 18
EPSILON = 1e-06
ROPE_BASE = 10000.0
AXES = ("ulysses", "blk")
MESH = pl.DeviceIdType.MESH


class Place:
    def __init__(self, U, B):
        self.U, self.B = U, B
        self.X, self.Y = U // 2, 2
        self.Z = B // self.Y
        self.Q, self.F = self.X * B, U * B
        u, b = lax.axis_index("ulysses"), lax.axis_index("blk")
        self.c, self.x = lax.rem(u, 2), lax.div(u, 2)
        self.y, self.z = lax.rem(b, self.Y), lax.div(b, self.Y)
        self.r = self.c * B + b
        self.me = u * B + b
        self.core_peer = self.dev(self.x, self.y, self.z, 1 - self.c)
        self.x_peer = self.dev(1 - self.x, self.y, self.z, self.c)

    def dev(self, x, y, z, c):
        return (x * 2 + c, z * self.Y + y)

    def block(self, x, y, z, c):
        return (x * 2 + c) * self.B + z * self.Y + y

    def chip(self, x, y, z):
        return x * self.B + z * self.Y + y

    def at(self, r, x):
        return x * 2 * self.B + r

    def plane_dev(self, r):
        return (self.x * 2 + lax.div(r, self.B), lax.rem(r, self.B))

    def flat_dev(self, f):
        return (lax.div(f, self.B), lax.rem(f, self.B))

    def others(self, axis):
        n = {"x": self.X, "y": self.Y, "z": self.Z}[axis]
        i = {"x": self.x, "y": self.y, "z": self.z}[axis]
        return [lax.rem(i + o, n) for o in range(1, n)]

    def far_first(self):
        table = [sorted((k for k in range(self.Z) if k != z), key=lambda k: (-abs(k - z), -k)) for z in range(self.Z)]
        out = []
        for n in range(self.Z - 1):
            k = 0
            for z in range(self.Z):
                k = k + jnp.where(self.z == z, table[z][n], 0)
            out.append(k)
        return out + [self.z]

    def barrier(self, reach):
        sem = pltpu.get_barrier_semaphore()

        def greet(d):
            pl.semaphore_signal(sem, inc=1, device_id=d, device_id_type=MESH)

        if reach == "every":
            @pl.loop(1, self.F)
            def _(o):
                greet(self.flat_dev(lax.rem(self.me + o, self.F)))

            pl.semaphore_wait(sem, self.F - 1)
            return
        if reach == "plane":
            greet(self.x_peer)

            @pl.loop(1, 2 * self.B)
            def _(o):
                greet(self.plane_dev(lax.rem(self.r + o, 2 * self.B)))

            pl.semaphore_wait(sem, 2 * self.B)
            return
        greet(self.core_peer)
        for k in self.others("x"):
            greet(self.dev(k, self.y, self.z, self.c))
        for k in self.others("y"):
            greet(self.dev(self.x, k, self.z, self.c))
        count = self.X + self.Y - 1
        if reach == "chain":
            below, above = self.z > 0, self.z < self.Z - 1

            @pl.when(below)
            def _():
                greet(self.dev(self.x, self.y, self.z - 1, self.c))

            @pl.when(above)
            def _():
                greet(self.dev(self.x, self.y, self.z + 1, self.c))

            count = count + jnp.where(below, 1, 0) + jnp.where(above, 1, 0)
        else:
            for k in self.others("z"):
                greet(self.dev(self.x, self.y, k, self.c))
            count += self.Z - 1
        pl.semaphore_wait(sem, count)


def remote(src, dst, send, recv, dev):
    return pltpu.make_async_remote_copy(
        src_ref=src, dst_ref=dst, send_sem=send, recv_sem=recv, device_id=dev, device_id_type=MESH)


class Gather:
    def __init__(self, p, src, out, send_sem, recv_sem, local_sem, like=(0, 1)):
        self.p, self.src, self.out, self.like = p, src, out, like
        self.send_sem, self.recv_sem, self.local_sem = send_sem, recv_sem, local_sem
        self.steps = p.Z + 2
        self.started = []
        self.always = p.z >= 0

    @staticmethod
    def semaphores(U, B):
        dma = pltpu.SemaphoreType.DMA
        return [dma((4 + U // 2, 2, U * B)), dma((2, U * B)), dma((1,))]

    def where(self, half, x, y, z):
        f = self.p.block(x, y, z, self.p.c)
        return self.out.at[f, half], (half, f)

    def send(self, cond, src_ref, dst_ref, ix, way, dev):
        cp = remote(src_ref, dst_ref, self.send_sem.at[(way,) + ix], self.recv_sem.at[ix], dev)

        @pl.when(cond)
        def _():
            cp.start()

        self.started.append((cond, cp))

    def wait(self, ref, ix):
        remote(ref, ref, self.send_sem.at[(0,) + ix], self.recv_sem.at[ix], self.p.core_peer).wait_recv()

    def along(self, cond, half, x, y, z, axes):
        p = self.p
        ref, ix = self.where(half, x, y, z)
        for ax in axes:
            if ax == "core":
                self.send(cond, ref, ref, ix, 0, p.core_peer)
            elif ax == "up":
                self.send(cond & (p.z < p.Z - 1), ref, ref, ix, 1, p.dev(p.x, p.y, p.z + 1, p.c))
            elif ax == "down":
                self.send(cond & (p.z > 0), ref, ref, ix, 2, p.dev(p.x, p.y, p.z - 1, p.c))
            elif ax == "y":
                for i, k in enumerate(p.others("y")):
                    self.send(cond, ref, ref, ix, 3 + i, p.dev(p.x, k, p.z, p.c))
            else:
                for i, k in enumerate(p.others("x")):
                    self.send(cond, ref, ref, ix, 2 + p.Y + i, p.dev(k, p.y, p.z, p.c))

    def zs(self, step):
        p = self.p
        if step == 0:
            return [(self.always, p.z, ())]
        return [(p.z - step >= 0, p.z - step, ("up",)), (p.z + step < p.Z, p.z + step, ("down",))]

    def arrive(self, cond, half, x, y, z, axes):
        ref, ix = self.where(half, x, y, z)

        @pl.when(cond)
        def _():
            self.wait(ref, ix)

        self.along(cond, half, x, y, z, axes)

    def step(self, n):
        p = self.p
        if n == 0:
            cp = pltpu.make_async_copy(self.src, self.out.at[p.me], self.local_sem.at[0])
            cp.start()
            cp.wait()
            for half in (0, 1):
                self.along(self.always, half, p.x, p.y, p.z, ("up", "down", "y", "x"))
            for half in (0, 1):
                self.along(self.always, half, p.x, p.y, p.z, ("core",))
            return
        if n < p.Z:
            for half in (0, 1):
                for cond, k, on in self.zs(n):
                    self.arrive(cond, half, p.x, p.y, k, on + ("y", "x", "core"))
        if n <= p.Z:
            for cond, k, _ in self.zs(n - 1):
                for half, way in enumerate(self.like):
                    if way == 0:
                        for i in p.others("y"):
                            self.arrive(cond, half, p.x, i, k, ("x", "core"))
                    else:
                        for j in p.others("x"):
                            self.arrive(cond, half, j, p.y, k, ("y", "core"))
        if n >= 2:
            for cond, k, _ in self.zs(n - 2):
                for half, way in enumerate(self.like):
                    if way == 0:
                        for j in p.others("x"):
                            self.arrive(cond, half, j, p.y, k, ("core",))
                    else:
                        for i in p.others("y"):
                            self.arrive(cond, half, p.x, i, k, ("core",))
                for half in (0, 1):
                    for j in p.others("x"):
                        for i in p.others("y"):
                            self.arrive(cond, half, j, i, k, ("core",))

    def end(self):
        p = self.p
        for k in range(p.Z):
            for j in range(p.X):
                for i in range(p.Y):
                    f = p.block(j, i, k, 1 - p.c)
                    for half in (0, 1):
                        self.wait(self.out.at[f, half], (half, f))
        for cond, cp in self.started:
            @pl.when(cond)
            def _(cp=cp):
                cp.wait_send()


class PlaneGather(Gather):
    def __init__(self, *a):
        super().__init__(*a)
        self.steps = self.p.Z + 1

    @staticmethod
    def semaphores(U, B):
        dma = pltpu.SemaphoreType.DMA
        return [dma((5, 1, U * B)), dma((1, U * B)), dma((1,))]

    def where(self, half, x, y, z):
        f = self.p.block(half, y, z, self.p.c)
        return self.out.at[f], (0, f)

    def step(self, n):
        p = self.p
        if n == 0:
            cp = pltpu.make_async_copy(self.src.at[p.x], self.out.at[p.me], self.local_sem.at[0])
            cp.start()
            self.send(self.always, self.src.at[1 - p.x], self.out.at[p.me], (0, p.me), 4, p.x_peer)
            cp.wait()
            self.along(self.always, p.x, p.x, p.y, p.z, ("up", "down", "y", "core"))
            self.arrive(self.always, 1 - p.x, p.x, p.y, p.z, ("up", "down", "y", "core"))
            return
        if n < p.Z:
            for half in (0, 1):
                for cond, k, on in self.zs(n):
                    self.arrive(cond, half, p.x, p.y, k, on + ("y", "core"))
        for half in (0, 1):
            for cond, k, _ in self.zs(n - 1):
                for i in p.others("y"):
                    self.arrive(cond, half, p.x, i, k, ("core",))

    def end(self):
        p = self.p
        for k in range(p.Z):
            for i in range(p.Y):
                for half in (0, 1):
                    f = p.block(half, i, k, 1 - p.c)
                    self.wait(self.out.at[f], (0, f))
        for cond, cp in self.started:
            @pl.when(cond)
            def _(cp=cp):
                cp.wait_send()


class Spread:
    def __init__(self, p, parts, out, send_sem, recv_sem, over_sem):
        self.p, self.parts, self.out = p, parts, out
        self.send_sem, self.recv_sem, self.over_sem = send_sem, recv_sem, over_sem

    @staticmethod
    def semaphores(U, B, n):
        dma = pltpu.SemaphoreType.DMA
        return [dma((n, 2 * B)), dma((n, 2 * B)), dma((2, 2 * B))]

    def out_to(self, o):
        p = self.p
        r = lax.rem(p.r + o, 2 * p.B)
        return [remote(src, self.out.at[(p.me,) + at], self.send_sem.at[n, r], self.recv_sem.at[n, p.r], p.plane_dev(r))
                for n, (src, at) in enumerate(self.parts(r))]

    def across(self, r):
        f = self.p.at(r, self.p.x)
        return remote(self.out.at[f], self.out.at[f], self.over_sem.at[0, r], self.over_sem.at[1, r], self.p.x_peer)

    def begin(self):
        p = self.p

        @pl.loop(1, 2 * p.B)
        def _(o):
            for cp in self.out_to(o):
                cp.start()

        mine = [pltpu.make_async_copy(src, self.out.at[(p.me,) + at], self.send_sem.at[n, p.r])
                for n, (src, at) in enumerate(self.parts(p.r))]
        for cp in mine:
            cp.start()
        for cp in mine:
            cp.wait()
        self.across(p.r).start()

    def middle(self):
        p = self.p

        @pl.loop(1, 2 * p.B)
        def _(o):
            r = lax.rem(p.r + o, 2 * p.B)
            for n, (_, at) in enumerate(self.parts(r)):
                ref = self.out.at[(p.at(r, p.x),) + at]
                remote(ref, ref, self.send_sem.at[n, 0], self.recv_sem.at[n, r], p.x_peer).wait_recv()
            self.across(r).start()

    def end(self):
        p = self.p

        @pl.loop(0, 2 * p.B)
        def _(r):
            f = p.at(r, 1 - p.x)
            remote(self.out.at[f], self.out.at[f], self.over_sem.at[0, 0], self.over_sem.at[1, r], p.x_peer).wait_recv()
            self.across(r).wait_send()

        @pl.loop(1, 2 * p.B)
        def _(o):
            for cp in self.out_to(o):
                cp.wait_send()


def any_specs(n):
    return [pl.BlockSpec(memory_space=pl.ANY)] * n


def gather_kernel(U, B, experts, RB, src, val, gate, out, hot_out, rg_out, send, recv, local, hot, rg, store):
    p = Place(U, B)
    p.barrier("chain")
    g = Gather(p, src, out, send, recv, local)
    G, _, KB = val.shape
    per = -(-G // (g.steps - 2))
    at = lax.broadcasted_iota(jnp.int32, (RB, KB), 0)
    saves = [pltpu.make_async_copy(hot, hot_out, store.at[0]), pltpu.make_async_copy(rg, rg_out, store.at[1])]
    for n in range(g.steps):
        g.step(n)

        @pl.loop(min(n * per, G), min((n + 1) * per, G))
        def _(m):
            for e in range(experts):
                hit = at == val[m, e:e + 1, :]
                hot[m, e * RB:(e + 1) * RB, :] = jnp.where(hit, 1.0, 0.0).astype(hot.dtype)
                w = jnp.sum(jnp.where(hit, gate[m, e:e + 1, :], 0.0), axis=1, keepdims=True)
                rg[e, pl.ds(pl.multiple_of(m * RB, RB), RB), :] = jnp.broadcast_to(w, (RB, 128))

        if n == g.steps - 2:
            for cp in saves:
                cp.start()
    g.end()
    for cp in saves:
        cp.wait()


def gather_blocks(v, val, gate, RB, U, B, cid):
    G, experts, KB = val.shape
    sds = jax.ShapeDtypeStruct
    vmem = pl.BlockSpec(memory_space=pltpu.VMEM)
    hot, rg = sds((G, experts * RB, KB), jnp.bfloat16), sds((experts, G * RB, 128), jnp.float32)
    return pl.pallas_call(
        functools.partial(gather_kernel, U, B, experts, RB),
        out_shape=[sds((U * B,) + v.shape, v.dtype), hot, rg],
        in_specs=any_specs(1) + [vmem, vmem],
        out_specs=any_specs(3),
        scratch_shapes=Gather.semaphores(U, B) + [
            pltpu.VMEM(hot.shape, hot.dtype), pltpu.VMEM(rg.shape, rg.dtype), pltpu.SemaphoreType.DMA((2,))],
        compiler_params=pltpu.CompilerParams(
            collective_id=cid, has_side_effects=True, vmem_limit_bytes=62 * 2**20),
    )(v, val, gate)


def front_kernel(U, B, width, copies, tok, small, wq, wk, wv, tok_out, small_out, weights_out, *sems):
    p = Place(U, B)
    p.barrier("plane")
    g = PlaneGather(p, tok, tok_out, *sems[:3])
    s = Spread(p, lambda r: [(small, ())], small_out, *sems[3:6])
    every = slice(None)

    def columns(r):
        h = lax.div(r, copies)
        cols = pl.ds(pl.multiple_of(h * width, width), width)
        return [(m.at[:, cols], (every, slice(n * width, (n + 1) * width))) for n, m in enumerate((wq, wk, wv))]

    w = Spread(p, columns, weights_out, *sems[6:9])
    s.begin()
    g.step(0)
    w.begin()
    for n in range(1, g.steps):
        g.step(n)
        if n == 1:
            s.middle()
            w.middle()
    s.end()
    w.end()
    g.end()


def front(tok, small, weights, width, copies, U, B, cid):
    F = U * B
    rows = weights[0].shape[0]
    shapes = [((F,) + tok.shape[1:], tok.dtype), ((F,) + small.shape, small.dtype), ((F, rows, 3 * width), weights[0].dtype)]
    return pl.pallas_call(
        functools.partial(front_kernel, U, B, width, copies),
        out_shape=[jax.ShapeDtypeStruct(*m) for m in shapes],
        in_specs=any_specs(5),
        out_specs=any_specs(3),
        scratch_shapes=PlaneGather.semaphores(U, B) + Spread.semaphores(U, B, 1) + Spread.semaphores(U, B, 3),
        compiler_params=pltpu.CompilerParams(collective_id=cid, has_side_effects=True),
    )(tok, small, *weights)


class Scatter:
    def __init__(self, p, acc, rc, rx0, rx1, ry0, ry1, rz, fin, loc, cs, cr, xs, xr, ys, yr, zs, zr, like=(0, 1), chain=False):
        self.p, self.like, self.chain = p, like, chain
        self.acc, self.rc, self.rx, self.ry, self.rz, self.fin = acc, rc, (rx0, rx1), (ry0, ry1), rz, fin
        self.loc, self.cs, self.cr = loc, cs, cr
        self.xs, self.xr, self.ys, self.yr, self.zs, self.zr = xs, xr, ys, yr, zs, zr
        self.order = p.far_first() if chain else p.others("z") + [p.z]
        self.steps = p.Z + 2
        self.started, self.maybe = [], []
        self.local = True

    @staticmethod
    def scratch(U, B, rows, D, t, like=(0, 1), chain=False):
        X, Y, Z, Q = U // 2, 2, B // 2, U * B // 2
        dma = pltpu.SemaphoreType.DMA
        x, y = max(X - 1, 1), Y - 1
        return [
            pltpu.VMEM((Q, 2, rows, D), t),
            pltpu.VMEM((Q, 2, rows, D), t),
            pltpu.VMEM((x, Z * Y, rows, D), t),
            pltpu.VMEM((x, Z if like[1] else Z * Y, rows, D), t),
            pltpu.VMEM((y, Z, rows, D), t),
            pltpu.VMEM((y, Z * X if like[1] else Z, rows, D), t),
            pltpu.VMEM((2, 2, Z, rows, D) if chain else (2, Z, rows, D), t),
            pltpu.VMEM((2, rows, D), jnp.float32),
            dma((Q, 2)),
            dma((Q, 2)),
            dma((Q, 2)),
            dma((2, x, Z * Y)),
            dma((2, x, Z * Y)),
            dma((2, y, Z * X)),
            dma((2, y, Z * X)),
            dma((2, Z)),
            dma((2, 2, Z) if chain else (2, Z)),
        ]

    SCRATCH = 17

    def start(self, *a):
        cp = remote(*a)
        cp.start()
        self.started.append(cp)

    def got(self, ref, sem):
        remote(ref, ref, sem, sem, self.p.core_peer).wait_recv()

    def load(self, src):
        p = self.p
        for k in self.order:
            for j in p.others("x") + [p.x]:
                for i in range(p.Y):
                    for h in (0, 1):
                        q = p.chip(j, i, k)
                        cp = self.across(src.at[p.block(j, i, k, 1 - p.c), h], q, h)
                        cp.start()
                        self.started.append(cp)
                        self.keep(src.at[p.block(j, i, k, p.c), h], q, h).start()

    def keep(self, src, q, h):
        return pltpu.make_async_copy(src, self.acc.at[q, h], self.loc.at[q, h])

    def across(self, src, q, h):
        return remote(src, self.rc.at[q, h], self.cs.at[q, h], self.cr.at[q, h], self.p.core_peer)

    def ready(self, h, j, i, k):
        q = self.p.chip(j, i, k)
        if self.local:
            self.keep(self.acc.at[q, h], q, h).wait()
        self.got(self.rc.at[q, h], self.cr.at[q, h])
        return [self.rc.at[q, h]]

    def send_x(self, h, q, j, s):
        p = self.p
        o = lax.rem(j - p.x + p.X, p.X) - 1
        self.start(self.acc.at[q, h], self.rx[h].at[o, s], self.xs.at[h, o, s], self.xr.at[h, o, s],
                   p.dev(j, p.y, p.z, p.c))

    def send_y(self, h, q, i, s):
        p = self.p
        o = lax.rem(i - p.y + p.Y, p.Y) - 1
        self.start(self.acc.at[q, h], self.ry[h].at[o, s], self.ys.at[h, o, s], self.yr.at[h, o, s],
                   p.dev(p.x, i, p.z, p.c))

    def from_x(self, h, s):
        out = []
        for o in range(self.p.X - 1):
            self.got(self.rx[h].at[o, s], self.xr.at[h, o, s])
            out.append(self.rx[h].at[o, s])
        return out

    def from_y(self, h, s):
        out = []
        for o in range(self.p.Y - 1):
            self.got(self.ry[h].at[o, s], self.yr.at[h, o, s])
            out.append(self.ry[h].at[o, s])
        return out

    def along_z(self, n, h, q, extra):
        p = self.p
        k = self.order[n]
        here = self.acc.at[q, h]
        add(here, extra)
        for way, cond in enumerate(((k >= p.z) & (p.z > 0), (k <= p.z) & (p.z < p.Z - 1))):
            @pl.when(cond)
            def _(way=way):
                self.got(self.rz.at[way, h, k], self.zr.at[way, h, k])
                add(here, [self.rz.at[way, h, k]])
        if n == p.Z - 1:
            add(here, [], self.fin.at[h])
            return
        for way, cond, z in ((0, k > p.z, p.z + 1), (1, k < p.z, p.z - 1)):
            cp = remote(here, self.rz.at[way, h, k], self.zs.at[h, k], self.zr.at[way, h, k], p.dev(p.x, p.y, z, p.c))

            @pl.when(cond)
            def _(cp=cp):
                cp.start()

            self.maybe.append((cond, cp))

    def last(self, n, h, q, extra):
        p = self.p
        if self.chain:
            self.along_z(n, h, q, extra)
            return
        k = self.order[n]
        if n < p.Z - 1:
            add(self.acc.at[q, h], extra)
            self.start(self.acc.at[q, h], self.rz.at[h, p.z], self.zs.at[h, k], self.zr.at[h, p.z],
                       p.dev(p.x, p.y, k, p.c))
        else:
            for a in p.others("z"):
                self.got(self.rz.at[h, a], self.zr.at[h, a])
                extra.append(self.rz.at[h, a])
            add(self.acc.at[q, h], extra, self.fin.at[h])

    def first(self, n, j):
        p = self.p
        k = self.order[n]
        for h, way in enumerate(self.like):
            if way == 0 and j is not p.x:
                for i in range(p.Y):
                    q = p.chip(j, i, k)
                    add(self.acc.at[q, h], self.ready(h, j, i, k))
                    self.send_x(h, q, j, k * p.Y + i)
            if way == 1:
                for i in p.others("y"):
                    q = p.chip(j, i, k)
                    add(self.acc.at[q, h], self.ready(h, j, i, k))
                    self.send_y(h, q, i, k * p.X + j)

    def rest(self, n):
        p = self.p
        X, Y, Z = p.X, p.Y, p.Z
        if 1 <= n <= Z:
            k = self.order[n - 1]
            for h, way in enumerate(self.like):
                if way == 0:
                    for i in p.others("y"):
                        q = p.chip(p.x, i, k)
                        add(self.acc.at[q, h], self.ready(h, p.x, i, k) + self.from_x(h, k * Y + i))
                        self.send_y(h, q, i, k)
                else:
                    for j in p.others("x"):
                        q = p.chip(j, p.y, k)
                        add(self.acc.at[q, h], self.ready(h, j, p.y, k) + self.from_y(h, k * X + j))
                        self.send_x(h, q, j, k)
        if n >= 2:
            k = self.order[n - 2]
            q = p.chip(p.x, p.y, k)
            for h, way in enumerate(self.like):
                extra = self.ready(h, p.x, p.y, k)
                if way == 0:
                    extra = extra + self.from_x(h, k * Y + p.y) + self.from_y(h, k)
                else:
                    extra = extra + self.from_y(h, k * X + p.x) + self.from_x(h, k)
                self.last(n - 2, h, q, extra)

    def step(self, n):
        if n < self.p.Z:
            for j in self.p.others("x") + [self.p.x]:
                self.first(n, j)
        self.rest(n)

    def sent(self):
        for cp in self.started:
            cp.wait_send()
        for cond, cp in self.maybe:
            @pl.when(cond)
            def _(cp=cp):
                cp.wait_send()


def add(dst, srcs, f32_out=None):
    step = 16

    def one(n, _):
        r = pl.ds(pl.multiple_of(n * step, step), step)
        t = dst[r, :].astype(jnp.float32)
        for s in srcs:
            t = t + s[r, :].astype(jnp.float32)
        if f32_out is None:
            dst[r, :] = t.astype(dst.dtype)
        else:
            f32_out[r, :] = t
        return 0

    lax.fori_loop(0, dst.shape[0] // step, one, 0)


class PlaneScatter(Scatter):
    def __init__(self, p, acc, rc, ry, rz, fin, loc, cs, cr, ys, yr, zs, zr):
        self.p = p
        self.acc, self.rc, self.rz, self.fin, self.ry = acc, rc, rz, fin, (ry.at[0], ry.at[1])
        self.loc, self.cs, self.cr = loc, cs, cr
        self.ys, self.yr, self.zs, self.zr = ys, yr, zs, zr
        self.chain = True
        self.order = p.far_first()
        self.steps = p.Z + 1
        self.started, self.maybe = [], []
        self.local = True

    @staticmethod
    def scratch(U, B, rows, D, t):
        Y, Z = 2, B // 2
        dma = pltpu.SemaphoreType.DMA
        return [
            pltpu.VMEM((B, 2, rows, D), t),
            pltpu.VMEM((B, 2, rows, D), t),
            pltpu.VMEM((2, Y - 1, Z, rows, D), t),
            pltpu.VMEM((2, 2, Z, rows, D), t),
            pltpu.VMEM((2, rows, D), jnp.float32),
            dma((B, 2)),
            dma((B, 2)),
            dma((B, 2)),
            dma((2, Y - 1, Z)),
            dma((2, Y - 1, Z)),
            dma((2, Z)),
            dma((2, 2, Z)),
        ]

    SCRATCH = 12

    def load(self, src):
        p = self.p
        for k in self.order:
            for i in p.others("y") + [p.y]:
                for h in (0, 1):
                    q = p.chip(0, i, k)
                    cp = self.across(src.at[p.block(h, i, k, 1 - p.c)], q, h)
                    cp.start()
                    self.started.append(cp)
                    self.keep(src.at[p.block(h, i, k, p.c)], q, h).start()

    def step(self, n):
        p = self.p
        if n < p.Z:
            k = self.order[n]
            for i in p.others("y"):
                q = p.chip(0, i, k)
                for h in (0, 1):
                    add(self.acc.at[q, h], self.ready(h, 0, i, k))
                    self.send_y(h, q, i, k)
        if n >= 1:
            k = self.order[n - 1]
            q = p.chip(0, p.y, k)
            for h in (0, 1):
                self.last(n - 1, h, q, self.ready(h, 0, p.y, k) + self.from_y(h, k))


def keep_sum(fin, out, sem):
    cp = pltpu.make_async_copy(fin, out, sem)
    cp.start()
    cp.wait()


class Combine:
    def __init__(self, s, rows_in, hot_in, cols, rows_buf, hot_buf, stage, sems):
        self.s, self.p = s, s.p
        self.rows_in, self.hot_in, self.cols = rows_in, hot_in, cols
        self.rows_buf, self.hot_buf, self.stage, self.sems = rows_buf, hot_buf, stage, sems
        self.sent = []
        s.local = False

    def loads(self, j, k):
        g = j * self.p.Z + k
        RB = self.rows_buf.shape[1]
        rows = pl.ds(pl.multiple_of(g * RB, RB), RB)
        return (
            pltpu.make_async_copy(self.rows_in.at[:, rows, self.cols], self.rows_buf, self.sems.at[0]),
            pltpu.make_async_copy(self.hot_in.at[g], self.hot_buf, self.sems.at[1]),
        )

    def fetch(self, j, k):
        for cp in self.loads(j, k):
            cp.start()

    def make(self, j, k):
        p, s = self.p, self.s
        for cp in self.loads(j, k):
            cp.wait()
        for cp in self.sent:
            cp.wait_send()
        self.sent.clear()
        experts, RB, D = self.rows_buf.shape
        KB = self.hot_buf.shape[1]
        cut = min(D, 512)

        half = KB // 2
        t = s.acc.shape[2]

        def blocks(core, put):
            hot = self.hot_buf[:, pl.ds(pl.multiple_of(core * half, half), half)]
            for n in range(0, D, cut):
                m = lax.dot_general(hot, self.rows_buf[:, :, n:n + cut].reshape(experts * RB, cut),
                                    (((0,), (0,)), ((), ())), preferred_element_type=jnp.float32).astype(s.acc.dtype)
                for i in range(p.Y):
                    for h in (0, 1):
                        at = (i * 2 + h) * t
                        put(i, h, n, m[at:at + t])

        def away(i, h, n, m):
            self.stage[i, h, :, n:n + cut] = m

        def own(i, h, n, m):
            s.acc[p.chip(j, i, k), h, :, n:n + cut] = m

        blocks(1 - p.c, away)
        for i in range(p.Y):
            for h in (0, 1):
                cp = s.across(self.stage.at[i, h], p.chip(j, i, k), h)
                cp.start()
                self.sent.append(cp)
        blocks(p.c, own)

    def end(self):
        for cp in self.sent:
            cp.wait_send()


def pair_kernel(U, B, cols, a, b, hot, out_a, out_b, *scratch):
    p = Place(U, B)
    p.barrier("lines")
    k = Scatter.SCRATCH
    work = [Scatter(p, *scratch[k * i:k * (i + 1)]) for i in range(2)]
    feed = [Combine(s, m, hot, cols, *scratch[2 * k:2 * k + 4]) for s, m in zip(work, (a, b))]
    feed[1].sent = feed[0].sent
    xs = p.others("x") + [p.x]
    todo = [(f, j, z) for z in work[0].order for f in feed for j in xs]
    todo[0][0].fetch(*todo[0][1:])
    at = 0
    for n in range(work[0].steps):
        for s in work:
            if n < p.Z:
                for x in xs:
                    f, j, z = todo[at]
                    f.make(j, z)
                    at += 1
                    if at < len(todo):
                        todo[at][0].fetch(*todo[at][1:])
                    s.first(n, x)
            s.rest(n)
    feed[0].end()
    for s, out in zip(work, (out_a, out_b)):
        keep_sum(s.fin, out, scratch[-1].at[0])
        s.sent()


def scatter_pair(a, b, hot, rows, U, B, cid):
    F = U * B
    experts, _, D = a.shape
    G, n, KB = hot.shape
    RB = n // experts
    parts = max(1, F // 32)
    D = D // parts
    dma = pltpu.SemaphoreType.DMA

    def call(c):
        return pl.pallas_call(
            functools.partial(pair_kernel, U, B, pl.ds(c * D, D)),
            out_shape=[jax.ShapeDtypeStruct((2, rows, D), jnp.float32)] * 2,
            in_specs=any_specs(3),
            out_specs=any_specs(2),
            scratch_shapes=Scatter.scratch(U, B, rows, D, a.dtype) * 2 + [
                pltpu.VMEM((experts, RB, D), a.dtype), pltpu.VMEM((n, KB), hot.dtype),
                pltpu.VMEM((2, 2, rows, D), a.dtype), dma((2,)), dma((1,))],
            compiler_params=pltpu.CompilerParams(
                collective_id=cid, has_side_effects=True, vmem_limit_bytes=62 * 2**20),
        )(a, b, hot)

    got = [call(c) for c in range(parts)]
    return tuple(jnp.concatenate([g[i] for g in got], axis=-1) for i in range(2))


class PairExchange:
    def __init__(self, p, src, out, acc, rc, local, send, recv):
        self.p, self.src, self.out, self.acc, self.rc = p, src, out, acc, rc
        self.local, self.send, self.recv = local, send, recv

    @staticmethod
    def scratch(U, B, rows, w, t):
        dma = pltpu.SemaphoreType.DMA
        return [pltpu.VMEM((2 * B, rows, w), t), pltpu.VMEM((2 * B, rows, w), t),
                dma((1,)), dma((1 + 2 * B,)), dma((1 + 2 * B,))]

    SCRATCH = 5

    def across(self):
        p = self.p
        return remote(self.src.at[1 - p.x], self.rc, self.send.at[0], self.recv.at[0], p.x_peer)

    def own(self):
        return pltpu.make_async_copy(self.src.at[self.p.x], self.acc, self.local.at[0])

    def away(self, o):
        p = self.p
        r = lax.rem(p.r + o, 2 * p.B)
        return remote(self.acc.at[r], self.out.at[p.r], self.send.at[1 + r], self.recv.at[1 + p.r], p.plane_dev(r))

    def begin(self):
        self.across().start()
        self.own().start()

    def middle(self):
        p = self.p
        self.own().wait()
        self.across().wait_recv()

        @pl.loop(0, 2 * p.B)
        def _(r):
            t = self.acc[r].astype(jnp.float32) + self.rc[r].astype(jnp.float32)
            self.acc[r] = t.astype(self.acc.dtype)

        @pl.loop(1, 2 * p.B)
        def _(o):
            self.away(o).start()

        cp = pltpu.make_async_copy(self.acc.at[p.r], self.out.at[p.r], self.local.at[0])
        cp.start()
        cp.wait()

    def end(self):
        p = self.p
        self.across().wait_send()

        @pl.loop(1, 2 * p.B)
        def _(o):
            r = lax.rem(p.r + o, 2 * p.B)
            part = self.out.at[r]
            remote(part, part, self.send.at[0], self.recv.at[1 + r], p.x_peer).wait_recv()
            self.away(o).wait_send()


def finish_kernel(U, B, more, *refs):
    p = Place(U, B)
    p.barrier("plane")
    n = 4 if more else 3
    srcs, outs, scratch = refs[:n], refs[n:2 * n + 1], refs[2 * n + 1:]
    at = PlaneScatter.SCRATCH
    work = [PlaneScatter(p, *scratch[:at])]
    if more:
        work.append(Scatter(p, *scratch[at:at + Scatter.SCRATCH], like=(0, 0), chain=True))
        at += Scatter.SCRATCH
    ex = []
    for i in range(2):
        ex.append(PairExchange(p, srcs[i], outs[i], *scratch[at:at + PairExchange.SCRATCH]))
        at += PairExchange.SCRATCH
    stage, sems = scratch[at:]
    for s, src in zip(work, srcs[2:]):
        s.load(src)
    for e in ex:
        e.begin()
    work[0].step(0)
    for e in ex:
        e.middle()
    for s in work[1:]:
        s.step(0)
    for j in range(1, p.Z + 1):
        for s in work:
            s.step(j)
    fin = work[0].fin
    rows = fin.shape[1]

    def one(m, _):
        r = pl.ds(pl.multiple_of(m * 16, 16), 16)
        stage[r, :] = fin[1 - p.x, r, :].astype(stage.dtype)
        return 0

    lax.fori_loop(0, rows // 16, one, 0)
    away = remote(stage, outs[3], sems.at[0], sems.at[1], p.x_peer)
    away.start()
    keep_sum(fin.at[p.x], outs[2], sems.at[2])
    if more:
        work[1].step(p.Z + 1)
        keep_sum(work[1].fin, outs[4], sems.at[2])
    away.wait_recv()
    away.wait_send()
    for s in work:
        s.sent()
    for e in ex:
        e.end()


def finish(weights, small, hidden, out, U, B, cid):
    F = U * B
    parts = max(1, F // 32)
    D = hidden.shape[-1] // parts
    sds, f32 = jax.ShapeDtypeStruct, jnp.float32

    def call(h, o, cid):
        args = [m.reshape((2, 2 * B) + m.shape[1:]) for m in (weights, small)] + [h]
        shapes = [sds((2 * B,) + m.shape[1:], m.dtype) for m in (weights, small)]
        shapes += [sds(h.shape[1:], f32), sds(h.shape[1:], h.dtype)]
        scratch = PlaneScatter.scratch(U, B, h.shape[1], h.shape[2], h.dtype)
        if o is not None:
            args.append(o)
            shapes.append(sds(o.shape[1:], f32))
            scratch += Scatter.scratch(U, B, o.shape[2], o.shape[3], o.dtype, (0, 0), True)
        for m in (weights, small):
            scratch += PairExchange.scratch(U, B, m.shape[1], m.shape[2], m.dtype)
        return pl.pallas_call(
            functools.partial(finish_kernel, U, B, o is not None),
            out_shape=shapes,
            in_specs=any_specs(len(args)),
            out_specs=any_specs(len(shapes)),
            scratch_shapes=scratch + [pltpu.VMEM(h.shape[1:], h.dtype), pltpu.SemaphoreType.DMA((3,))],
            compiler_params=pltpu.CompilerParams(
                collective_id=cid, has_side_effects=True, vmem_limit_bytes=62 * 2**20),
        )(*args)

    if parts == 1:
        return call(hidden, out, cid)
    got = [call(hidden[..., n * D:(n + 1) * D], None, cid) for n in range(parts)]
    own, other = (jnp.concatenate([g[i] for g in got], axis=-1) for i in (2, 3))
    return got[0][0], got[0][1], own, other, scatter_by_permutes(out, U, B)


def scatter_by_permutes(v, U, B):
    X, Y, Z = U // 2, 2, B // 2
    f32 = jnp.float32
    u, b = lax.axis_index("ulysses"), lax.axis_index("blk")
    c, x, y, z = lax.rem(u, 2), lax.div(u, 2), lax.rem(b, Y), lax.div(b, Y)
    where = {"c": c, "x": x, "y": y, "z": z}
    size = {"c": 2, "x": X, "y": Y, "z": Z}

    def pairs(axis, by):
        out = []
        for f in range(U * B):
            at = {"x": f // B // 2, "c": f // B % 2, "z": f % B // Y, "y": f % Y}
            at[axis] = (at[axis] + by) % size[axis]
            out.append((f, (at["x"] * 2 + at["c"]) * B + at["z"] * Y + at["y"]))
        return out

    def fold(m, axis, dim):
        n = size[axis]
        total = lax.dynamic_index_in_dim(m, where[axis], dim, keepdims=False).astype(f32)
        for by in range(1, n):
            part = lax.dynamic_index_in_dim(m, lax.rem(where[axis] + by, n), dim, keepdims=False)
            total = total + lax.ppermute(part, ("ulysses", "blk"), pairs(axis, by)).astype(f32)
        return total

    rows, D = v.shape[-2:]
    m = fold(v.reshape(X, 2, Z, Y, 2, rows, D), "c", 1).astype(v.dtype)
    first = fold(m[:, :, :, 0], "x", 0).astype(v.dtype)
    first = fold(first, "y", 1).astype(v.dtype)
    second = fold(m[:, :, :, 1], "y", 2).astype(v.dtype)
    second = fold(second, "x", 0).astype(v.dtype)
    return fold(jnp.stack([first, second], axis=1), "z", 0)


def rms_norm(values, gains):
    return values * lax.rsqrt(jnp.mean(values * values, axis=-1, keepdims=True) + EPSILON) * gains


def dot(a, b, ca, cb):
    return lax.dot_general(a, b, (((ca,), (cb,)), ((), ())), preferred_element_type=jnp.float32)


def attend_kernel(U, B, bq, scale, q_ref, k_ref, vt_ref, out_ref, lse_ref, rows_ref, send, recv):
    p = Place(U, B)
    p.barrier("every")
    per = bq // rows_ref.shape[1]
    n = q_ref.shape[0] // bq

    def away(f):
        return remote(rows_ref.at[f], out_ref.at[p.me], send.at[f], recv.at[p.me], p.flat_dev(f))

    @pl.loop(0, n)
    def _(t):
        i = lax.rem(t + lax.div(p.me, per), n)
        rows = pl.ds(pl.multiple_of(i * bq, bq), bq)
        s = dot(k_ref[...], q_ref[rows, :], 1, 1) * scale
        top = jnp.max(s, axis=0, keepdims=True)
        e = jnp.exp(s - top)
        total = jnp.sum(e, axis=0, keepdims=True)
        o = dot(vt_ref[...], e.astype(jnp.bfloat16), 1, 0) / total
        lse_ref[:, rows] = top + jnp.log(total)
        rows_ref[pl.ds(i * per, per)] = o.T.astype(rows_ref.dtype).reshape((per,) + rows_ref.shape[1:])
        for d in range(per):
            f = i * per + d

            @pl.when(f != p.me)
            def _():
                away(f).start()

    cp = pltpu.make_async_copy(rows_ref.at[p.me], out_ref.at[p.me], recv.at[p.me])
    cp.start()
    cp.wait()

    @pl.loop(1, p.F)
    def _(o):
        f = lax.rem(p.me + o, p.F)
        remote(out_ref.at[f], out_ref.at[f], send.at[f], recv.at[f], p.flat_dev(f)).wait_recv()
        away(f).wait_send()


def attend(q, k, vt, positions, U, B, cid):
    n = q.shape[0]
    F = U * B
    bq = 256 if n <= 2048 else 128
    vmem = pl.BlockSpec(memory_space=pltpu.VMEM)
    dma = pltpu.SemaphoreType.DMA
    return pl.pallas_call(
        functools.partial(attend_kernel, U, B, bq, 1.0 / math.sqrt(HD)),
        in_specs=[vmem] * 3,
        out_specs=any_specs(1) + [vmem],
        out_shape=[jax.ShapeDtypeStruct((F, positions, HD), jnp.bfloat16), jax.ShapeDtypeStruct((1, n), jnp.float32)],
        scratch_shapes=[pltpu.VMEM((F, positions, HD), jnp.bfloat16), dma((F,)), dma((F,))],
        compiler_params=pltpu.CompilerParams(
            collective_id=cid, has_side_effects=True, vmem_limit_bytes=40 * 2**20),
    )(q, k, vt)


def attend_back_kernel(U, B, bq, scale, src_ref, q_ref, lse_ref, k_ref, kt_ref, v_ref,
                       dq_ref, dk_ref, dv_ref, do_ref, send, recv, local):
    p = Place(U, B)
    p.barrier("every")
    per = bq // do_ref.shape[1]
    n = q_ref.shape[0] // bq

    def away(f):
        return remote(src_ref.at[f], do_ref.at[p.me], send.at[f], recv.at[p.me], p.flat_dev(f))

    @pl.loop(1, p.F)
    def _(o):
        away(lax.rem(p.me + o, p.F)).start()

    cp = pltpu.make_async_copy(src_ref.at[p.me], do_ref.at[p.me], local.at[0])
    cp.start()
    dk_ref[...] = jnp.zeros_like(dk_ref)
    dv_ref[...] = jnp.zeros_like(dv_ref)
    cp.wait()

    @pl.loop(0, n)
    def _(t):
        i = lax.rem(n - t + lax.div(p.me, per), n)
        rows = pl.ds(pl.multiple_of(i * bq, bq), bq)
        e = jnp.exp(dot(k_ref[...], q_ref[rows, :], 1, 1) * scale - lse_ref[:, rows])
        for d in range(per):
            f = i * per + d

            @pl.when(f != p.me)
            def _():
                remote(do_ref.at[f], do_ref.at[f], send.at[f], recv.at[f], p.flat_dev(f)).wait_recv()

        do = do_ref[pl.ds(i * per, per)].reshape(bq, HD)
        dp = dot(v_ref[...], do, 1, 1)
        delta = jnp.sum(e * dp, axis=0, keepdims=True)
        ds = (e * (dp - delta)).astype(jnp.bfloat16)
        dv_ref[...] += dot(e.astype(jnp.bfloat16), do, 1, 0)
        dk_ref[...] += dot(ds, q_ref[rows, :], 1, 0) * scale
        dq_ref[rows, :] = (dot(kt_ref[...], ds, 1, 0) * scale).T

    @pl.loop(1, p.F)
    def _(o):
        away(lax.rem(p.me + o, p.F)).wait_send()


def attend_back(grads, q, lse, k, kt, v, U, B, cid):
    n = q.shape[0]
    F = U * B
    bq = 256 if n <= 2048 else 128
    vmem = pl.BlockSpec(memory_space=pltpu.VMEM)
    dma = pltpu.SemaphoreType.DMA
    return pl.pallas_call(
        functools.partial(attend_back_kernel, U, B, bq, 1.0 / math.sqrt(HD)),
        in_specs=any_specs(1) + [vmem] * 5,
        out_specs=[vmem] * 3,
        out_shape=[jax.ShapeDtypeStruct((n, HD), jnp.float32)] * 3,
        scratch_shapes=[pltpu.VMEM(grads.shape, grads.dtype), dma((F,)), dma((F,)), dma((1,))],
        compiler_params=pltpu.CompilerParams(
            collective_id=cid, has_side_effects=True, vmem_limit_bytes=58 * 2**20),
    )(grads, q, lse, k, kt, v)


def turn(v, cosine, sine):
    return v * cosine + pltpu.roll(v, HD // 2, 1) * sine


def project_kernel(tok_ref, gain_ref, w_ref, qk_ref, cos_ref, sin_ref,
                   q_ref, k_ref, v_ref, kt_ref, vt_ref, rq_ref, rk_ref):
    bf16 = jnp.bfloat16
    raw = dot(rms_norm(tok_ref[...].astype(jnp.float32), gain_ref[...]).astype(bf16), w_ref[...], 1, 0)
    rq, rk, v = raw[:, :HD], raw[:, HD:2 * HD], raw[:, 2 * HD:].astype(bf16)
    rq_ref[...] = rq
    rk_ref[...] = rk
    q_ref[...] = turn(rms_norm(rq, qk_ref[0:1]), cos_ref[...], sin_ref[...]).astype(bf16)
    k = turn(rms_norm(rk, qk_ref[1:2]), cos_ref[...], sin_ref[...])
    k_ref[...] = k.astype(bf16)
    kt_ref[...] = k.T.astype(bf16)
    v_ref[...] = v
    vt_ref[...] = raw[:, 2 * HD:].T.astype(bf16)


def project(tok, gain, w, qk, cosine, sine):
    n, D = tok.shape
    bm = 512
    row, whole = (lambda i: (i, 0)), (lambda i: (0, 0))
    head, across = pl.BlockSpec((bm, HD), row), pl.BlockSpec((HD, bm), lambda i: (0, i))
    sds = jax.ShapeDtypeStruct
    f32, bf16 = jnp.float32, jnp.bfloat16
    return pl.pallas_call(
        project_kernel,
        grid=(n // bm,),
        in_specs=[
            pl.BlockSpec((bm, D), row), pl.BlockSpec((1, D), whole), pl.BlockSpec((D, 3 * HD), whole),
            pl.BlockSpec((2, HD), whole), head, head,
        ],
        out_specs=[head, head, head, across, across, head, head],
        out_shape=[sds((n, HD), bf16)] * 3 + [sds((HD, n), bf16)] * 2 + [sds((n, HD), f32)] * 2,
        compiler_params=pltpu.CompilerParams(vmem_limit_bytes=58 * 2**20),
    )(tok, gain, w, qk, cosine, sine)


def head_back_kernel(dq_ref, dk_ref, dv_ref, rq_ref, rk_ref, cos_ref, sin_ref, qk_ref, tok_ref, gain_ref, w_ref,
                     part_ref, dwout_ref, dg_ref, da_ref, dw_ref):
    f32, bf16 = jnp.float32, jnp.bfloat16

    @pl.when(pl.program_id(0) == 0)
    def _():
        dw_ref[...] = jnp.zeros_like(dw_ref)
        dg_ref[...] = jnp.zeros_like(dg_ref)
        da_ref[...] = jnp.zeros_like(da_ref)

    grads = []
    for n, (g_ref, raw_ref) in enumerate(((dq_ref, rq_ref), (dk_ref, rk_ref))):
        w = turn(g_ref[...].astype(bf16).astype(f32), cos_ref[...], -sin_ref[...])
        u = raw_ref[...]
        r = lax.rsqrt(jnp.mean(u * u, axis=-1, keepdims=True) + EPSILON)
        norm = u * r
        dg_ref[n:n + 1, :] += jnp.sum(w * norm, axis=0, keepdims=True)
        m = w * qk_ref[n:n + 1]
        grads.append((r * (m - norm * jnp.mean(m * norm, axis=-1, keepdims=True))).astype(bf16))
    grads.append(dv_ref[...].astype(bf16))
    grad = jnp.concatenate(grads, axis=1)
    across = grad.T
    tok = tok_ref[...].astype(f32)
    norm = tok * lax.rsqrt(jnp.mean(tok * tok, axis=-1, keepdims=True) + EPSILON)
    hidden = (norm * gain_ref[...]).astype(bf16)
    D = tok.shape[1]
    cut = min(D, 512)
    for n in range(0, D, cut):
        part = dot(grad, w_ref[n:n + cut, :], 1, 1)
        part_ref[:, n:n + cut] = part.astype(bf16)
        da_ref[0:1, n:n + cut] += jnp.sum(part * norm[:, n:n + cut], axis=0, keepdims=True)
        dw_ref[:, n:n + cut] += dot(across, hidden[:, n:n + cut], 1, 0)

    @pl.when(pl.program_id(0) == pl.num_programs(0) - 1)
    def _():
        for n in range(0, D, cut):
            dwout_ref[n:n + cut, :] = dw_ref[:, n:n + cut].T.astype(bf16)


def head_back(dq, dk, dv, rq, rk, cosine, sine, qk, tok, gain, w):
    n, D = tok.shape
    bm = 512
    row, whole = (lambda i: (i, 0)), (lambda i: (0, 0))
    head = pl.BlockSpec((bm, HD), row)
    sds = jax.ShapeDtypeStruct
    return pl.pallas_call(
        head_back_kernel,
        grid=(n // bm,),
        in_specs=[head] * 7 + [
            pl.BlockSpec((2, HD), whole), pl.BlockSpec((bm, D), row), pl.BlockSpec((1, D), whole),
            pl.BlockSpec((D, 3 * HD), whole)],
        out_specs=[
            pl.BlockSpec((bm, D), row), pl.BlockSpec((D, 3 * HD), whole), pl.BlockSpec((8, HD), whole),
            pl.BlockSpec((8, D), whole)],
        out_shape=[sds((n, D), jnp.bfloat16), sds((D, 3 * HD), jnp.bfloat16), sds((8, HD), jnp.float32),
                   sds((8, D), jnp.float32)],
        scratch_shapes=[pltpu.VMEM((3 * HD, D), jnp.float32)],
        compiler_params=pltpu.CompilerParams(vmem_limit_bytes=58 * 2**20),
    )(dq, dk, dv, rq, rk, cosine, sine, qk, tok, gain, w)


def dispatch_kernel(hot_ref, rg_ref, norm_ref, cot_ref, x_ref, pg_ref):
    bf16 = jnp.bfloat16
    experts, RB, D = x_ref.shape
    hot = hot_ref[0]
    KB = hot.shape[1]
    weight = rg_ref[:, :, 0:1].reshape(experts * RB, 1)
    cut = min(D, 512)
    norm = norm_ref[...].reshape(KB, D)
    cot = cot_ref[...].reshape(KB, D)
    for n in range(0, D, cut):
        x = dot(hot, norm[:, n:n + cut], 1, 0).astype(bf16)
        x_ref[:, :, n:n + cut] = x.reshape(experts, RB, cut)
        g = (dot(hot, cot[:, n:n + cut], 1, 0) * weight).astype(bf16)
        pg_ref[:, :, n:n + cut] = g.reshape(experts, RB, cut)


def group_spec(shape, Z):
    X, two, _, Y, T, D = shape
    return pl.BlockSpec((1, two, 1, Y, T, D), lambda g: (g // Z, 0, g % Z, 0, 0, 0))


def dispatch(hot, rg, normed, cot):
    G, rows, KB = hot.shape
    experts, D, Z = rg.shape[0], normed.shape[-1], normed.shape[2]
    RB = rows // experts
    out = pl.BlockSpec((experts, RB, D), lambda g: (0, g, 0))
    return pl.pallas_call(
        dispatch_kernel,
        grid=(G,),
        in_specs=[pl.BlockSpec((1, rows, KB), lambda g: (g, 0, 0)), pl.BlockSpec((experts, RB, 128), lambda g: (0, g, 0)),
                  group_spec(normed.shape, Z), group_spec(cot.shape, Z)],
        out_specs=[out, out],
        out_shape=[jax.ShapeDtypeStruct((experts, G * RB, D), jnp.bfloat16)] * 2,
        compiler_params=pltpu.CompilerParams(vmem_limit_bytes=62 * 2**20),
    )(hot, rg, normed, cot)


def expert_kernel(x_ref, pg_ref, rg_ref, wg_ref, wu_ref, wd_ref, y_ref, dx_ref, dwg_ref, dwu_ref, dwd_ref):
    bf16 = jnp.bfloat16
    x, pg = x_ref[0], pg_ref[0]
    D = x.shape[1]
    gate, up = dot(x, wg_ref[0], 1, 0), dot(x, wu_ref[0], 1, 0)
    sigma = jax.nn.sigmoid(gate)
    silu = gate * sigma
    inner = (silu * up).astype(bf16)
    back = dot(pg, wd_ref[0], 1, 1)
    dgate = (back * up * sigma * (1.0 + gate * (1.0 - sigma))).astype(bf16)
    dup = (back * silu).astype(bf16)
    cut = min(D, 1024)
    weight = rg_ref[0, :, 0:1]
    both = jnp.concatenate([dgate, dup], axis=1)
    ff = dgate.shape[1]
    first = pl.program_id(1) == 0

    def put(ref, ix, value):
        if pl.num_programs(1) == 1:
            ref[ix] = value
        else:
            ref[ix] = value + jnp.where(first, 0.0, ref[ix])

    for n in range(0, D, cut):
        c = slice(n, n + cut)
        y_ref[0, :, c] = (dot(inner, wd_ref[0, :, c], 1, 0) * weight).astype(bf16)
        dx_ref[0, :, c] = (dot(dgate, wg_ref[0, c, :], 1, 1) + dot(dup, wu_ref[0, c, :], 1, 1)).astype(bf16)
        d = dot(x_ref[0, :, c], both, 0, 0)
        put(dwg_ref, (0, c, slice(None)), d[:, :ff])
        put(dwu_ref, (0, c, slice(None)), d[:, ff:])
        put(dwd_ref, (0, slice(None), c), dot(inner, pg_ref[0, :, c], 0, 0))


def expert_layer(x, pg, rg, wg, wu, wd):
    rows = x.shape[1]
    step = 640 if rows % 640 == 0 else rows
    some = lambda a: pl.BlockSpec((1, step) + a.shape[2:], lambda e, i: (e, i, 0))
    whole = lambda a: pl.BlockSpec((1,) + a.shape[1:], lambda e, i: (e, 0, 0))
    sds = jax.ShapeDtypeStruct
    return pl.pallas_call(
        expert_kernel,
        grid=(x.shape[0], rows // step),
        in_specs=[some(a) for a in (x, pg, rg)] + [whole(a) for a in (wg, wu, wd)],
        out_specs=[some(a) for a in (x, x)] + [whole(a) for a in (wg, wu, wd)],
        out_shape=[sds(x.shape, x.dtype)] * 2 + [sds(a.shape, jnp.float32) for a in (wg, wu, wd)],
        compiler_params=pltpu.CompilerParams(vmem_limit_bytes=62 * 2**20),
    )(x, pg, rg, wg, wu, wd)


def middle_kernel(res_ref, gain_ref, grad_ref, cot_ref, att_ref, w_ref, back_ref, gain_out_ref, heads_ref, part_ref, low_ref):
    f32, bf16 = jnp.float32, jnp.bfloat16

    @pl.when(pl.program_id(0) == 0)
    def _():
        u = res_ref[...]
        r = lax.rsqrt(jnp.mean(u * u, axis=-1, keepdims=True) + EPSILON)
        norm = u * r
        w = grad_ref[...]
        gain_out_ref[...] = jnp.broadcast_to(jnp.sum(w * norm, axis=0, keepdims=True), gain_out_ref.shape)
        m = w * gain_ref[...]
        back = cot_ref[...].astype(f32) + r * (m - norm * jnp.mean(m * norm, axis=-1, keepdims=True))
        back_ref[...] = back
        low_ref[...] = back.astype(bf16)

    low = low_ref[...]
    seqs, heads, positions, _ = heads_ref.shape
    grad = dot(low, w_ref[...], 1, 1).astype(bf16)
    for s in range(seqs):
        for h in range(heads):
            heads_ref[s, h] = grad[s * positions:(s + 1) * positions, h * HD:(h + 1) * HD]
    part_ref[...] = dot(att_ref[...], low, 0, 0).astype(bf16)


def middle(residual, gain, normed_grad, cot, attended, out_w, seqs):
    T, D = residual.shape
    features = attended.shape[1]
    cut = 512
    whole = lambda n: (0, 0)
    sds, f32, bf16 = jax.ShapeDtypeStruct, jnp.float32, jnp.bfloat16
    full = pl.BlockSpec((T, D), whole)
    rows = pl.BlockSpec((cut, D), lambda n: (n, 0))
    return pl.pallas_call(
        middle_kernel,
        grid=(features // cut,),
        in_specs=[full, pl.BlockSpec((1, D), whole), full, full, pl.BlockSpec((T, cut), lambda n: (0, n)), rows],
        out_specs=[full, pl.BlockSpec((8, D), whole),
                   pl.BlockSpec((seqs, cut // HD, T // seqs, HD), lambda n: (0, n, 0, 0)), rows],
        out_shape=[sds((T, D), f32), sds((8, D), f32), sds((seqs, features // HD, T // seqs, HD), bf16),
                   sds((features, D), bf16)],
        scratch_shapes=[pltpu.VMEM((T, D), bf16)],
        compiler_params=pltpu.CompilerParams(vmem_limit_bytes=58 * 2**20),
    )(residual, gain, normed_grad, cot, attended, out_w)


def close_kernel(x_ref, w_ref, own_ref, other_ref, back_ref, tok_ref, gain_ref, q_ref, k_ref, v_ref, in_ref):
    f32 = jnp.float32
    for h in range(w_ref.shape[0]):
        for n, ref in enumerate((q_ref, k_ref, v_ref)):
            ref[:, h * HD:(h + 1) * HD] = w_ref[h, :, n * HD:(n + 1) * HD].astype(f32)
    here = x_ref[0]
    for s in (0, 1):
        grad = jnp.where(here == s, own_ref[...], other_ref[...].astype(f32))
        tok = tok_ref[s].astype(f32)
        inv = lax.rsqrt(jnp.mean(tok * tok, axis=-1, keepdims=True) + EPSILON)
        norm = tok * inv
        m = grad * gain_ref[...]
        in_ref[s] = back_ref[s] + inv * (m - norm * jnp.mean(m * norm, axis=-1, keepdims=True))


def close(here, weight_grad, own, other, back, tok, gain):
    heads, W, _ = weight_grad.shape
    vmem = pl.BlockSpec(memory_space=pltpu.VMEM)
    sds = jax.ShapeDtypeStruct
    return pl.pallas_call(
        close_kernel,
        in_specs=[pl.BlockSpec(memory_space=pltpu.SMEM)] + [vmem] * 6,
        out_specs=[vmem] * 4,
        out_shape=[sds((W, heads * HD), jnp.float32)] * 3 + [sds(tok.shape, jnp.float32)],
        compiler_params=pltpu.CompilerParams(vmem_limit_bytes=32 * 2**20),
    )(here, weight_grad, own, other, back, tok, gain)


def body(tokens, w_query, w_key, w_value, w_out, attn_gain, ffn_gain, qk_gain,
         expert_gate, expert_up, expert_down, routes, gates, order, cotangent):
    f32, bf16 = jnp.float32, jnp.bfloat16
    positions, seqs, D = tokens.shape
    U, B = lax.axis_size("ulysses"), lax.axis_size("blk")
    F = U * B
    u, b = lax.axis_index("ulysses"), lax.axis_index("blk")
    H = w_query.shape[1] // HD
    W = w_query.shape[0]
    L = F * positions
    T = seqs * positions
    top_count = routes.shape[-1]
    local_experts = expert_gate.shape[0]
    E = local_experts * B
    R = 2 * B // H
    x_here = u // 2
    first_copy = lax.rem((u % 2) * B + b, R) == 0

    tok = tokens.transpose(1, 0, 2)
    cot = cotangent.transpose(1, 0, 2)
    rows_f = tok.reshape(T, D).astype(f32)

    expert_of = routes.transpose(1, 0, 2).reshape(-1)
    prio = order.reshape(positions, seqs, top_count).transpose(1, 0, 2).reshape(-1)
    same = expert_of[:, None] == expert_of[None, :]
    ranks = jnp.sum((same & (prio[None, :] < prio[:, None])).astype(jnp.int32), axis=1)
    slot = jnp.where(ranks < CAP, expert_of * CAP + ranks, -1).astype(f32)
    pairs = slot.shape[0]

    nq = qk_gain.shape[1]
    small = jnp.concatenate(
        [slot, gates.transpose(1, 0, 2).reshape(-1)]
        + [g.astype(f32) for g in (attn_gain, ffn_gain, qk_gain[0], qk_gain[1])])
    small = jnp.pad(small, (0, -small.shape[0] % 1024)).reshape(-1, 128)
    seq_tok, table, head_w = front(tok, small, (w_query, w_key, w_value), HD, R, U, B, 1)
    seq_tok, head_w = seq_tok.reshape(L, D), head_w.reshape(D, 3 * HD)
    out_w = lax.all_gather(w_out, AXES, axis=0, tiled=True)
    cot_all = lax.all_gather(cot, AXES, axis=0)
    table = table.reshape(F, -1)
    cut = 2 * pairs
    attn_g = table[:, cut:cut + W].reshape(1, D)
    ffn_g = table[:, cut + W:cut + 2 * W].reshape(1, D)
    cut = cut + 2 * W
    qk_g = jnp.stack([table[:, cut:cut + nq].reshape(-1), table[:, cut + nq:cut + 2 * nq].reshape(-1)])

    groups = (U // 2, 2, B // 2, 2)
    GB = 4
    G, KB = F // GB, GB * T
    RB = -(-GB * CAP // 16) * 16
    slot_all = table[:, :pairs].astype(jnp.int32).reshape(F, T, top_count)
    gate_all = table[:, pairs:2 * pairs].reshape(F, T, top_count)
    place = ((np.arange(F) // B % 2) * 2 + np.arange(F) % 2).astype(np.int32)
    base = (b * local_experts + jnp.arange(local_experts, dtype=jnp.int32)) * CAP
    off = slot_all[:, :, :, None] - base
    mine = (off >= 0) & (off < CAP)
    val = jnp.sum(jnp.where(mine, off + 1, 0), axis=2)
    val = jnp.where(val > 0, val - 1 + jnp.asarray(place)[:, None, None] * CAP, -1)
    gate_of = jnp.sum(jnp.where(mine, gate_all[:, :, :, None], 0.0), axis=2)

    def by_group(m):
        return m.reshape(groups + (T, local_experts)).transpose(0, 2, 5, 1, 3, 4).reshape(G, local_experts, KB)

    val, gate_of = by_group(val), by_group(gate_of)

    inverse = (ROPE_BASE ** (-2.0 * np.arange(HD // 2) / HD)).astype(np.float32)
    angles = np.arange(L).astype(np.float32)[:, None] * inverse[None, :]
    cosine = jnp.asarray(np.concatenate([np.cos(angles)] * 2, axis=1).astype(np.float32))
    sine = jnp.asarray(np.concatenate([-np.sin(angles), np.sin(angles)], axis=1).astype(np.float32))
    q, k, v, kt, vt, raw_q, raw_k = project(seq_tok, attn_g, head_w, qk_g, cosine, sine)
    att_rows, lse = attend(q, k, vt, positions, U, B, 5)

    def from_heads(m):
        m = m.reshape(2, 2 * B, positions, HD).transpose(0, 2, 1, 3)
        return m.reshape(2, positions, H, R, HD)[:, :, :, 0].reshape(T, H * HD)

    attended = from_heads(att_rows)
    residual = rows_f + jnp.dot(attended, out_w, preferred_element_type=f32)
    normed = rms_norm(residual, ffn_g).astype(bf16).reshape(2, positions, D)

    normed_all, hot, row_gate = gather_blocks(normed, val, gate_of, RB, U, B, 2)
    shape = groups + (T, D)
    normed_all, cot_all = normed_all.reshape(shape), cot_all.reshape(shape)
    weights = (expert_gate, expert_up, expert_down)
    x, pair_grad = dispatch(hot, row_gate, normed_all, cot_all)
    y, dx, gate_grad, up_grad, down_grad = expert_layer(x, pair_grad, row_gate, *weights)
    normed_grad, mixed_sum = scatter_pair(dx, y, hot, positions, U, B, 3)
    mixed = (residual + mixed_sum.reshape(T, D)).reshape(2, positions, D).transpose(1, 0, 2).astype(bf16)
    normed_grad = normed_grad.reshape(T, D)

    residual_grad, ffn_gain_part, att_grad, out_part = middle(
        residual, ffn_g, normed_grad, cot.reshape(T, D), attended, out_w, seqs)
    att_grad = jnp.repeat(att_grad, R, axis=1).reshape(F, positions, HD)
    out_part = out_part.reshape(F, 2, W // 2, D)
    dq, dk, dv = attend_back(att_grad, q, lse, k, kt, v, U, B, 6)
    if R > 1:
        dq, dk, dv = (jnp.where(first_copy, m, 0.0) for m in (dq, dk, dv))
    hidden_part, weight_part, qk_part, attn_gain_part = head_back(
        dq, dk, dv, raw_q, raw_k, cosine, sine, qk_g, seq_tok, attn_g, head_w)
    weight_part = weight_part.reshape(F, W, 3 * HD)
    small = jnp.concatenate(
        [attn_gain_part[0].reshape(F, W), ffn_gain_part[0].reshape(F, W),
         qk_part[0].reshape(F, nq), qk_part[1].reshape(F, nq)], axis=1)
    small = jnp.pad(small, ((0, 0), (0, -small.shape[1] % 1024))).reshape(F, -1, 128)
    weight_grad, small, own, other, out_grad = finish(
        weight_part, small, hidden_part.reshape(F, positions, D), out_part, U, B, 4)
    small = jnp.sum(small, axis=0).reshape(-1)
    if R > 1:
        weight_grad = weight_grad.reshape(H, R, W, 3 * HD).astype(f32).sum(axis=1)
    query_grad, key_grad, value_grad, input_grad = close(
        x_here.reshape(1), weight_grad, own, other, residual_grad.reshape(2, positions, D), tok, attn_g)
    input_grad = input_grad.transpose(1, 0, 2)
    out_grad = out_grad.reshape(W, D)
    return (
        mixed, input_grad, query_grad, key_grad, value_grad, out_grad,
        small[:W], small[W:2 * W], small[2 * W:2 * W + 2 * nq].reshape(2, nq),
        gate_grad, up_grad, down_grad,
    )


def solution(mesh):
    rows = P(AXES, None, None)
    flat = P(AXES, None)
    by_expert = (P("blk", None, "ulysses"), P("blk", None, "ulysses"), P("blk", "ulysses", None))
    in_specs = (rows, flat, flat, flat, flat, P(AXES), P(AXES), P(None, AXES)) + by_expert + (rows, rows, flat, rows)
    out_specs = (rows, rows, flat, flat, flat, flat, P(AXES), P(AXES), P(None, AXES)) + by_expert
    return jax.shard_map(body, mesh=mesh, in_specs=in_specs, out_specs=out_specs, check_vma=False)
```
